32 devices in a mesh: dp: 8 (over z, y), chan: 4 (over x, core).
Axes of the slice: x: 2, y: 2, z: 4, core: 2. Of those that a mesh axis runs over, the one named last changes fastest.
Arguments:
- images: bfloat16 [64, 32, 32, 512], P('dp', None, None, 'chan'), may hold values from -6 to 6
- cotangent: bfloat16 [64, 16, 16, 1024], P('dp', None, None, 'chan'), may hold values from -6 to 6
- groups: int32 [64], P('dp'), may hold values from 0 to 2
- first_reduce: bfloat16 [512, 256], P(None, 'chan'), may hold values from -0.25 to 0.25
- first_reducegain: float32 [256], P('chan'), may hold values from 0.5 to 1.5
- first_reducebias: float32 [256], P('chan'), may hold values from -1.5 to 1.5
- first_split: bfloat16 [3, 3, 128, 2, 256], P(None, None, None, None, 'chan'), may hold values from -0.1875 to 0.1875
- first_splitgain: float32 [2, 256], P(None, 'chan'), may hold values from 0.5 to 1.5
- first_splitbias: float32 [2, 256], P(None, 'chan'), may hold values from -1.5 to 1.5
- first_squeeze: bfloat16 [256, 128], P('chan'), may hold values from -0.375 to 0.375
- first_squeezegain: float32 [128], replicated, may hold values from 0.5 to 1.5
- first_squeezebias: float32 [128], replicated, may hold values from -1.5 to 1.5
- first_excite: bfloat16 [128, 2, 256], P(None, None, 'chan'), may hold values from -0.5 to 0.5
- first_excitebias: float32 [2, 256], P(None, 'chan'), may hold values from -2 to 2
- first_expand: bfloat16 [256, 1024], P(None, 'chan'), may hold values from -0.375 to 0.375
- first_expandgain: float32 [1024], P('chan'), may hold values from 0.5 to 1.5
- first_expandbias: float32 [1024], P('chan'), may hold values from -1.5 to 1.5
- first_shortcut: bfloat16 [512, 1024], P(None, 'chan'), may hold values from -0.25 to 0.25
- first_shortgain: float32 [1024], P('chan'), may hold values from 0.5 to 1.5
- first_shortbias: float32 [1024], P('chan'), may hold values from -1.5 to 1.5
- second_reduce: bfloat16 [1024, 256], P(None, 'chan'), may hold values from -0.1875 to 0.1875
- second_reducegain: float32 [256], P('chan'), may hold values from 0.5 to 1.5
- second_reducebias: float32 [256], P('chan'), may hold values from -1.5 to 1.5
- second_split: bfloat16 [3, 3, 128, 2, 256], P(None, None, None, None, 'chan'), may hold values from -0.1875 to 0.1875
- second_splitgain: float32 [2, 256], P(None, 'chan'), may hold values from 0.5 to 1.5
- second_splitbias: float32 [2, 256], P(None, 'chan'), may hold values from -1.5 to 1.5
- second_squeeze: bfloat16 [256, 128], P('chan'), may hold values from -0.375 to 0.375
- second_squeezegain: float32 [128], replicated, may hold values from 0.5 to 1.5
- second_squeezebias: float32 [128], replicated, may hold values from -1.5 to 1.5
- second_excite: bfloat16 [128, 2, 256], P(None, None, 'chan'), may hold values from -0.5 to 0.5
- second_excitebias: float32 [2, 256], P(None, 'chan'), may hold values from -2 to 2
- second_expand: bfloat16 [256, 1024], P(None, 'chan'), may hold values from -0.375 to 0.375
- second_expandgain: float32 [1024], P('chan'), may hold values from 0.5 to 1.5
- second_expandbias: float32 [1024], P('chan'), may hold values from -1.5 to 1.5
Outputs:
- out_image: float32 [64, 16, 16, 1024], P('dp', None, None, 'chan')
- grad_images: float32 [64, 32, 32, 512], P('dp', None, None, 'chan')
- grad_first_reduce: float32 [512, 256], P(None, 'chan')
- grad_first_reducegain: float32 [256], P('chan')
- grad_first_reducebias: float32 [256], P('chan')
- grad_first_split: float32 [3, 3, 128, 2, 256], P(None, None, None, None, 'chan')
- grad_first_splitgain: float32 [2, 256], P(None, 'chan')
- grad_first_splitbias: float32 [2, 256], P(None, 'chan')
- grad_first_squeeze: float32 [256, 128], P('chan')
- grad_first_squeezegain: float32 [128], replicated
- grad_first_squeezebias: float32 [128], replicated
- grad_first_excite: float32 [128, 2, 256], P(None, None, 'chan')
- grad_first_excitebias: float32 [2, 256], P(None, 'chan')
- grad_first_expand: float32 [256, 1024], P(None, 'chan')
- grad_first_expandgain: float32 [1024], P('chan')
- grad_first_expandbias: float32 [1024], P('chan')
- grad_first_shortcut: float32 [512, 1024], P(None, 'chan')
- grad_first_shortgain: float32 [1024], P('chan')
- grad_first_shortbias: float32 [1024], P('chan')
- grad_second_reduce: float32 [1024, 256], P(None, 'chan')
- grad_second_reducegain: float32 [256], P('chan')
- grad_second_reducebias: float32 [256], P('chan')
- grad_second_split: float32 [3, 3, 128, 2, 256], P(None, None, None, None, 'chan')
- grad_second_splitgain: float32 [2, 256], P(None, 'chan')
- grad_second_splitbias: float32 [2, 256], P(None, 'chan')
- grad_second_squeeze: float32 [256, 128], P('chan')
- grad_second_squeezegain: float32 [128], replicated
- grad_second_squeezebias: float32 [128], replicated
- grad_second_excite: float32 [128, 2, 256], P(None, None, 'chan')
- grad_second_excitebias: float32 [2, 256], P(None, 'chan')
- grad_second_expand: float32 [256, 1024], P(None, 'chan')
- grad_second_expandgain: float32 [1024], P('chan')
- grad_second_expandbias: float32 [1024], P('chan')
The draws below stay inside these ranges and needn't reach their ends.
Inputs may be any that keep to these rules, and one draw needn't show every extreme that they name: `groups`: an image of group g holds real pixels in the top-left (16 - 4 + 2 g) squared pixels of its output tile and twice that side of its input tile; all other pixels are padding.
All inputs are finite; a program needn't handle non-finite values.
Results may differ from the reference program's by a relative error of at most 0.033.
Values may be sent and summed in bfloat16 or wider, within the bound.
A program may use at most 256 MiB of HBM per device.

```python
import jax
import jax.numpy as jnp
from jax import lax

C_IN = 512
C_OUT = 1024
MID = 256
ATT = 128
RADIX = 2
HOUT = 16
IMAGES = 64


def with_ends(drawn, own_key, low, largest):
    longest = drawn.shape.index(max(drawn.shape))
    spots = []
    for shift in (0, 1):
        where = [jax.random.randint(jax.random.fold_in(own_key, axis), (), 0, length) for axis, length in enumerate(drawn.shape)]
        where[longest] = (where[longest] + shift) % drawn.shape[longest]
        spots.append(tuple(where))
    return drawn.at[spots[0]].set(low).at[spots[1]].set(largest)


def block_levels(stream_key, shape, pieces, smallest, largest):
    loudness = 1.0
    for position, parts in pieces:
        steps = jax.random.uniform(jax.random.fold_in(jax.random.fold_in(stream_key, 6), position), (parts,), jnp.float32, smallest / len(pieces), largest / len(pieces))
        loudness = loudness * jnp.repeat(jnp.exp(steps), shape[position] // parts).reshape((-1,) + (1,) * (len(shape) - 1 - position))
    return loudness


def gaussian(rng, dims, deviation, most, cuts=(), kind=jnp.bfloat16):
    loudness = block_levels(rng, dims, cuts, -0.22, 0.18) if cuts else 1.0
    values = jax.random.normal(rng, dims, jnp.float32) * deviation * loudness
    return jnp.minimum(jnp.maximum(values, -most), most).astype(kind)


def setup_inputs(seed: int = 0) -> dict:
    key_of = jax.random.split(jax.random.key(seed), 35)
    images = gaussian(key_of[0], (IMAGES, 2 * HOUT, 2 * HOUT, C_IN), 1.0, 6.0, ((0, 8), (3, 4)))
    cotangent = gaussian(key_of[1], (IMAGES, HOUT, HOUT, C_OUT), 1.0, 6.0, ((0, 8), (3, 4)))
    groups = with_ends(jax.random.randint(key_of[2], (IMAGES,), 0, 3), jax.random.fold_in(key_of[2], 1), 0, 2).astype(jnp.int32)
    first_reduce = gaussian(key_of[3], (C_IN, MID), C_IN ** -0.5, 0.25, ((1, 4),))
    first_reducegain = jnp.clip(1.0 + 0.1 * jax.random.normal(key_of[4], (MID,), jnp.float32), 0.5, 1.5)
    first_reducebias = gaussian(key_of[5], (MID,), 0.3, 1.5, ((0, 4),), jnp.float32)
    first_split = gaussian(key_of[6], (3, 3, MID // RADIX, RADIX, MID), (9 * MID // RADIX) ** -0.5, 0.1875, ((4, 4),))
    first_splitgain = jnp.clip(1.0 + 0.1 * jax.random.normal(key_of[7], (RADIX, MID), jnp.float32), 0.5, 1.5)
    first_splitbias = gaussian(key_of[8], (RADIX, MID), 0.3, 1.5, ((1, 4),), jnp.float32)
    first_squeeze = gaussian(key_of[9], (MID, ATT), MID ** -0.5, 0.375, ((0, 4),))
    first_squeezegain = jnp.clip(1.0 + 0.1 * jax.random.normal(key_of[10], (ATT,), jnp.float32), 0.5, 1.5)
    first_squeezebias = gaussian(key_of[11], (ATT,), 0.3, 1.5, (), jnp.float32)
    first_excite = gaussian(key_of[12], (ATT, RADIX, MID), ATT ** -0.5, 0.5, ((2, 4),))
    first_excitebias = gaussian(key_of[13], (RADIX, MID), 0.5, 2.0, ((1, 4),), jnp.float32)
    first_expand = gaussian(key_of[14], (MID, C_OUT), MID ** -0.5, 0.375, ((1, 4),))
    first_expandgain = jnp.clip(1.0 + 0.1 * jax.random.normal(key_of[15], (C_OUT,), jnp.float32), 0.5, 1.5)
    first_expandbias = gaussian(key_of[16], (C_OUT,), 0.3, 1.5, ((0, 4),), jnp.float32)
    first_shortcut = gaussian(key_of[17], (C_IN, C_OUT), C_IN ** -0.5, 0.25, ((1, 4),))
    first_shortgain = jnp.clip(1.0 + 0.1 * jax.random.normal(key_of[18], (C_OUT,), jnp.float32), 0.5, 1.5)
    first_shortbias = gaussian(key_of[19], (C_OUT,), 0.3, 1.5, ((0, 4),), jnp.float32)
    second_reduce = gaussian(key_of[20], (C_OUT, MID), C_OUT ** -0.5, 0.1875, ((1, 4),))
    second_reducegain = jnp.clip(1.0 + 0.1 * jax.random.normal(key_of[21], (MID,), jnp.float32), 0.5, 1.5)
    second_reducebias = gaussian(key_of[22], (MID,), 0.3, 1.5, ((0, 4),), jnp.float32)
    second_split = gaussian(key_of[23], (3, 3, MID // RADIX, RADIX, MID), (9 * MID // RADIX) ** -0.5, 0.1875, ((4, 4),))
    second_splitgain = jnp.clip(1.0 + 0.1 * jax.random.normal(key_of[24], (RADIX, MID), jnp.float32), 0.5, 1.5)
    second_splitbias = gaussian(key_of[25], (RADIX, MID), 0.3, 1.5, ((1, 4),), jnp.float32)
    second_squeeze = gaussian(key_of[26], (MID, ATT), MID ** -0.5, 0.375, ((0, 4),))
    second_squeezegain = jnp.clip(1.0 + 0.1 * jax.random.normal(key_of[27], (ATT,), jnp.float32), 0.5, 1.5)
    second_squeezebias = gaussian(key_of[28], (ATT,), 0.3, 1.5, (), jnp.float32)
    second_excite = gaussian(key_of[29], (ATT, RADIX, MID), ATT ** -0.5, 0.5, ((2, 4),))
    second_excitebias = gaussian(key_of[30], (RADIX, MID), 0.5, 2.0, ((1, 4),), jnp.float32)
    second_expand = gaussian(key_of[31], (MID, C_OUT), MID ** -0.5, 0.375, ((1, 4),))
    second_expandgain = jnp.clip(1.0 + 0.1 * jax.random.normal(key_of[32], (C_OUT,), jnp.float32), 0.5, 1.5)
    second_expandbias = gaussian(key_of[33], (C_OUT,), 0.3, 1.5, ((0, 4),), jnp.float32)
    return dict(images=images, cotangent=cotangent, groups=groups, first_reduce=first_reduce, first_reducegain=first_reducegain, first_reducebias=first_reducebias, first_split=first_split, first_splitgain=first_splitgain, first_splitbias=first_splitbias, first_squeeze=first_squeeze, first_squeezegain=first_squeezegain, first_squeezebias=first_squeezebias, first_excite=first_excite, first_excitebias=first_excitebias, first_expand=first_expand, first_expandgain=first_expandgain, first_expandbias=first_expandbias, first_shortcut=first_shortcut, first_shortgain=first_shortgain, first_shortbias=first_shortbias, second_reduce=second_reduce, second_reducegain=second_reducegain, second_reducebias=second_reducebias, second_split=second_split, second_splitgain=second_splitgain, second_splitbias=second_splitbias, second_squeeze=second_squeeze, second_squeezegain=second_squeezegain, second_squeezebias=second_squeezebias, second_excite=second_excite, second_excitebias=second_excitebias, second_expand=second_expand, second_expandgain=second_expandgain, second_expandbias=second_expandbias)


HIGHEST = lax.Precision.HIGHEST
EPSILON = 1e-05

@jax.custom_vjp
def low(v):
    return lax.optimization_barrier(v.astype(jnp.bfloat16)).astype(jnp.float32)

@jax.custom_vjp
def low_back(v):
    return v

def low_keep(v):
    return (low(v), None)

def low_pass(kept, grad):
    return (grad,)

def back_keep(v):
    return (v, None)

def back_low(kept, grad):
    return (low(grad),)
low.defvjp(low_keep, low_pass)
low_back.defvjp(back_keep, back_low)

def to_float(array_value):
    return array_value.astype(jnp.float32)

def normalize(values, mask, count, norm_gain, norm_bias):
    reduce_axes = tuple(range(values.ndim - 1))
    average = lax.optimization_barrier(jnp.sum(values * mask, axis=reduce_axes)) / count
    square = lax.optimization_barrier(jnp.sum(values * values * mask, axis=reduce_axes)) / count
    inverse = lax.rsqrt(square - average * average + EPSILON)
    return (values - average) * inverse * norm_gain + norm_bias

def pointwise(values, weight):
    return jnp.einsum('bhwc,co->bhwo', values, weight, precision=HIGHEST)

def split_attention_block(hidden_activation, block_parameters, input_mask, output_mask, input_count, output_count, valid_pixel_area, spatial_step, spatial_downsampling):
    hidden_low = low(hidden_activation)
    reduced = low_back(pointwise(hidden_low, block_parameters['reduce']))
    middle = low(jax.nn.silu(normalize(reduced, input_mask, input_count, block_parameters['reducegain'], block_parameters['reducebias'])) * input_mask)
    kernel = block_parameters['split'].reshape(3, 3, MID // RADIX, RADIX * MID)
    split_pre = low_back(lax.conv_general_dilated(middle, kernel, (spatial_step, spatial_step), ((1, 1), (1, 1)), dimension_numbers=('NHWC', 'HWIO', 'NHWC'), feature_group_count=RADIX, precision=HIGHEST))
    split_act = jax.nn.silu(normalize(split_pre, output_mask, output_count, block_parameters['splitgain'].reshape(-1), block_parameters['splitbias'].reshape(-1))) * output_mask
    shaped = split_act.reshape(split_act.shape[:3] + (RADIX, MID))
    pooled_mean = lax.optimization_barrier(jnp.sum(shaped, axis=(1, 2, 3))) / valid_pixel_area[:, None]
    squeezed = jnp.dot(pooled_mean, block_parameters['squeeze'], precision=HIGHEST)
    excited_in = jax.nn.silu(normalize(squeezed, 1.0, IMAGES * 1.0, block_parameters['squeezegain'], block_parameters['squeezebias']))
    logits = jnp.einsum('bk,krc->brc', excited_in, block_parameters['excite'], precision=HIGHEST) + block_parameters['excitebias']
    attention = jax.nn.softmax(logits, axis=1)
    mixture = low(lax.optimization_barrier(jnp.sum(shaped * attention[:, None, None], axis=3)))
    expanded = low_back(pointwise(mixture, block_parameters['expand']))
    combined = normalize(expanded, output_mask, output_count, block_parameters['expandgain'], block_parameters['expandbias'])
    if spatial_downsampling:
        dims_in = hidden_low.shape
        pooled = low(lax.optimization_barrier(jnp.mean(hidden_low.reshape(dims_in[0], dims_in[1] // 2, 2, dims_in[2] // 2, 2, dims_in[3]), axis=(2, 4))))
        shortcut = low_back(pointwise(pooled, block_parameters['shortcut']))
        combined = combined + normalize(shortcut, output_mask, output_count, block_parameters['shortgain'], block_parameters['shortbias'])
    else:
        combined = combined + hidden_activation
    return jax.nn.silu(combined) * output_mask
FIRST_KEYS = ('reduce', 'reducegain', 'reducebias', 'split', 'splitgain', 'splitbias', 'squeeze', 'squeezegain', 'squeezebias', 'excite', 'excitebias', 'expand', 'expandgain', 'expandbias', 'shortcut', 'shortgain', 'shortbias')

def reference(images, cotangent, groups, first_reduce, first_reducegain, first_reducebias, first_split, first_splitgain, first_splitbias, first_squeeze, first_squeezegain, first_squeezebias, first_excite, first_excitebias, first_expand, first_expandgain, first_expandbias, first_shortcut, first_shortgain, first_shortbias, second_reduce, second_reducegain, second_reducebias, second_split, second_splitgain, second_splitbias, second_squeeze, second_squeezegain, second_squeezebias, second_excite, second_excitebias, second_expand, second_expandgain, second_expandbias):
    valid_side = (HOUT - 4 + 2 * groups).astype(jnp.float32)
    rows_out = jnp.arange(HOUT).astype(jnp.float32)
    rows_in = jnp.arange(2 * HOUT).astype(jnp.float32)
    output_mask = ((rows_out[None, :, None] < valid_side[:, None, None]) & (rows_out[None, None, :] < valid_side[:, None, None])).astype(jnp.float32)[..., None]
    input_mask = ((rows_in[None, :, None] < 2.0 * valid_side[:, None, None]) & (rows_in[None, None, :] < 2.0 * valid_side[:, None, None])).astype(jnp.float32)[..., None]
    valid_pixel_area = valid_side * valid_side
    output_count = jnp.sum(valid_pixel_area)
    input_count = 4.0 * output_count
    first_values = (first_reduce, first_reducegain, first_reducebias, first_split, first_splitgain, first_splitbias, first_squeeze, first_squeezegain, first_squeezebias, first_excite, first_excitebias, first_expand, first_expandgain, first_expandbias, first_shortcut, first_shortgain, first_shortbias)
    second_values = (second_reduce, second_reducegain, second_reducebias, second_split, second_splitgain, second_splitbias, second_squeeze, second_squeezegain, second_squeezebias, second_excite, second_excitebias, second_expand, second_expandgain, second_expandbias)
    first_params = dict(zip(FIRST_KEYS, [to_float(entry) for entry in first_values]))
    second_params = dict(zip(FIRST_KEYS[:14], [to_float(entry) for entry in second_values]))

    def forward(image_values, block_one, block_two):
        hidden_activation = image_values * input_mask
        middle_out = split_attention_block(hidden_activation, block_one, input_mask, output_mask, input_count, output_count, valid_pixel_area, 2, True)
        return split_attention_block(middle_out, block_two, output_mask, output_mask, output_count, output_count, valid_pixel_area, 1, False)
    outputs, pullback = jax.vjp(forward, to_float(images), first_params, second_params)
    grad_input, grad_one, grad_two = pullback(to_float(cotangent))
    results = [outputs.astype(jnp.float32), grad_input.astype(jnp.float32)]
    results = results + [grad_one[keyname] for keyname in FIRST_KEYS] + [grad_two[keyname] for keyname in FIRST_KEYS[:14]]
    return tuple(results)
```

```python
import functools
from types import SimpleNamespace

import jax
import jax.numpy as jnp
from jax import lax
from jax.experimental import pallas as pl
from jax.experimental.pallas import tpu as pltpu
from jax.sharding import PartitionSpec as P

EPSILON = 1e-05
F32, BF16 = jnp.float32, jnp.bfloat16
HIGHEST = lax.Precision.HIGHEST
MESH = pl.DeviceIdType.MESH
LANES = 128
TAPS = 9
DP, CHAN = "dp", "chan"
REDUCE, SPLIT, SQUEEZE, EXCITE, EXPAND, SHORTCUT = range(6)
MATRIX, MID_VECTOR, PAIR_VECTOR, ATT_VECTOR, OUT_VECTOR = range(5)
SYNC_ROWS = (24, 8, 8, 16, 8, 8, 8, 16, 16, 8, 8, 8, 24, 8, 8, 8)

NT = (((1,), (1,)), ((), ()))
NN = (((1,), (0,)), ((), ()))
TN = (((0,), (0,)), ((), ()))


def dot(a, b, dims=NN):
    return lax.dot_general(a, b, dims, preferred_element_type=F32)


def dot_exact(a, b, dims=NN):
    return lax.dot_general(
        a.astype(F32), b.astype(F32), dims, precision=HIGHEST, preferred_element_type=F32
    )


def sigmoid(v):
    return 0.5 * jnp.tanh(0.5 * v) + 0.5


def silu(v):
    return v * sigmoid(v)


def silu_slope(v):
    q = sigmoid(v)
    return q * (1.0 + v * (1.0 - q))


def tiled(v, width):
    return jnp.concatenate([v] * (width // LANES), axis=1) if width > LANES else v


def sum8(v):
    return jnp.sum(v.reshape(v.shape[0] // 8, 8, v.shape[1]), axis=0)


def fold(v):
    return jnp.sum(v, axis=0, keepdims=True)


def span(start, size):
    if isinstance(start, int):
        return pl.ds(start, size)
    return pl.ds(pl.multiple_of(start, size), size)


class Sizes:
    def __init__(self, mesh, images, reduce_w, expand_w, squeeze_w):
        self.nd, self.nc = mesh.shape[DP], mesh.shape[CHAN]
        self.b = images.shape[0] // self.nc
        self.si = images.shape[1]
        self.so = self.si // 2
        self.cis = images.shape[3]
        self.ci = self.cis * self.nc
        self.mids = reduce_w.shape[1]
        self.mid = self.mids * self.nc
        self.cos = expand_w.shape[1]
        self.co = self.cos * self.nc
        self.att = squeeze_w.shape[1]
        self.po = self.so * self.so
        self.pi = self.si * self.si
        self.no = self.b * self.po
        self.ni = self.b * self.pi
        self.grp = self.mid // 2
        self.kk = TAPS * self.grp
        cin = {1: self.ci, 2: self.co}
        self.piece_rows = {
            (k, name): rows
            for k in (1, 2)
            for name, rows in (
                (REDUCE, cin[k] // LANES * self.mids),
                (SPLIT, 2 * TAPS * self.mids),
                (SQUEEZE, self.mids),
                (EXCITE, 2 * self.mids),
                (EXPAND, self.cos // LANES * self.mid),
                (SHORTCUT, self.cos // LANES * self.ci),
            )
        }
        self.lay, self.rows = {}, {}
        for group, members in GROUPS.items():
            at = 0
            for key in members:
                self.lay[key] = (group, at)
                at += self.piece_rows[key]
            self.rows[group] = -(-at // (16 * self.nd)) * 16 * self.nd


GROUPS = {
    0: ((2, EXPAND), (2, EXCITE), (2, SQUEEZE), (2, SPLIT), (2, REDUCE)),
    1: ((1, EXPAND), (1, EXCITE), (1, SHORTCUT)),
    2: ((1, SPLIT), (1, SQUEEZE)),
    3: ((1, REDUCE),),
}
VEC_ROWS = {
    1: SimpleNamespace(rg=0, rb=1, sg=2, sb=4, xb=6, eg=8, eb=10, hg=12, hb=14, qg=16, qb=17),
    2: SimpleNamespace(rg=18, rb=19, sg=20, sb=22, xb=24, eg=26, eb=28, qg=30, qb=31),
}
NVEC = 32
STO_ROWS = {
    2: SimpleNamespace(eb=0, eg=8, qb=16, qg=17, sb=18, sg=22, rb=26, rg=28, xb=30),
    1: SimpleNamespace(eb=34, eg=42, qb=50, qg=51, sb=52, sg=56, rb=60, rg=62, xb=64, hg=68),
}
NSTO = 80
QUARTERS = 4


def space(tree):
    if not isinstance(tree, dict):
        return tree
    inner = {k: space(v) for k, v in tree.items()}
    return SimpleNamespace(**inner) if all(isinstance(k, str) for k in inner) else inner


def scratch_tree(z):
    def f32(*shape):
        return pltpu.VMEM(shape, F32)

    def bf16(*shape):
        return pltpu.VMEM(shape, BF16)

    def sem(*shape):
        return pltpu.SemaphoreType.DMA(shape)

    ns = z.nd * z.nc // 2
    return dict(
        x=bf16(z.ni, z.ci),
        cot=bf16(z.no, z.co),
        wsh=bf16(z.ci, z.co),
        vv=f32(z.nc, NVEC, LANES),
        mo=f32(z.no, LANES),
        mi=bf16(z.ni, LANES),
        red1=f32(z.mid // LANES, z.b * z.so, 2, z.si, LANES),
        u1=f32(z.mid // LANES, z.b * z.so, 2, z.si, LANES),
        pool=bf16(z.no, z.ci),
        short=f32(z.no, z.co),
        h=bf16(z.no, z.co),
        red2=f32(z.no, z.mid),
        u2=f32(z.no, z.mid),
        g=f32(z.no, z.co),
        eg=bf16(z.no, z.co),
        shg=bf16(z.no, z.co),
        mg=f32(z.no, z.mid),
        su=f32(z.no, 2 * z.mid),
        sgb=bf16(z.no, 2 * z.mid),
        sgt=bf16(2 * z.mid, z.no),
        mixt=bf16(z.mid, z.no),
        dcol=f32(z.po + 2 * z.so, z.kk),
        rg1=bf16(z.ni, z.mid),
        rgt=bf16(z.mid, z.ni),
        pg=bf16(z.no, z.ci),
        ags=f32(8, 2 * z.mid),
        mgr=f32(8, z.mid),
        blk={
            k: dict(
                wrt=bf16(z.mid, z.ci if k == 1 else z.co),
                wst=bf16(TAPS, 2, z.mid, z.grp),
                sq=bf16(z.mid, z.att),
                ext=bf16(2, z.mid, z.att),
                we=bf16(z.mid, z.co),
                im=bf16(2, z.no + 2 * z.so, z.kk),
                sp=f32(z.no, 2 * z.mid),
                sa=f32(z.no, 2 * z.mid),
                mix=bf16(z.no, z.mid),
                exp=f32(z.no, z.co),
                att=f32(8, 2 * z.mid),
                pm=f32(8, z.mid),
            )
            for k in (1, 2)
        },
        group={
            n: dict(
                pk=bf16(z.nc // 2, 2, rows, LANES),
                r1=bf16(z.nc // 2, rows, LANES),
                r2=bf16(rows, LANES),
                r3=bf16(z.nd, rows // z.nd, LANES),
                q1=sem(2),
                q2=sem(2),
                q3s=sem(z.nd),
                q3r=sem(z.nd),
                q4s=sem(z.nd),
                q4r=sem(z.nd),
            )
            for n, rows in z.rows.items()
        },
        sync={
            k: dict(sa=f32(rows, LANES), sb=f32(rows, LANES), st=f32(rows, LANES))
            for k, rows in enumerate(SYNC_ROWS)
        },
        slots={p: f32(ns, max(SYNC_ROWS), LANES) for p in range(2)},
        gather_send=sem(13, z.nc),
        gather_recv=sem(13, z.nc),
        image_send=sem(QUARTERS, z.nc),
        image_recv=sem(QUARTERS, z.nc),
        out_send=sem(1 + QUARTERS, z.nc),
        out_got=sem(1 + QUARTERS, z.nc),
        s0s=sem(1),
        s0r=sem(2),
        s1s=sem(ns),
        s1r=sem(2, ns),
    )


def mega_kernel(z, tree, *refs):
    given, made, r = (space(t) for t in jax.tree.unflatten(tree, refs))
    nc, nd = z.nc, z.nd
    b, so, si, po, pi_, no, ni = z.b, z.so, z.si, z.po, z.pi, z.no, z.ni
    mid, co, ci, att, grp, kk = z.mid, z.co, z.ci, z.att, z.grp, z.kk
    d, c = lax.axis_index(DP), lax.axis_index(CHAN)
    ns = nd * nc // 2
    me = d * (nc // 2) + lax.div(c, 2)
    odd = lax.rem(c, 2)

    def chan_at(i):
        return lax.rem(c + i, nc)

    def place(s):
        return (lax.div(s, nc // 2), lax.rem(s, nc // 2) * 2 + odd)

    partner = (d, c + 1 - 2 * odd)

    barrier = pltpu.get_barrier_semaphore()
    for i in range(1, nc):
        pl.semaphore_signal(barrier, inc=1, device_id=(d, chan_at(i)), device_id_type=MESH)

    def greet(j, _):
        pl.semaphore_signal(
            barrier, inc=1, device_id=place(lax.rem(me + j, ns)), device_id_type=MESH
        )
        return 0

    lax.fori_loop(1, ns, greet, 0)
    pl.semaphore_wait(barrier, nc - 1 + ns - 1)

    class Exchange:
        def __init__(self, src, dst, send, recv):
            self.src, self.dst, self.send, self.recv = src, dst, send, recv

        def copy(self, i):
            to = chan_at(i)
            return pltpu.make_async_remote_copy(
                src_ref=self.src(to), dst_ref=self.dst(c), send_sem=self.send.at[i],
                recv_sem=self.recv.at[i], device_id=(d, to), device_id_type=MESH,
            )

        def local(self):
            return pltpu.make_async_copy(self.src(c), self.dst(c), self.recv.at[0])

        def start(self):
            for i in (2, 1, 3) if nc == 4 else range(1, nc):
                self.copy(i).start()
            self.local().start()

        def wait(self):
            self.local().wait()
            for i in range(1, nc):
                frm = lax.rem(c - i + nc, nc)
                pltpu.make_async_remote_copy(
                    src_ref=self.src(c), dst_ref=self.dst(frm), send_sem=self.send.at[i],
                    recv_sem=self.recv.at[i], device_id=(d, frm), device_id_type=MESH,
                ).wait_recv()
                self.copy(i).wait_send()

    gs_sem, gr_sem = r.gather_send, r.gather_recv
    xs_sem, xr_sem = r.image_send, r.image_recv
    os_sem, or_sem = r.out_send, r.out_got

    def lanes_of(ref, width):
        return lambda s: ref.at[:, pl.ds(pl.multiple_of(s * width, LANES), width)]

    def rows_of(ref, size):
        return lambda s: ref.at[pl.ds(pl.multiple_of(s * size, size), size), :]

    def mids_of(ref, size):
        return lambda s: ref.at[:, pl.ds(pl.multiple_of(s * size, size), size), :]

    def taps_of(ref, size):
        return lambda s: ref.at[:, :, pl.ds(pl.multiple_of(s * size, size), size), :]

    whole = lambda ref: (lambda s: ref)
    ms = z.mids
    sem_rows = iter(range(13))

    def gathered(src, dst):
        e = next(sem_rows)
        return Exchange(src, dst, gs_sem.at[e], gr_sem.at[e])

    ex = SimpleNamespace(
        vec=gathered(whole(given.vec), lambda s: r.vv.at[s]),
        wsh=gathered(whole(given.wsh), lanes_of(r.wsh, z.cos)),
        cot=gathered(rows_of(given.cot, no), lanes_of(r.cot, z.cos)),
        blk={
            k: SimpleNamespace(
                wrt=gathered(whole(given.blk[k].wrt), rows_of(r.blk[k].wrt, ms)),
                wst=gathered(whole(given.blk[k].wst), taps_of(r.blk[k].wst, ms)),
                sq=gathered(whole(given.blk[k].sq), rows_of(r.blk[k].sq, ms)),
                ext=gathered(whole(given.blk[k].ext), mids_of(r.blk[k].ext, ms)),
                we=gathered(whole(given.blk[k].we), lanes_of(r.blk[k].we, z.cos)),
            )
            for k in (1, 2)
        },
        x=[],
    )
    nq = QUARTERS
    part = ni // nq
    for q in range(nq):
        ex.x.append(Exchange(
            lambda s, q=q: given.images.at[pl.ds(pl.multiple_of(s * ni + q * part, part), part), :],
            lambda s, q=q: r.x.at[
                pl.ds(q * part, part), pl.ds(pl.multiple_of(s * z.cis, LANES), z.cis)
            ],
            xs_sem.at[q],
            xr_sem.at[q],
        ))
    ex.blk[1].wrt.start()
    ex.vec.start()
    ex.x[0].start()
    ex.wsh.start()
    for q in range(1, nq):
        ex.x[q].start()
    for k in (1, 2):
        w = ex.blk[k]
        for e in ((w.wst, w.sq, w.ext, w.we) if k == 1 else (w.wrt, w.wst, w.sq, w.ext, w.we)):
            e.start()
    ex.cot.start()

    ss0, rs0, ss1, rs1 = r.s0s, r.s0r, r.s1s, r.s1r

    def put(k, row, v):
        for t in range(v.shape[1] // LANES):
            r.sync[k].sa[row + t : row + t + 1, :] = v[:, t * LANES : (t + 1) * LANES]

    def allreduce(k, used, meanwhile=None):
        sa, sb, st = r.sync[k].sa, r.sync[k].sb, r.sync[k].st
        rows = SYNC_ROWS[k]
        sc = r.slots[k % 2].at[:, :rows, :]
        if used < rows:
            sa[used:rows, :] = jnp.zeros((rows - used, LANES), F32)
        first = pltpu.make_async_remote_copy(
            src_ref=sa, dst_ref=sb, send_sem=ss0.at[0], recv_sem=rs0.at[k % 2],
            device_id=partner, device_id_type=MESH,
        )
        first.start()
        first.wait()
        pair = sa[...] + sb[...]
        sc[me] = pair

        def send(i, _):
            j = lax.rem(i + ns // 3, ns - 1) + 1
            pltpu.make_async_remote_copy(
                src_ref=sc.at[me], dst_ref=sc.at[me], send_sem=ss1.at[j],
                recv_sem=rs1.at[k % 2, me], device_id=place(lax.rem(me + j, ns)),
                device_id_type=MESH,
            ).start()
            return 0

        lax.fori_loop(0, ns - 1, send, 0)

        if meanwhile is not None:
            meanwhile()

        def arrive(j, _):
            s = lax.rem(me + j, ns)
            pltpu.make_async_remote_copy(
                src_ref=sc.at[me], dst_ref=sc.at[s], send_sem=ss1.at[j],
                recv_sem=rs1.at[k % 2, s], device_id=place(s), device_id_type=MESH,
            ).wait()
            return 0

        lax.fori_loop(1, ns, arrive, 0)
        if ns <= 16:
            total = sc[0]
            for s in range(1, ns):
                total = total + sc[s]
        else:
            total = lax.fori_loop(1, ns, lambda s, t: t + sc[s], sc[0])
        st[...] = total

    def total(k, row, width):
        st = r.sync[k].st
        return jnp.concatenate(
            [st[row + t : row + t + 1, :] for t in range(width // LANES)], axis=1
        )

    sto = made.sto

    def keep(row, v):
        for t in range(v.shape[1] // LANES):
            sto[row + t : row + t + 1, :] = v[:, t * LANES : (t + 1) * LANES]

    half = lambda rows: lax.broadcasted_iota(jnp.int32, (rows, LANES), 0)
    groups = given.groups
    sides = [(so - 4 + 2 * groups[c * b + k]) for k in range(b)]
    areas = [(s * s).astype(F32) for s in sides]
    for k in range(b):
        def fill_out(t, _, k=k):
            p = half(2 * so) + t * (2 * so)
            ok = (lax.div(p, so) < sides[k]) & (lax.rem(p, so) < sides[k])
            r.mo[span(k * po + t * (2 * so), 2 * so), :] = jnp.where(ok, 1.0, 0.0)
            return 0

        lax.fori_loop(0, po // (2 * so), fill_out, 0)

        def fill_in(t, _, k=k):
            p = half(2 * si) + t * (2 * si)
            ok = (lax.div(p, si) < 2 * sides[k]) & (lax.rem(p, si) < 2 * sides[k])
            r.mi[span(k * pi_ + t * (2 * si), 2 * si), :] = jnp.where(ok, 1.0, 0.0).astype(BF16)
            return 0

        lax.fori_loop(0, pi_ // (2 * si), fill_in, 0)
    row8 = lax.broadcasted_iota(jnp.int32, (8, LANES), 0)
    live8 = jnp.where(row8 < b, 1.0, 0.0)
    inv_area = jnp.zeros((8, LANES), F32)
    for k in range(b):
        inv_area = jnp.where(row8 == k, 1.0 / jnp.full((8, LANES), areas[k], F32), inv_area)
    for ref in (r.blk[1].pm, r.blk[2].pm, r.ags):
        ref[...] = jnp.zeros_like(ref)

    pool_rows = part // 4

    def pool_matrix(out_axis):
        shape = (pool_rows, part) if out_axis == 0 else (part, pool_rows)
        o = lax.broadcasted_iota(jnp.int32, shape, out_axis)
        p = lax.broadcasted_iota(jnp.int32, shape, 1 - out_axis)
        row, col = lax.div(p, si), lax.rem(p, si)
        hit = (lax.div(row, 2) * so + lax.div(col, 2)) == o
        return jnp.where(hit, 0.25, 0.0).astype(BF16)

    low_half = lax.broadcasted_iota(jnp.int32, (1, LANES), 1) < z.mids
    vv = r.vv

    def v_mid(row):
        return jnp.concatenate(
            [
                jnp.where(low_half, vv[s, row : row + 1, :], vv[s + 1, row : row + 1, :])
                for s in range(0, nc, 2)
            ],
            axis=1,
        )

    def v_split(row):
        return jnp.concatenate([v_mid(row), v_mid(row + 1)], axis=1)

    def v_co(row):
        return jnp.concatenate(
            [
                vv[s, row + t : row + t + 1, :]
                for s in range(nc)
                for t in range(z.cos // LANES)
            ],
            axis=1,
        )

    def norm(k, row1, row2, width, inv_n, gain, bias):
        n = tiled(inv_n, width)
        mean = total(k, row1, width) * n
        inv = lax.rsqrt(total(k, row2, width) * n - mean * mean + EPSILON)
        scale = gain * inv
        return SimpleNamespace(mean=mean, inv=inv, gs=scale, sh=bias - mean * scale)

    def norm_grad(k, rowu, rowv, width, inv_n, nm):
        n = tiled(inv_n, width)
        su = total(k, rowu, width)
        sux = nm.inv * (total(k, rowv, width) - nm.mean * su)
        t = sux * n
        return (
            su,
            sux,
            nm.gs * (su * n - nm.mean * nm.inv * t),
            nm.gs * nm.inv * t,
        )

    def loop(n, tile, body, init):
        def step(i, carry):
            return body(pl.multiple_of(i * tile, tile), carry)

        return lax.fori_loop(0, n // tile, step, init)

    def zero8(width):
        return jnp.zeros((8, width), F32)

    def moments(ref, rows, width, tile):
        def body(at, carry):
            s1, s2 = carry
            v = ref[pl.ds(at, tile), :]
            mv = v * tiled(r.mo[pl.ds(at, tile), :], width)
            return s1 + sum8(mv), s2 + sum8(mv * v)

        s1, s2 = loop(rows, tile, body, (zero8(width), zero8(width)))
        return fold(s1), fold(s2)

    red1 = r.red1

    def row_pair(ref, i):
        return jnp.concatenate(
            [ref[t, pl.ds(i, 1)].reshape(2 * si, LANES) for t in range(mid // LANES)], axis=1
        )

    def phase_of(t, lead, p, q):
        return red1[t, lead, p, pl.ds(q, so, stride=2), :].reshape(4 * so, LANES)

    pool_m = pool_matrix(0)
    ex.blk[1].wrt.wait()
    r1, r2 = zero8(mid), zero8(mid)
    for q in range(nq):
        ex.x[q].wait()
        xv = r.x[q * part : (q + 1) * part, :]
        lead = part // (2 * si)
        reduced = dot(xv, r.blk[1].wrt[...], NT)
        for t in range(mid // LANES):
            red1[t, q * lead : (q + 1) * lead] = reduced[:, t * LANES : (t + 1) * LANES].reshape(
                lead, 2, si, LANES
            )

        def red_sums(i, carry, q=q, lead=lead):
            s1, s2 = carry
            v = row_pair(red1, q * lead + i)
            m = r.mi[span((q * lead + i) * 2 * si, 2 * si), :].astype(F32)
            mv = v * tiled(m, mid)
            return s1 + sum8(mv), s2 + sum8(mv * v)

        r1, r2 = lax.fori_loop(0, lead, red_sums, (r1, r2))
        pooled = dot(pool_m, xv).astype(BF16)
        r.pool[q * pool_rows : (q + 1) * pool_rows, :] = pooled
    ex.wsh.wait()
    for n0 in range(0, co, 256):
        r.short[:, n0 : n0 + 256] = dot(r.pool[...], r.wsh[:, n0 : n0 + 256])
    h1, h2 = moments(r.short, no, co, 16)
    put(0, 0, fold(r1))
    put(0, mid // LANES, fold(r2))
    at = 2 * mid // LANES
    put(0, at, h1)
    put(0, at + co // LANES, h2)
    local_area = areas[0]
    for k in range(1, b):
        local_area = local_area + areas[k]
    put(0, at + 2 * co // LANES, jnp.full((1, LANES), local_area, F32))
    allreduce(0, at + 2 * co // LANES + 1)
    ex.vec.wait()
    count = total(0, at + 2 * co // LANES, LANES)
    inv_out = 1.0 / count
    inv_in = 0.25 * inv_out
    vr1, vr2 = VEC_ROWS[1], VEC_ROWS[2]
    nred1 = norm(0, 0, mid // LANES, mid, inv_in, v_mid(vr1.rg), v_mid(vr1.rb))
    nshort = norm(0, at, at + co // LANES, co, inv_out, v_co(vr1.hg), v_co(vr1.hb))

    lane16 = lax.rem(lax.broadcasted_iota(jnp.int32, (4 * so, mid), 0), so)
    not_first = lane16 > 0
    not_last = lane16 < so - 1

    def im_put(im, at, w, di, dj, shift):
        tap = di * 3 + dj
        low = w.astype(BF16)
        for g in range(2):
            im[g, pl.ds(pl.multiple_of(at + so + shift * so, so), 4 * so), tap * grp : (tap + 1) * grp] = (
                low[:, g * grp : (g + 1) * grp]
            )

    def im_zero(im, di, last):
        for k in range(b):
            row = so + k * po + (po - so if last else 0)
            for g in range(2):
                im[g, row : row + so, di * 3 * grp : (di + 1) * 3 * grp] = jnp.zeros(
                    (so, 3 * grp), BF16
                )

    im1 = r.blk[1].im

    def build1(i, _):
        at = pl.multiple_of(i * 4 * so, 4 * so)
        m = tiled(r.mo[pl.ds(at, 4 * so), :], mid)
        for p in range(2):
            for q in range(2):
                v = jnp.concatenate(
                    [phase_of(t, pl.ds(i * 4, 4), p, q) for t in range(mid // LANES)], axis=1
                )
                w = silu(v * nred1.gs + nred1.sh) * m
                for dj in ((1,) if q == 0 else (2, 0)):
                    wj = w
                    if dj == 0:
                        wj = jnp.where(not_first, pltpu.roll(w, 1, 0), 0.0)
                    for di in ((1,) if p == 0 else (2, 0)):
                        im_put(im1, at, wj, di, dj, 1 if di == 0 else 0)
        return 0

    lax.fori_loop(0, no // (4 * so), build1, 0)
    im_zero(im1, 0, False)

    def split_weights(k, g):
        return jnp.concatenate([r.blk[k].wst[t, g] for t in range(TAPS)], axis=1)

    def split_conv(k):
        ex.blk[k].wst.wait()
        for g in range(2):
            r.blk[k].sp[:, g * mid : (g + 1) * mid] = dot(
                r.blk[k].im[g, so : so + no, :], split_weights(k, g), NT
            )
        return moments(r.blk[k].sp, no, 2 * mid, 32)

    def attention_forward(k, vr, sync):
        s1, s2 = split_conv(k)
        put(sync, 0, s1)
        put(sync, 4, s2)
        allreduce(sync, 8)
        nsplit = norm(sync, 0, 4, 2 * mid, inv_out, v_split(vr.sg), v_split(vr.sb))
        sp, sa, pm = r.blk[k].sp, r.blk[k].sa, r.blk[k].pm
        for img in range(b):
            def act(at, s, img=img):
                rows = pl.ds(pl.multiple_of(at + img * po, 32), 32)
                v = silu(sp[rows, :] * nsplit.gs + nsplit.sh)
                v = v * tiled(r.mo[rows, :], 2 * mid)
                sa[rows, :] = v
                return s + sum8(v)

            s = fold(loop(po, 32, act, zero8(2 * mid)))
            pm[img : img + 1, :] = (s[:, :mid] + s[:, mid:]) * tiled(inv_area[img : img + 1, :], mid)
        ex.blk[k].sq.wait()
        squeezed = dot_exact(pm[...], r.blk[k].sq[...])
        put(sync + 1, 0, fold(squeezed))
        put(sync + 1, 1, fold(squeezed * squeezed))
        put(sync + 1, 2, fold(pm[...]))
        allreduce(sync + 1, 4)
        inv_images = jnp.full((1, LANES), 1.0 / (b * nc * nd), F32)
        natt = norm(
            sync + 1, 0, 1, att, inv_images, vv[0, vr.qg : vr.qg + 1, :],
            vv[0, vr.qb : vr.qb + 1, :],
        )
        xhat = (squeezed - natt.mean) * natt.inv
        centred = pm[...] - total(sync + 1, 2, mid) * tiled(inv_images, mid)
        pre = squeezed * natt.gs + natt.sh
        excited = silu(pre) * live8
        ex.blk[k].ext.wait()
        halves = []
        for g in range(2):
            bias = v_mid(vr.xb + g)
            halves.append(dot_exact(excited, r.blk[k].ext[g], NT) + bias)
        top = jnp.maximum(halves[0], halves[1])
        e0, e1 = jnp.exp(halves[0] - top), jnp.exp(halves[1] - top)
        whole_sum = e0 + e1
        at_ref = r.blk[k].att
        at_ref[:, :mid] = e0 / whole_sum
        at_ref[:, mid:] = e1 / whole_sum
        for img in range(b):
            def mix(at, _, img=img):
                rows = pl.ds(pl.multiple_of(at + img * po, 32), 32)
                v = sa[rows, :] * at_ref[img : img + 1, :]
                r.blk[k].mix[rows, :] = (v[:, :mid] + v[:, mid:]).astype(BF16)
                return 0

            loop(po, 32, mix, 0)
        ex.blk[k].we.wait()
        for n0 in range(0, co, 256):
            r.blk[k].exp[:, n0 : n0 + 256] = dot(r.blk[k].mix[...], r.blk[k].we[:, n0 : n0 + 256])
        s1, s2 = moments(r.blk[k].exp, no, co, 16)
        put(sync + 2, 0, s1)
        put(sync + 2, co // LANES, s2)
        allreduce(sync + 2, 2 * co // LANES)
        nexp = norm(sync + 2, 0, co // LANES, co, inv_out, v_co(vr.eg), v_co(vr.eb))
        return SimpleNamespace(nsplit=nsplit, natt=natt, xhat=xhat, pre=pre, excited=excited, nexp=nexp, centred=centred)

    f1 = attention_forward(1, vr1, 1)

    def summed1(rows):
        return (
            r.blk[1].exp[rows, :] * f1.nexp.gs
            + f1.nexp.sh
            + r.short[rows, :] * nshort.gs
            + nshort.sh
        )

    def hidden(at, _):
        rows = pl.ds(at, 16)
        r.h[rows, :] = (silu(summed1(rows)) * tiled(r.mo[rows, :], co)).astype(BF16)
        return 0

    loop(no, 16, hidden, 0)

    ex.blk[2].wrt.wait()
    r.red2[...] = dot(r.h[...], r.blk[2].wrt[...], NT)
    s1, s2 = moments(r.red2, no, mid, 64)
    put(4, 0, s1)
    put(4, 2, s2)
    allreduce(4, 4)
    nred2 = norm(4, 0, 2, mid, inv_out, v_mid(vr2.rg), v_mid(vr2.rb))
    im2 = r.blk[2].im

    def build2(i, _):
        at = pl.multiple_of(i * 4 * so, 4 * so)
        m = tiled(r.mo[pl.ds(at, 4 * so), :], mid)
        w = silu(r.red2[pl.ds(at, 4 * so), :] * nred2.gs + nred2.sh) * m
        for dj in range(3):
            wj = w
            if dj == 0:
                wj = jnp.where(not_first, pltpu.roll(w, 1, 0), 0.0)
            if dj == 2:
                wj = jnp.where(not_last, pltpu.roll(w, 4 * so - 1, 0), 0.0)
            for di in range(3):
                im_put(im2, at, wj, di, dj, 1 - di)
        return 0

    lax.fori_loop(0, no // (4 * so), build2, 0)
    im_zero(im2, 0, False)
    im_zero(im2, 2, True)
    f2 = attention_forward(2, vr2, 5)

    ex.cot.wait()

    def finish(at, carry):
        su, sv = carry
        rows = pl.ds(at, 16)
        m = tiled(r.mo[rows, :], co)
        v = r.blk[2].exp[rows, :]
        s = v * f2.nexp.gs + f2.nexp.sh + r.h[rows, :].astype(F32)
        q = sigmoid(s)
        u = r.cot[rows, :].astype(F32) * m * (q * (1.0 + s * (1.0 - q)))
        r.cot[rows, :] = (s * q * m).astype(BF16)
        r.g[rows, :] = u
        return su + sum8(u), sv + sum8(u * v)

    su, sv = loop(no, 16, finish, (zero8(co), zero8(co)))
    out_ex = Exchange(
        lambda s: r.cot.at[:, pl.ds(pl.multiple_of(s * z.cos, LANES), z.cos)],
        lambda s: made.out.at[pl.ds(pl.multiple_of(s * no, no), no), :],
        os_sem.at[0],
        or_sem.at[0],
    )
    out_ex.start()
    put(8, 0, fold(su))
    put(8, co // LANES, fold(sv))
    allreduce(8, 2 * co // LANES)

    def pack_rows(k, name, skip, v):
        group, at = z.lay[(k, name)]
        at, share = at + skip * z.mids, z.mids
        for s in range(nc):
            for t in range(v.shape[1] // LANES):
                r.group[group].pk[s // 2, s % 2, at + t * share : at + (t + 1) * share, :] = v[
                    s * share : (s + 1) * share, t * LANES : (t + 1) * LANES
                ].astype(BF16)

    def pack_lanes(k, name, s, v):
        group, at = z.lay[(k, name)]
        rows = v.shape[0]
        for t in range(v.shape[1] // LANES):
            r.group[group].pk[s // 2, s % 2, at + t * rows : at + (t + 1) * rows, :] = v[
                :, t * LANES : (t + 1) * LANES
            ].astype(BF16)

    class Reduction:
        def __init__(self, group):
            own = r.group[group]
            self.pk, self.r1, self.r2, self.r3 = own.pk, own.r1, own.r2, own.r3
            self.rows = z.rows[group]
            self.piece = self.rows // nd
            self.res = made.res[group]
            self.sems = [own.q1, own.q2, own.q3s, own.q3r, own.q4s, own.q4r]
            self.across = lax.div(c, 2)

        def piece_at(self, n):
            return pl.ds(pl.multiple_of(n * self.piece, 16), self.piece)

        def copy1(self):
            return pltpu.make_async_remote_copy(
                src_ref=self.pk.at[:, 1 - odd], dst_ref=self.r1, send_sem=self.sems[0].at[0],
                recv_sem=self.sems[0].at[1], device_id=partner, device_id_type=MESH,
            )

        def copy2(self):
            return pltpu.make_async_remote_copy(
                src_ref=self.pk.at[1 - self.across, odd], dst_ref=self.r2,
                send_sem=self.sems[1].at[0], recv_sem=self.sems[1].at[1],
                device_id=(d, chan_at(2)), device_id_type=MESH,
            )

        def copy3(self, to, src):
            return pltpu.make_async_remote_copy(
                src_ref=self.pk.at[self.across, odd, self.piece_at(to), :],
                dst_ref=self.r3.at[src], send_sem=self.sems[2].at[to],
                recv_sem=self.sems[3].at[src], device_id=(to, c), device_id_type=MESH,
            )

        def copy4(self, to, src):
            return pltpu.make_async_remote_copy(
                src_ref=self.r3.at[d], dst_ref=self.res.at[self.piece_at(src), :],
                send_sem=self.sems[4].at[to], recv_sem=self.sems[5].at[src],
                device_id=(to, c), device_id_type=MESH,
            )

        def local4(self):
            return pltpu.make_async_copy(
                self.r3.at[d], self.res.at[self.piece_at(d), :], self.sems[5].at[d]
            )

        def add(self, which, other):
            def body(at, _):
                rows = pl.ds(at, 128)
                self.pk[which, odd, rows, :] = (
                    self.pk[which, odd, rows, :].astype(F32) + other(rows).astype(F32)
                ).astype(BF16)
                return 0

            loop(self.rows, 128, body, 0)

        def step1(self):
            self.copy1().start()

        def step2(self):
            self.copy1().wait()
            away = 1 - self.across
            self.add(away, lambda rows: self.r1[away, rows, :])
            self.copy2().start()
            self.add(self.across, lambda rows: self.r1[self.across, rows, :])

        def step3(self):
            self.copy2().wait_recv()
            self.add(self.across, lambda rows: self.r2[rows, :])

            def send(j, _):
                self.copy3(lax.rem(d + j, nd), d).start()
                return 0

            lax.fori_loop(1, nd, send, 0)
            self.copy2().wait_send()

        def step4(self):
            self.r3[d] = self.pk[self.across, odd, self.piece_at(d), :]

            def arrive(j, _):
                to, src = lax.rem(d + j, nd), lax.rem(d - j + nd, nd)
                self.copy3(to, d).wait_send()
                self.copy3(src, src).wait_recv()
                return 0

            lax.fori_loop(1, nd, arrive, 0)

            def body(at, _):
                rows = pl.ds(at, 16)

                def term(n, t):
                    return t + self.r3[n, rows, :].astype(F32)

                t = self.r3[0, rows, :].astype(F32)
                if nd <= 8:
                    for n in range(1, nd):
                        t = term(n, t)
                else:
                    t = lax.fori_loop(1, nd, term, t)
                self.r3[d, rows, :] = t.astype(BF16)
                return 0

            loop(self.piece, 16, body, 0)
            self.local4().start()

            def send(j, _):
                self.copy4(lax.rem(d + j, nd), d).start()
                return 0

            lax.fori_loop(1, nd, send, 0)

        def finish(self):
            self.local4().wait()

            def arrive(j, _):
                to, src = lax.rem(d + j, nd), lax.rem(d - j + nd, nd)
                self.copy4(to, d).wait_send()
                self.copy4(src, src).wait_recv()
                return 0

            lax.fori_loop(1, nd, arrive, 0)

    sums_of = {group: Reduction(group) for group in GROUPS}

    def attention_backward(k, f, sync):
        srow = STO_ROWS[k]
        nexp, nsplit, natt = f.nexp, f.nsplit, f.natt
        first = k == 1
        cw = co // LANES
        su, sux, ea, eb = norm_grad(sync, 0, cw, co, inv_out, nexp)
        keep(srow.eb, su)
        keep(srow.eg, sux)
        if first:
            _, suxh, ha, hb = norm_grad(sync, 0, 2 * cw, co, inv_out, nshort)
            keep(srow.hg, suxh)

        def expand_grad(at, _):
            rows = pl.ds(at, 16)
            m = tiled(r.mo[rows, :], co)
            u = r.g[rows, :]
            r.eg[rows, :] = (nexp.gs * u - m * (ea + eb * r.blk[k].exp[rows, :])).astype(BF16)
            if first:
                r.shg[rows, :] = (
                    nshort.gs * u - m * (ha + hb * r.short[rows, :])
                ).astype(BF16)
            return 0

        loop(no, 16, expand_grad, 0)
        r.mg[...] = dot(r.eg[...], r.blk[k].we[...], NT)
        sa = r.blk[k].sa
        for img in range(b):
            def att_grad(at, s, img=img):
                rows = pl.ds(pl.multiple_of(at + img * po, 32), 32)
                return s + sum8(sa[rows, :] * tiled_pair(r.mg[rows, :]))

            r.ags[img : img + 1, :] = fold(loop(po, 32, att_grad, zero8(2 * mid)))
        ags, at_ref = r.ags, r.blk[k].att
        a0, a1 = at_ref[:, :mid], at_ref[:, mid:]
        g0, g1 = ags[:, :mid], ags[:, mid:]
        mean = a0 * g0 + a1 * g1
        l0, l1 = a0 * (g0 - mean), a1 * (g1 - mean)
        ext = r.blk[k].ext
        excited_grad = dot_exact(l0, ext[0]) + dot_exact(l1, ext[1])
        au = excited_grad * silu_slope(f.pre)
        put(sync + 1, 0, fold(au))
        put(sync + 1, 1, fold(au * f.xhat))
        put(sync + 1, 2, fold(l0))
        put(sync + 1, 4, fold(l1))

        def matrices():
            r.mixt[...] = jnp.transpose(r.blk[k].mix[...])
            for s in range(nc):
                share = slice(s * z.cos, (s + 1) * z.cos)
                pack_lanes(k, EXPAND, s, dot(r.mixt[...], r.eg[:, share]))
            pack_rows(k, EXCITE, 0, dot_exact(l0, f.excited, TN))
            pack_rows(k, EXCITE, 1, dot_exact(l1, f.excited, TN))
            if first:
                r.sgt[...] = jnp.transpose(r.pool[...])
                for s in range(nc):
                    share = slice(s * z.cos, (s + 1) * z.cos)
                    pack_lanes(k, SHORTCUT, s, dot(r.sgt[...], r.shg[:, share]))
                sums_of[1].step1()
                r.pg[...] = dot(r.shg[...], r.wsh[...], NT).astype(BF16)

        allreduce(sync + 1, 6, matrices)
        inv_images = 1.0 / (b * nc * nd)
        su, sux = total(sync + 1, 0, att), total(sync + 1, 1, att)
        keep(srow.qb, su)
        keep(srow.qg, sux)
        keep(srow.xb, total(sync + 1, 2, 2 * mid))
        sb = natt.gs * (au - su * inv_images - f.xhat * (sux * inv_images)) * live8
        if first:
            sums_of[0].step3()
            sums_of[1].step2()
        r.mgr[...] = dot_exact(sb, r.blk[k].sq[...], NT) * tiled(inv_area, mid)
        sp = r.blk[k].sp
        carry = (zero8(2 * mid), zero8(2 * mid))
        for img in range(b):
            def split_up(at, carry, img=img):
                s1, s2 = carry
                rows = pl.ds(pl.multiple_of(at + img * po, 32), 32)
                m = tiled(r.mo[rows, :], 2 * mid)
                v = sp[rows, :]
                grad = tiled_pair(r.mg[rows, :]) * at_ref[img : img + 1, :] + tiled_pair(
                    r.mgr[img : img + 1, :]
                )
                u = grad * m * silu_slope(v * nsplit.gs + nsplit.sh)
                r.su[rows, :] = u
                return s1 + sum8(u), s2 + sum8(u * v)

            carry = loop(po, 32, split_up, carry)
        put(sync + 2, 0, fold(carry[0]))
        put(sync + 2, 4, fold(carry[1]))

        def squeeze_matrix():
            pack_rows(k, SQUEEZE, 0, dot_exact(f.centred, sb, TN))

        allreduce(sync + 2, 8, squeeze_matrix)
        su, sux, ca, cb = norm_grad(sync + 2, 0, 4, 2 * mid, inv_out, nsplit)
        keep(srow.sb, su)
        keep(srow.sg, sux)

        def split_grad(at, _):
            rows = pl.ds(at, 32)
            m = tiled(r.mo[rows, :], 2 * mid)
            r.sgb[rows, :] = (
                nsplit.gs * r.su[rows, :] - m * (ca + cb * sp[rows, :])
            ).astype(BF16)
            return 0

        loop(no, 32, split_grad, 0)

    def tiled_pair(v):
        return jnp.concatenate([v, v], axis=1)

    def split_matrix(k):
        r.sgt[...] = jnp.transpose(r.sgb[...])
        for g in range(2):
            for t in range(3):
                v = dot(
                    r.sgt[g * mid : (g + 1) * mid, :],
                    r.blk[k].im[g, so : so + no, 3 * t * grp : 3 * (t + 1) * grp],
                )
                for u in range(3):
                    pack_rows(
                        k, SPLIT, (3 * t + u) * 2 + g, v[:, u * grp : (u + 1) * grp]
                    )

    dcol = r.dcol
    dcol[:so, :] = jnp.zeros((so, kk), F32)
    dcol[so + po :, :] = jnp.zeros((so, kk), F32)

    def columns(k, img, g):
        dcol[so : so + po, :] = dot(
            r.sgb[img * po : (img + 1) * po, g * mid : (g + 1) * mid], split_weights(k, g)
        )

    tile = 4 * so
    first_g, last_g = not_first[:, :grp], not_last[:, :grp]

    def tap(at, di, dj, shift):
        t = di * 3 + dj
        return dcol[pl.ds(pl.multiple_of(at + so - shift * so, so), tile), t * grp : (t + 1) * grp]

    def from_left(v):
        return jnp.where(first_g, pltpu.roll(v, 1, 0), 0.0)

    def from_right(v):
        return jnp.where(last_g, pltpu.roll(v, tile - 1, 0), 0.0)

    attention_backward(2, f2, 8)
    sums = []
    for g in range(2):
        carry = (zero8(grp), zero8(grp))
        lanes = slice(g * grp, (g + 1) * grp)
        for img in range(b):
            columns(2, img, g)

            def back2(at, carry, img=img, g=g, lanes=lanes):
                s1, s2 = carry
                cols = [
                    tap(at, 0, dj, -1) + tap(at, 1, dj, 0) + tap(at, 2, dj, 1) for dj in range(3)
                ]
                grad = cols[1] + from_right(cols[0]) + from_left(cols[2])
                rows = pl.ds(pl.multiple_of(at + img * po, tile), tile)
                v = r.red2[rows, lanes]
                u = (
                    grad
                    * tiled(r.mo[rows, :], grp)
                    * silu_slope(v * nred2.gs[:, lanes] + nred2.sh[:, lanes])
                )
                r.u2[rows, lanes] = u
                return s1 + sum8(u), s2 + sum8(u * v)

            carry = loop(po, tile, back2, carry)
        sums.append(carry)
    put(11, 0, jnp.concatenate([fold(s[0]) for s in sums], axis=1))
    put(11, 2, jnp.concatenate([fold(s[1]) for s in sums], axis=1))
    allreduce(11, 4, lambda: split_matrix(2))
    su, sux, ca, cb = norm_grad(11, 0, 2, mid, inv_out, nred2)
    keep(STO_ROWS[2].rb, su)
    keep(STO_ROWS[2].rg, sux)

    def reduce_grad2(at, _):
        rows = pl.ds(at, 64)
        m = tiled(r.mo[rows, :], mid)
        r.rg1[rows, :] = (
            nred2.gs * r.u2[rows, :] - m * (ca + cb * r.red2[rows, :])
        ).astype(BF16)
        return 0

    loop(no, 64, reduce_grad2, 0)
    for n0 in range(0, co, 256):
        cols = slice(n0, n0 + 256)
        r.g[:, cols] = r.g[:, cols] + dot(r.rg1[:no, :], r.blk[2].wrt[:, cols])

    def first_up(at, carry):
        s1, s2, s3 = carry
        rows = pl.ds(at, 16)
        u = r.g[rows, :] * tiled(r.mo[rows, :], co) * silu_slope(summed1(rows))
        r.g[rows, :] = u
        return (
            s1 + sum8(u),
            s2 + sum8(u * r.blk[1].exp[rows, :]),
            s3 + sum8(u * r.short[rows, :]),
        )

    s1, s2, s3 = loop(no, 16, first_up, (zero8(co), zero8(co), zero8(co)))
    put(12, 0, fold(s1))
    put(12, co // LANES, fold(s2))
    put(12, 2 * co // LANES, fold(s3))

    def reduce_matrix2():
        r.rgt[:, :no] = jnp.transpose(r.rg1[:no, :])
        for n0 in range(0, co, 256):
            pack_rows(2, REDUCE, n0 // LANES, dot(r.rgt[:, :no], r.h[:, n0 : n0 + 256]))
        sums_of[0].step1()

    allreduce(12, 3 * co // LANES, reduce_matrix2)
    sums_of[0].step2()

    attention_backward(1, f1, 12)
    sums = []
    for g in range(2):
        carry = (zero8(grp), zero8(grp))
        lanes = slice(g * grp, (g + 1) * grp)
        for img in range(b):
            columns(1, img, g)

            def back1(at, carry, img=img, g=g, lanes=lanes):
                s1, s2 = carry
                rows = pl.ds(pl.multiple_of(at + img * po, tile), tile)
                m = tiled(r.mo[rows, :], grp)
                lead = pl.ds(pl.multiple_of(lax.div(at, so) + img * so, 4), 4)
                for p in range(2):
                    for q in range(2):
                        def col(dj):
                            if p == 0:
                                return tap(at, 1, dj, 0)
                            return tap(at, 0, dj, -1) + tap(at, 2, dj, 0)

                        grad = col(1) if q == 0 else col(2) + from_right(col(0))
                        v = phase_of(g, lead, p, q)
                        u = grad * m * silu_slope(v * nred1.gs[:, lanes] + nred1.sh[:, lanes])
                        r.u1[g, lead, p, pl.ds(q, so, stride=2), :] = u.reshape(4, so, grp)
                        s1, s2 = s1 + sum8(u), s2 + sum8(u * v)
                return s1, s2

            carry = loop(po, tile, back1, carry)
        sums.append(carry)
    put(15, 0, jnp.concatenate([fold(s[0]) for s in sums], axis=1))
    put(15, 2, jnp.concatenate([fold(s[1]) for s in sums], axis=1))

    def split_matrix1():
        split_matrix(1)
        sums_of[2].step1()

    allreduce(15, 4, split_matrix1)
    sums_of[0].step4()
    sums_of[2].step2()
    su, sux, ca, cb = norm_grad(15, 0, 2, mid, inv_in, nred1)
    keep(STO_ROWS[1].rb, su)
    keep(STO_ROWS[1].rg, sux)

    def reduce_grad1(i, _):
        rows = pl.ds(pl.multiple_of(i * 2 * si, 2 * si), 2 * si)
        m = tiled(r.mi[rows, :].astype(F32), mid)
        u, v = row_pair(r.u1, i), row_pair(red1, i)
        r.rg1[rows, :] = (nred1.gs * u - m * (ca + cb * v)).astype(BF16)
        return 0

    lax.fori_loop(0, b * so, reduce_grad1, 0)
    r.rgt[...] = jnp.transpose(r.rg1[...])
    for n0 in range(0, ci, 256):
        pack_rows(1, REDUCE, n0 // LANES, dot(r.rgt[...], r.x[:, n0 : n0 + 256]))
    sums_of[3].step1()
    sums_of[1].step3()
    spread = pool_matrix(1)
    last = []
    for q in range(nq):
        rows = slice(q * part, (q + 1) * part)
        m = tiled(r.mi[rows, :].astype(F32), 256)
        for n0 in range(0, ci, 256):
            cols = slice(n0, n0 + 256)
            v = dot(r.rg1[rows, :], r.blk[1].wrt[:, cols]) + dot(
                spread, r.pg[q * pool_rows : (q + 1) * pool_rows, cols]
            )
            r.x[rows, cols] = (v * m).astype(BF16)
        e = Exchange(
            lambda s, q=q: r.x.at[
                pl.ds(q * part, part), pl.ds(pl.multiple_of(s * z.cis, LANES), z.cis)
            ],
            lambda s, q=q: made.gx.at[
                pl.ds(pl.multiple_of(s * ni + q * part, part), part), :
            ],
            os_sem.at[1 + q],
            or_sem.at[1 + q],
        )
        e.start()
        last.append(e)
    sums_of[3].step2()
    sums_of[2].step3()
    sums_of[1].step4()
    sums_of[3].step3()
    sums_of[2].step4()
    sums_of[3].step4()
    out_ex.wait()
    for e in last:
        e.wait()
    for sums in (sums_of[0], sums_of[1], sums_of[2], sums_of[3]):
        sums.finish()


class Weights:
    def __init__(self, values):
        (
            self.reduce, self.reducegain, self.reducebias,
            self.split, self.splitgain, self.splitbias,
            self.squeeze, self.squeezegain, self.squeezebias,
            self.excite, self.excitebias,
            self.expand, self.expandgain, self.expandbias,
        ) = values[:14]
        self.extra = values[14:]


def doubled(v):
    return jnp.concatenate([v, v], axis=-1).reshape(-1, LANES)


def per_device(mesh, images, cotangent, groups, *weights):
    first, second = Weights(weights[:17]), Weights(weights[17:])
    z = Sizes(mesh, images, first.reduce, first.expand, first.squeeze)

    def vectors(w):
        parts = [
            doubled(w.reducegain[None]), doubled(w.reducebias[None]),
            doubled(w.splitgain), doubled(w.splitbias), doubled(w.excitebias),
        ]
        parts += [v.reshape(-1, LANES) for v in (w.expandgain, w.expandbias) + w.extra[1:]]
        return parts + [w.squeezegain.reshape(-1, LANES), w.squeezebias.reshape(-1, LANES)]

    def block(w):
        return dict(
            wrt=w.reduce.T,
            wst=jnp.transpose(w.split, (0, 1, 3, 4, 2)).reshape(TAPS, 2, z.mids, z.grp),
            sq=w.squeeze,
            ext=jnp.transpose(w.excite, (1, 2, 0)),
            we=w.expand,
        )

    inputs = dict(
        images=images.reshape(-1, z.cis),
        cot=cotangent.reshape(-1, z.cos),
        groups=groups,
        vec=jnp.concatenate(vectors(first) + vectors(second), axis=0),
        wsh=first.extra[0],
        blk={1: block(first), 2: block(second)},
    )
    in_specs = jax.tree.map(lambda v: pl.BlockSpec(memory_space=pl.ANY), inputs)
    in_specs.update(groups=pl.BlockSpec(memory_space=pltpu.SMEM))
    outs = dict(
        out=jax.ShapeDtypeStruct((z.nc * z.no, z.cos), BF16),
        gx=jax.ShapeDtypeStruct((z.nc * z.ni, z.cis), BF16),
        sto=jax.ShapeDtypeStruct((NSTO, LANES), F32),
        res={n: jax.ShapeDtypeStruct((rows, LANES), BF16) for n, rows in z.rows.items()},
    )
    out_specs = jax.tree.map(lambda v: pl.BlockSpec(memory_space=pl.ANY), outs)
    out_specs.update(sto=pl.BlockSpec(memory_space=pltpu.VMEM))
    scratch = scratch_tree(z)
    tree = jax.tree.structure((inputs, outs, scratch))
    results = pl.pallas_call(
        functools.partial(mega_kernel, z, tree),
        out_shape=jax.tree.leaves(outs),
        in_specs=jax.tree.leaves(in_specs),
        out_specs=jax.tree.leaves(out_specs),
        scratch_shapes=jax.tree.leaves(scratch),
        compiler_params=pltpu.CompilerParams(
            collective_id=0, has_side_effects=True, vmem_limit_bytes=62 << 20
        ),
        name="two_blocks",
    )(*jax.tree.leaves(inputs))
    return unpack(z, jax.tree.unflatten(jax.tree.structure(outs), results))


def unpack_kernel(z, plan, tree, *refs):
    given, (out_image, gx, *outs) = jax.tree.unflatten(tree, refs)
    given = space(given)
    out_in, gx_in, sto, res = given.out, given.gx, given.sto, given.res
    c = lax.axis_index(CHAN)
    out_image[...] = out_in[...].astype(F32)
    gx[...] = gx_in[...].astype(F32)

    def mid_share(row):
        v = sto[pl.ds(row + lax.div(c, 2), 1), :]
        return jnp.where(lax.rem(c, 2) == 0, v[:, : z.mids], v[:, z.mids :])

    @pl.when(pl.program_id(0) == 0)
    def _():
        for (kind, k, name), o in zip(plan, outs):
            if kind == MATRIX:
                group, at = z.lay[(k, name)]
                rows = o.shape[0]
                for t in range(o.shape[1] // LANES):
                    o[:, t * LANES : (t + 1) * LANES] = res[group][
                        at + t * rows : at + (t + 1) * rows, :
                    ].astype(F32)
                continue
            row = name
            if kind == MID_VECTOR:
                o[...] = mid_share(row)
            elif kind == PAIR_VECTOR:
                o[0:1, :] = mid_share(row)
                o[1:2, :] = mid_share(row + z.mid // LANES)
            elif kind == ATT_VECTOR:
                o[...] = sto[row : row + 1, :]
            else:
                n = z.cos // LANES
                for t in range(n):
                    o[:, t * LANES : (t + 1) * LANES] = sto[pl.ds(row + c * n + t, 1), :]


def unpack(z, results):
    plan = []
    for k in (1, 2):
        v = STO_ROWS[k]
        plan += [
            (MATRIX, k, REDUCE), (MID_VECTOR, k, v.rg), (MID_VECTOR, k, v.rb),
            (MATRIX, k, SPLIT), (PAIR_VECTOR, k, v.sg), (PAIR_VECTOR, k, v.sb),
            (MATRIX, k, SQUEEZE), (ATT_VECTOR, k, v.qg), (ATT_VECTOR, k, v.qb),
            (MATRIX, k, EXCITE), (PAIR_VECTOR, k, v.xb),
            (MATRIX, k, EXPAND), (OUT_VECTOR, k, v.eg), (OUT_VECTOR, k, v.eb),
        ]
        if k == 1:
            plan += [(MATRIX, k, SHORTCUT), (OUT_VECTOR, k, v.hg), (OUT_VECTOR, k, v.eb)]

    def shape_of(kind, k, name):
        if kind == MATRIX:
            return (
                (z.mids, z.ci if k == 1 else z.co),
                (2 * TAPS * z.mids, LANES),
                (z.mids, z.att),
                (2 * z.mids, z.att),
                (z.mid, z.cos),
                (z.ci, z.cos),
            )[name]
        return (None, (1, z.mids), (2, z.mids), (1, z.att), (1, z.cos))[kind]

    shapes = [shape_of(*entry) for entry in plan]
    steps = 8
    whole = lambda shape: pl.BlockSpec(shape, lambda i: (0, 0))
    slab = lambda v: pl.BlockSpec((v.shape[0] // steps, v.shape[1]), lambda i: (i, 0))
    in_specs = {n: slab(v) if n in ("out", "gx") else jax.tree.map(lambda a: whole(a.shape), v)
                for n, v in results.items()}
    images = [results["out"], results["gx"]]
    outs = [jax.ShapeDtypeStruct(v.shape, F32) for v in images]
    outs += [jax.ShapeDtypeStruct(s, F32) for s in shapes]
    flat = pl.pallas_call(
        functools.partial(unpack_kernel, z, plan, jax.tree.structure((results, outs))),
        grid=(steps,),
        out_shape=outs,
        in_specs=jax.tree.leaves(in_specs),
        out_specs=[slab(v) for v in images] + [whole(s) for s in shapes],
        compiler_params=pltpu.CompilerParams(vmem_limit_bytes=40 << 20),
        name="unpack",
    )(*jax.tree.leaves(results))
    final = [
        flat[0].reshape(z.nc * z.b, z.so, z.so, z.cos),
        flat[1].reshape(z.nc * z.b, z.si, z.si, z.cis),
    ]
    for (kind, _, name), v in zip(plan, flat[2:]):
        if (kind, name) == (MATRIX, REDUCE):
            v = v.T
        elif (kind, name) == (MATRIX, SPLIT):
            v = jnp.transpose(v.reshape(3, 3, 2, z.mids, z.grp), (0, 1, 4, 2, 3))
        elif (kind, name) == (MATRIX, EXCITE):
            v = jnp.transpose(v.reshape(2, z.mids, z.att), (2, 0, 1))
        elif kind in (MID_VECTOR, ATT_VECTOR, OUT_VECTOR):
            v = v.reshape(-1)
        final.append(v)
    return tuple(final)


def specs():
    block = [
        P(None, CHAN), P(CHAN), P(CHAN),
        P(None, None, None, None, CHAN), P(None, CHAN), P(None, CHAN),
        P(CHAN, None), P(), P(), P(None, None, CHAN), P(None, CHAN),
        P(None, CHAN), P(CHAN), P(CHAN),
    ]
    short = [P(None, CHAN), P(CHAN), P(CHAN)]
    return block + short + block


def solution(mesh):
    image = P(DP, None, None, CHAN)
    return jax.shard_map(
        functools.partial(per_device, mesh),
        mesh=mesh,
        in_specs=tuple([image, image, P(DP)] + specs()),
        out_specs=tuple([image, image] + specs()),
        check_vma=False,
    )
```

```python
import functools
from types import SimpleNamespace

import jax
import jax.numpy as jnp
from jax import lax
from jax.experimental import pallas as pl
from jax.experimental.pallas import tpu as pltpu
from jax.sharding import PartitionSpec as P

EPSILON = 1e-05
F32, BF16 = jnp.float32, jnp.bfloat16
HIGHEST = lax.Precision.HIGHEST
MESH = pl.DeviceIdType.MESH
LANES = 128
TAPS = 9
DP, CHAN = "dp", "chan"
REDUCE, SPLIT, SQUEEZE, EXCITE, EXPAND, SHORTCUT = range(6)
MATRIX, MID_VECTOR, PAIR_VECTOR, ATT_VECTOR, OUT_VECTOR = range(5)
SYNC_ROWS = (8, 8, 8, 32, 8, 8, 8, 16, 16, 8, 8, 8, 24, 8, 8, 8)

NT = (((1,), (1,)), ((), ()))
NN = (((1,), (0,)), ((), ()))
TN = (((0,), (0,)), ((), ()))


def dot(a, b, dims=NN):
    return lax.dot_general(a, b, dims, preferred_element_type=F32)


def dot_exact(a, b, dims=NN):
    return lax.dot_general(
        a.astype(F32), b.astype(F32), dims, precision=HIGHEST, preferred_element_type=F32
    )


def sigmoid(v):
    return 0.5 * jnp.tanh(0.5 * v) + 0.5


def silu(v):
    return v * sigmoid(v)


def silu_slope(v):
    q = sigmoid(v)
    return q * (1.0 + v * (1.0 - q))


def tiled(v, width):
    return jnp.concatenate([v] * (width // LANES), axis=1) if width > LANES else v


def sum8(v):
    return jnp.sum(v.reshape(v.shape[0] // 8, 8, v.shape[1]), axis=0)


def fold(v):
    return jnp.sum(v, axis=0, keepdims=True)


def span(start, size):
    if isinstance(start, int):
        return pl.ds(start, size)
    return pl.ds(pl.multiple_of(start, size), size)


class Sizes:
    def __init__(self, mesh, images, reduce_w, expand_w, squeeze_w):
        self.nd, self.nc = mesh.shape[DP], mesh.shape[CHAN]
        self.near = min(self.nd, 8)
        self.far = self.nd // self.near
        self.b = images.shape[0] // self.nc
        self.si = images.shape[1]
        self.so = self.si // 2
        self.cis = images.shape[3]
        self.ci = self.cis * self.nc
        self.mids = reduce_w.shape[1]
        self.mid = self.mids * self.nc
        self.cos = expand_w.shape[1]
        self.co = self.cos * self.nc
        self.att = squeeze_w.shape[1]
        self.po = self.so * self.so
        self.pi = self.si * self.si
        self.no = self.b * self.po
        self.ni = self.b * self.pi
        self.grp = self.mid // 2
        self.kk = TAPS * self.grp
        cin = {1: self.ci, 2: self.co}
        self.piece_rows = {
            (k, name): rows
            for k in (1, 2)
            for name, rows in (
                (REDUCE, cin[k] // LANES * self.mids),
                (SPLIT, 2 * TAPS * self.mids),
                (SQUEEZE, self.mids),
                (EXCITE, 2 * self.mids),
                (EXPAND, self.cos // LANES * self.mid),
                (SHORTCUT, self.cos // LANES * self.ci),
            )
        }
        self.lay, self.rows = {}, {}
        for group, members in GROUPS.items():
            at = 0
            for key in members:
                self.lay[key] = (group, at)
                at += self.piece_rows[key]
            self.rows[group] = -(-at // (16 * self.near)) * 16 * self.near


GROUPS = {
    0: ((2, EXPAND), (2, EXCITE)),
    1: ((2, SPLIT), (2, SQUEEZE)),
    2: ((2, REDUCE), (1, EXPAND), (1, EXCITE), (1, SHORTCUT)),
    3: ((1, SPLIT), (1, SQUEEZE)),
    4: ((1, REDUCE),),
}
VEC_ROWS = {
    1: SimpleNamespace(rg=0, rb=1, sg=2, sb=4, xb=6, eg=8, eb=10, hg=12, hb=14, qg=16, qb=17),
    2: SimpleNamespace(rg=18, rb=19, sg=20, sb=22, xb=24, eg=26, eb=28, qg=30, qb=31),
}
NVEC = 32
STO_ROWS = {
    2: SimpleNamespace(eb=0, eg=8, qb=16, qg=17, sb=18, sg=22, rb=26, rg=28, xb=30),
    1: SimpleNamespace(eb=34, eg=42, qb=50, qg=51, sb=52, sg=56, rb=60, rg=62, xb=64, hg=68),
}
NSTO = 80
QUARTERS = 4


def space(tree):
    if not isinstance(tree, dict):
        return tree
    inner = {k: space(v) for k, v in tree.items()}
    return SimpleNamespace(**inner) if all(isinstance(k, str) for k in inner) else inner


def scratch_tree(z, vec):
    def f32(*shape):
        return pltpu.VMEM(shape, F32)

    def bf16(*shape):
        return pltpu.VMEM(shape, BF16)

    def sem(*shape):
        return pltpu.SemaphoreType.DMA(shape)

    ns = z.nd * z.nc // 2
    return dict(
        x=bf16(z.ni, z.ci),
        cot=bf16(z.no, z.co),
        wsh=bf16(z.ci, z.co),
        vv=f32(z.nc, NVEC, LANES),
        vmine=f32(NVEC, LANES),
        vraw=[f32(*v.shape) for v in vec],
        vsem=sem(len(vec)),
        mo=f32(z.no, LANES),
        mi=bf16(z.ni, LANES),
        red1=f32(z.mid // LANES, z.b * z.so, 2, z.si, LANES),
        u1=f32(z.mid // LANES, z.b * z.so, 2, z.si, LANES),
        pool=bf16(z.no, z.ci),
        short=f32(z.no, z.co),
        h=bf16(z.no, z.co),
        red2=f32(z.no, z.mid),
        u2=f32(z.no, z.mid),
        g=f32(z.no, z.co),
        eg=bf16(z.no, z.co),
        shg=bf16(z.no, z.co),
        mg=f32(z.no, z.mid),
        su=f32(z.no, 2 * z.mid),
        sgb=bf16(z.no, 2 * z.mid),
        sgt=bf16(2 * z.mid, z.no),
        mixt=bf16(z.mid, z.no),
        dcol=f32(z.po + 2 * z.so, z.kk),
        rg1=bf16(z.ni, z.mid),
        rgt=bf16(z.mid, z.ni),
        pg=bf16(z.no, z.ci),
        ags=f32(8, 2 * z.mid),
        mgr=f32(8, z.mid),
        blk={
            k: dict(
                wrt=bf16(z.mid, z.ci if k == 1 else z.co),
                wst=bf16(TAPS, 2, z.mid, z.grp),
                sq=bf16(z.mid, z.att),
                ext=bf16(2, z.mid, z.att),
                we=bf16(z.mid, z.co),
                im=bf16(2, z.no + 2 * z.so, z.kk),
                sp=f32(z.no, 2 * z.mid),
                sa=f32(z.no, 2 * z.mid),
                mix=bf16(z.no, z.mid),
                exp=f32(z.no, z.co),
                att=f32(8, 2 * z.mid),
                pm=f32(8, z.mid),
            )
            for k in (1, 2)
        },
        group={
            n: dict(
                pk=bf16(z.nc // 2, 2, rows, LANES),
                r1=bf16(z.nc // 2, rows, LANES),
                r2=bf16(rows, LANES),
                r3=bf16(z.near, rows // z.near, LANES),
                r4=bf16(z.far, rows // z.near, LANES),
                q1=sem(2),
                q2=sem(2),
                q3s=sem(z.near),
                q3r=sem(z.near),
                q4s=sem(z.near),
                q4r=sem(z.near),
                q5s=sem(z.far),
                q5r=sem(z.far),
            )
            for n, rows in z.rows.items()
        },
        sync={
            k: dict(sa=f32(rows, LANES), sb=f32(rows, LANES), st=f32(rows, LANES))
            for k, rows in enumerate(SYNC_ROWS)
        },
        slots={p: f32(ns, max(SYNC_ROWS), LANES) for p in range(2)},
        gather_send=sem(13, z.nc),
        gather_recv=sem(13, z.nc),
        image_send=sem(QUARTERS, z.nc),
        image_recv=sem(QUARTERS, z.nc),
        out_send=sem(1 + QUARTERS, z.nc),
        out_got=sem(1 + QUARTERS, z.nc),
        s0s=sem(1),
        s0r=sem(2),
        s1s=sem(1),
        s1r=sem(2),
    )


def mega_kernel(z, tree, *refs):
    given, made, r = (space(t) for t in jax.tree.unflatten(tree, refs))
    nc, nd = z.nc, z.nd
    b, so, si, po, pi_, no, ni = z.b, z.so, z.si, z.po, z.pi, z.no, z.ni
    mid, co, ci, att, grp, kk = z.mid, z.co, z.ci, z.att, z.grp, z.kk
    d, c = lax.axis_index(DP), lax.axis_index(CHAN)
    ns = nd * nc // 2
    me = d * (nc // 2) + lax.div(c, 2)
    odd = lax.rem(c, 2)

    def chan_at(i):
        return lax.rem(c + i, nc)

    def place(s):
        return (lax.div(s, nc // 2), lax.rem(s, nc // 2) * 2 + odd)

    partner = (d, c + 1 - 2 * odd)
    far_first = []
    if ns <= 16:
        for n in range(ns - 1):
            far_first.append(place(lax.rem(me + (n + ns // 3) % (ns - 1) + 1, ns)))

    barrier = pltpu.get_barrier_semaphore()
    for i in range(1, nc):
        pl.semaphore_signal(barrier, inc=1, device_id=(d, chan_at(i)), device_id_type=MESH)

    def greet(j, _):
        pl.semaphore_signal(
            barrier, inc=1, device_id=place(lax.rem(me + j, ns)), device_id_type=MESH
        )
        return 0

    lax.fori_loop(1, ns, greet, 0)
    pl.semaphore_wait(barrier, nc - 1 + ns - 1)

    class Exchange:
        def __init__(self, src, dst, send, recv):
            self.src, self.dst, self.send, self.recv = src, dst, send, recv

        def copy(self, i):
            to = chan_at(i)
            return pltpu.make_async_remote_copy(
                src_ref=self.src(to), dst_ref=self.dst(c), send_sem=self.send.at[i],
                recv_sem=self.recv.at[i], device_id=(d, to), device_id_type=MESH,
            )

        def local(self):
            return pltpu.make_async_copy(self.src(c), self.dst(c), self.recv.at[0])

        def start(self):
            for i in (2, 1, 3) if nc == 4 else range(1, nc):
                self.copy(i).start()
            self.local().start()

        def wait(self):
            self.local().wait()
            for i in range(1, nc):
                frm = lax.rem(c - i + nc, nc)
                pltpu.make_async_remote_copy(
                    src_ref=self.src(c), dst_ref=self.dst(frm), send_sem=self.send.at[i],
                    recv_sem=self.recv.at[i], device_id=(d, frm), device_id_type=MESH,
                ).wait_recv()
                self.copy(i).wait_send()

    class Relay:
        def __init__(self, src, dst, send, recv):
            self.src, self.dst, self.send, self.recv = src, dst, send, recv
            self.far = chan_at(2)

        def copy(self, n, src, which, to):
            return pltpu.make_async_remote_copy(
                src_ref=src, dst_ref=self.dst(which), send_sem=self.send.at[n],
                recv_sem=self.recv.at[n], device_id=to, device_id_type=MESH,
            )

        def across(self, which):
            return self.copy(1, self.src(c), which, (d, self.far))

        def beside(self, which):
            return self.copy(2, self.src(c), which, partner)

        def onward(self, which):
            return self.copy(3, self.dst(self.far), which, partner)

        def local(self):
            return pltpu.make_async_copy(self.src(c), self.dst(c), self.recv.at[0])

        def start(self):
            self.across(c).start()
            self.beside(c).start()
            self.local().start()

        def forward(self):
            self.across(self.far).wait_recv()
            self.onward(self.far).start()

        def wait(self):
            self.local().wait()
            self.across(c).wait_send()
            self.beside(c).wait_send()
            self.onward(self.far).wait_send()
            self.beside(partner[1]).wait_recv()
            self.onward(lax.rem(partner[1] + 2, nc)).wait_recv()

    gs_sem, gr_sem = r.gather_send, r.gather_recv
    xs_sem, xr_sem = r.image_send, r.image_recv
    os_sem, or_sem = r.out_send, r.out_got

    def lanes_of(ref, width):
        return lambda s: ref.at[:, pl.ds(pl.multiple_of(s * width, LANES), width)]

    def rows_of(ref, size):
        return lambda s: ref.at[pl.ds(pl.multiple_of(s * size, size), size), :]

    def mids_of(ref, size):
        return lambda s: ref.at[:, pl.ds(pl.multiple_of(s * size, size), size), :]

    def taps_of(ref, size):
        return lambda s: ref.at[:, :, pl.ds(pl.multiple_of(s * size, size), size), :]

    whole = lambda ref: (lambda s: ref)
    ms = z.mids
    sem_rows = iter(range(13))

    def gathered(src, dst, kind=Relay):
        e = next(sem_rows)
        return kind(src, dst, gs_sem.at[e], gr_sem.at[e])

    ex = SimpleNamespace(
        vec=gathered(whole(r.vmine), lambda s: r.vv.at[s], Exchange),
        wsh=gathered(whole(given.wsh), lanes_of(r.wsh, z.cos)),
        cot=gathered(rows_of(given.cot, no), lanes_of(r.cot, z.cos), Exchange),
        blk={
            k: SimpleNamespace(
                wrt=gathered(whole(given.blk[k].wrt), rows_of(r.blk[k].wrt, ms)),
                wst=gathered(whole(given.blk[k].wst), taps_of(r.blk[k].wst, ms)),
                sq=gathered(whole(given.blk[k].sq), rows_of(r.blk[k].sq, ms)),
                ext=gathered(whole(given.blk[k].ext), mids_of(r.blk[k].ext, ms)),
                we=gathered(whole(given.blk[k].we), lanes_of(r.blk[k].we, z.cos)),
            )
            for k in (1, 2)
        },
        x=[],
    )
    nq = QUARTERS
    part = ni // nq
    for q in range(nq):
        ex.x.append(Exchange(
            lambda s, q=q: given.images.at[pl.ds(pl.multiple_of(s * ni + q * part, part), part), :],
            lambda s, q=q: r.x.at[
                pl.ds(q * part, part), pl.ds(pl.multiple_of(s * z.cis, LANES), z.cis)
            ],
            xs_sem.at[q],
            xr_sem.at[q],
        ))
    first_w, second_w = ex.blk[1], ex.blk[2]
    first_w.wrt.start()
    raw = [
        pltpu.make_async_copy(v, to, r.vsem.at[n]) for n, (v, to) in enumerate(zip(given.vec, r.vraw))
    ]
    for copy in raw:
        copy.start()
    ex.x[0].start()
    for q in range(1, nq):
        ex.x[q].start()
    row = 0
    for copy, v in zip(raw, r.vraw):
        copy.wait()
        rows, width = v.shape
        for k in range(rows):
            one = v[k : k + 1, :]
            if width < LANES:
                one = jnp.concatenate([one, one], axis=1)
            for t in range(one.shape[1] // LANES):
                r.vmine[row : row + 1, :] = one[:, t * LANES : (t + 1) * LANES]
                row += 1
    ex.vec.start()

    ss0, rs0, ss1, rs1 = r.s0s, r.s0r, r.s1s, r.s1r

    def put(k, row, v):
        for t in range(v.shape[1] // LANES):
            r.sync[k].sa[row + t : row + t + 1, :] = v[:, t * LANES : (t + 1) * LANES]

    def allreduce(k, used, meanwhile=None):
        sa, sb, st = r.sync[k].sa, r.sync[k].sb, r.sync[k].st
        rows = SYNC_ROWS[k]
        sc = r.slots[k % 2].at[:, :rows, :]
        if used < rows:
            sa[used:rows, :] = jnp.zeros((rows - used, LANES), F32)
        first = pltpu.make_async_remote_copy(
            src_ref=sa, dst_ref=sb, send_sem=ss0.at[0], recv_sem=rs0.at[k % 2],
            device_id=partner, device_id_type=MESH,
        )
        first.start()
        first.wait()
        pair = sa[...] + sb[...]
        sc[me] = pair

        def send(to):
            pltpu.make_async_remote_copy(
                src_ref=sc.at[me], dst_ref=sc.at[me], send_sem=ss1.at[0],
                recv_sem=rs1.at[k % 2], device_id=to, device_id_type=MESH,
            ).start()

        if ns <= 16:
            for to in far_first:
                send(to)
        else:

            def send_one(j, _):
                send(place(lax.rem(me + j, ns)))
                return 0

            lax.fori_loop(1, ns, send_one, 0)
        if meanwhile is not None:
            meanwhile()
        others = sc.at[pl.ds(0, ns - 1)]
        pltpu.make_async_remote_copy(
            src_ref=others, dst_ref=others, send_sem=ss1.at[0], recv_sem=rs1.at[k % 2],
            device_id=partner, device_id_type=MESH,
        ).wait()
        if ns <= 16:
            total = sc[0]
            for s in range(1, ns):
                total = total + sc[s]
        else:
            total = lax.fori_loop(1, ns, lambda s, t: t + sc[s], sc[0])
        st[...] = total

    def total(k, row, width):
        st = r.sync[k].st
        return jnp.concatenate(
            [st[row + t : row + t + 1, :] for t in range(width // LANES)], axis=1
        )

    sto = made.sto

    def keep(row, v):
        for t in range(v.shape[1] // LANES):
            sto[row + t : row + t + 1, :] = v[:, t * LANES : (t + 1) * LANES]

    half = lambda rows: lax.broadcasted_iota(jnp.int32, (rows, LANES), 0)
    groups = given.groups
    sides = [(so - 4 + 2 * groups[c * b + k]) for k in range(b)]
    areas = [(s * s).astype(F32) for s in sides]
    for k in range(b):
        def fill_out(t, _, k=k):
            p = half(2 * so) + t * (2 * so)
            ok = (lax.div(p, so) < sides[k]) & (lax.rem(p, so) < sides[k])
            r.mo[span(k * po + t * (2 * so), 2 * so), :] = jnp.where(ok, 1.0, 0.0)
            return 0

        lax.fori_loop(0, po // (2 * so), fill_out, 0)

        def fill_in(t, _, k=k):
            p = half(2 * si) + t * (2 * si)
            ok = (lax.div(p, si) < 2 * sides[k]) & (lax.rem(p, si) < 2 * sides[k])
            r.mi[span(k * pi_ + t * (2 * si), 2 * si), :] = jnp.where(ok, 1.0, 0.0).astype(BF16)
            return 0

        lax.fori_loop(0, pi_ // (2 * si), fill_in, 0)
    row8 = lax.broadcasted_iota(jnp.int32, (8, LANES), 0)
    live8 = jnp.where(row8 < b, 1.0, 0.0)
    inv_area = jnp.zeros((8, LANES), F32)
    for k in range(b):
        inv_area = jnp.where(row8 == k, 1.0 / jnp.full((8, LANES), areas[k], F32), inv_area)
    for ref in (r.blk[1].pm, r.blk[2].pm, r.ags):
        ref[...] = jnp.zeros_like(ref)

    pool_rows = part // 4

    def pool_matrix(out_axis):
        shape = (pool_rows, part) if out_axis == 0 else (part, pool_rows)
        o = lax.broadcasted_iota(jnp.int32, shape, out_axis)
        p = lax.broadcasted_iota(jnp.int32, shape, 1 - out_axis)
        row, col = lax.div(p, si), lax.rem(p, si)
        hit = (lax.div(row, 2) * so + lax.div(col, 2)) == o
        return jnp.where(hit, 0.25, 0.0).astype(BF16)

    low_half = lax.broadcasted_iota(jnp.int32, (1, LANES), 1) < z.mids
    vv = r.vv

    def v_mid(row):
        return jnp.concatenate(
            [
                jnp.where(low_half, vv[s, row : row + 1, :], vv[s + 1, row : row + 1, :])
                for s in range(0, nc, 2)
            ],
            axis=1,
        )

    def v_split(row):
        return jnp.concatenate([v_mid(row), v_mid(row + 1)], axis=1)

    def v_co(row):
        return jnp.concatenate(
            [
                vv[s, row + t : row + t + 1, :]
                for s in range(nc)
                for t in range(z.cos // LANES)
            ],
            axis=1,
        )

    def norm(k, row1, row2, width, inv_n, gain, bias):
        n = tiled(inv_n, width)
        mean = total(k, row1, width) * n
        inv = lax.rsqrt(total(k, row2, width) * n - mean * mean + EPSILON)
        scale = gain * inv
        return SimpleNamespace(mean=mean, inv=inv, gs=scale, sh=bias - mean * scale)

    def norm_grad(k, rowu, rowv, width, inv_n, nm):
        n = tiled(inv_n, width)
        su = total(k, rowu, width)
        sux = nm.inv * (total(k, rowv, width) - nm.mean * su)
        t = sux * n
        return (
            su,
            sux,
            nm.gs * (su * n - nm.mean * nm.inv * t),
            nm.gs * nm.inv * t,
        )

    def loop(n, tile, body, init):
        def step(i, carry):
            return body(pl.multiple_of(i * tile, tile), carry)

        return lax.fori_loop(0, n // tile, step, init)

    def zero8(width):
        return jnp.zeros((8, width), F32)

    def moments(ref, rows, width, tile):
        def body(at, carry):
            s1, s2 = carry
            v = ref[pl.ds(at, tile), :]
            mv = v * tiled(r.mo[pl.ds(at, tile), :], width)
            return s1 + sum8(mv), s2 + sum8(mv * v)

        s1, s2 = loop(rows, tile, body, (zero8(width), zero8(width)))
        return fold(s1), fold(s2)

    red1 = r.red1

    def row_pair(ref, i):
        return jnp.concatenate(
            [ref[t, pl.ds(i, 1)].reshape(2 * si, LANES) for t in range(mid // LANES)], axis=1
        )

    def phase_of(t, lead, p, q):
        return red1[t, lead, p, pl.ds(q, so, stride=2), :].reshape(4 * so, LANES)

    pool_m = pool_matrix(0)
    first_w.wrt.forward()
    first_w.wrt.wait()
    r1, r2 = zero8(mid), zero8(mid)
    for q in range(nq):
        ex.x[q].wait()
        xv = r.x[q * part : (q + 1) * part, :]
        lead = part // (2 * si)
        reduced = dot(xv, r.blk[1].wrt[...], NT)
        for t in range(mid // LANES):
            red1[t, q * lead : (q + 1) * lead] = reduced[:, t * LANES : (t + 1) * LANES].reshape(
                lead, 2, si, LANES
            )

        def red_sums(i, carry, q=q, lead=lead):
            s1, s2 = carry
            v = row_pair(red1, q * lead + i)
            m = r.mi[span((q * lead + i) * 2 * si, 2 * si), :].astype(F32)
            mv = v * tiled(m, mid)
            return s1 + sum8(mv), s2 + sum8(mv * v)

        r1, r2 = lax.fori_loop(0, lead, red_sums, (r1, r2))
    first_w.wst.start()
    put(0, 0, fold(r1))
    put(0, mid // LANES, fold(r2))
    at = 2 * mid // LANES
    local_area = areas[0]
    for k in range(1, b):
        local_area = local_area + areas[k]
    put(0, at, jnp.full((1, LANES), local_area, F32))

    def pooling():
        for q in range(nq):
            r.pool[q * pool_rows : (q + 1) * pool_rows, :] = dot(
                pool_m, r.x[q * part : (q + 1) * part, :]
            ).astype(BF16)

    allreduce(0, at + 1, pooling)
    ex.vec.wait()
    count = total(0, at, LANES)
    inv_out = 1.0 / count
    inv_in = 0.25 * inv_out
    vr1, vr2 = VEC_ROWS[1], VEC_ROWS[2]
    nred1 = norm(0, 0, mid // LANES, mid, inv_in, v_mid(vr1.rg), v_mid(vr1.rb))
    lane16 = lax.rem(lax.broadcasted_iota(jnp.int32, (4 * so, mid), 0), so)
    not_first = lane16 > 0
    not_last = lane16 < so - 1

    def im_put(im, at, w, di, dj, shift):
        tap = di * 3 + dj
        low = w.astype(BF16)
        for g in range(2):
            im[g, pl.ds(pl.multiple_of(at + so + shift * so, so), 4 * so), tap * grp : (tap + 1) * grp] = (
                low[:, g * grp : (g + 1) * grp]
            )

    def im_zero(im, di, last):
        for k in range(b):
            row = so + k * po + (po - so if last else 0)
            for g in range(2):
                im[g, row : row + so, di * 3 * grp : (di + 1) * 3 * grp] = jnp.zeros(
                    (so, 3 * grp), BF16
                )

    im1 = r.blk[1].im

    def build1(i, _):
        at = pl.multiple_of(i * 4 * so, 4 * so)
        m = tiled(r.mo[pl.ds(at, 4 * so), :], mid)
        for p in range(2):
            for q in range(2):
                v = jnp.concatenate(
                    [phase_of(t, pl.ds(i * 4, 4), p, q) for t in range(mid // LANES)], axis=1
                )
                w = silu(v * nred1.gs + nred1.sh) * m
                for dj in ((1,) if q == 0 else (2, 0)):
                    wj = w
                    if dj == 0:
                        wj = jnp.where(not_first, pltpu.roll(w, 1, 0), 0.0)
                    for di in ((1,) if p == 0 else (2, 0)):
                        im_put(im1, at, wj, di, dj, 1 if di == 0 else 0)
        return 0

    for e in (first_w.sq, first_w.ext, first_w.we, ex.wsh):
        e.start()
    lax.fori_loop(0, no // (4 * so), build1, 0)
    first_w.wst.forward()
    im_zero(im1, 0, False)

    def split_weights(k, g):
        return jnp.concatenate([r.blk[k].wst[t, g] for t in range(TAPS)], axis=1)

    def split_conv(k):
        ex.blk[k].wst.wait()
        for g in range(2):
            r.blk[k].sp[:, g * mid : (g + 1) * mid] = dot(
                r.blk[k].im[g, so : so + no, :], split_weights(k, g), NT
            )
        return moments(r.blk[k].sp, no, 2 * mid, 32)

    def attention_forward(k, vr, sync, fills):
        s1, s2 = split_conv(k)
        put(sync, 0, s1)
        put(sync, 4, s2)
        allreduce(sync, 8, fills[0])
        nsplit = norm(sync, 0, 4, 2 * mid, inv_out, v_split(vr.sg), v_split(vr.sb))
        sp, sa, pm = r.blk[k].sp, r.blk[k].sa, r.blk[k].pm
        for img in range(b):
            def act(at, s, img=img):
                rows = pl.ds(pl.multiple_of(at + img * po, 32), 32)
                v = silu(sp[rows, :] * nsplit.gs + nsplit.sh)
                v = v * tiled(r.mo[rows, :], 2 * mid)
                sa[rows, :] = v
                return s + sum8(v)

            s = fold(loop(po, 32, act, zero8(2 * mid)))
            pm[img : img + 1, :] = (s[:, :mid] + s[:, mid:]) * tiled(inv_area[img : img + 1, :], mid)
        ex.blk[k].sq.wait()
        squeezed = dot_exact(pm[...], r.blk[k].sq[...])
        put(sync + 1, 0, fold(squeezed))
        put(sync + 1, 1, fold(squeezed * squeezed))
        put(sync + 1, 2, fold(pm[...]))
        allreduce(sync + 1, 4, fills[1])
        inv_images = jnp.full((1, LANES), 1.0 / (b * nc * nd), F32)
        natt = norm(
            sync + 1, 0, 1, att, inv_images, vv[0, vr.qg : vr.qg + 1, :],
            vv[0, vr.qb : vr.qb + 1, :],
        )
        xhat = (squeezed - natt.mean) * natt.inv
        centred = pm[...] - total(sync + 1, 2, mid) * tiled(inv_images, mid)
        pre = squeezed * natt.gs + natt.sh
        excited = silu(pre) * live8
        ex.blk[k].ext.wait()
        halves = []
        for g in range(2):
            bias = v_mid(vr.xb + g)
            halves.append(dot_exact(excited, r.blk[k].ext[g], NT) + bias)
        top = jnp.maximum(halves[0], halves[1])
        e0, e1 = jnp.exp(halves[0] - top), jnp.exp(halves[1] - top)
        whole_sum = e0 + e1
        at_ref = r.blk[k].att
        at_ref[:, :mid] = e0 / whole_sum
        at_ref[:, mid:] = e1 / whole_sum
        for img in range(b):
            def mix(at, _, img=img):
                rows = pl.ds(pl.multiple_of(at + img * po, 32), 32)
                v = sa[rows, :] * at_ref[img : img + 1, :]
                r.blk[k].mix[rows, :] = (v[:, :mid] + v[:, mid:]).astype(BF16)
                return 0

            loop(po, 32, mix, 0)
        ex.blk[k].we.wait()
        for n0 in range(0, co, 256):
            r.blk[k].exp[:, n0 : n0 + 256] = dot(r.blk[k].mix[...], r.blk[k].we[:, n0 : n0 + 256])
        s1, s2 = moments(r.blk[k].exp, no, co, 16)
        put(sync + 2, 0, s1)
        put(sync + 2, co // LANES, s2)
        if k == 1:
            for n, v in enumerate(short_sums):
                put(sync + 2, (2 + n) * co // LANES, v)
        allreduce(sync + 2, (4 if k == 1 else 2) * co // LANES, fills[2])
        nexp = norm(sync + 2, 0, co // LANES, co, inv_out, v_co(vr.eg), v_co(vr.eb))
        return SimpleNamespace(nsplit=nsplit, natt=natt, xhat=xhat, pre=pre, excited=excited, nexp=nexp, centred=centred)

    short_sums = []

    def shortcut_forward():
        ex.wsh.wait()
        for n0 in range(0, co, 256):
            r.short[:, n0 : n0 + 256] = dot(r.pool[...], r.wsh[:, n0 : n0 + 256])
        short_sums.extend(moments(r.short, no, co, 16))

    def forward_first():
        for e in (first_w.sq, first_w.ext, first_w.we):
            e.forward()
        second_w.wrt.start()

    def between():
        ex.wsh.forward()
        second_w.wst.start()
        shortcut_forward()

    def forward_second():
        second_w.wrt.forward()
        for e in (second_w.sq, second_w.ext, second_w.we):
            e.start()

    f1 = attention_forward(1, vr1, 1, (forward_first, between, forward_second))
    nshort = norm(
        3, 2 * co // LANES, 3 * co // LANES, co, inv_out, v_co(vr1.hg), v_co(vr1.hb)
    )

    def summed1(rows):
        return (
            r.blk[1].exp[rows, :] * f1.nexp.gs
            + f1.nexp.sh
            + r.short[rows, :] * nshort.gs
            + nshort.sh
        )

    def hidden(at, _):
        rows = pl.ds(at, 16)
        r.h[rows, :] = (silu(summed1(rows)) * tiled(r.mo[rows, :], co)).astype(BF16)
        return 0

    loop(no, 16, hidden, 0)

    ex.blk[2].wrt.wait()
    r.red2[...] = dot(r.h[...], r.blk[2].wrt[...], NT)
    s1, s2 = moments(r.red2, no, mid, 64)
    put(4, 0, s1)
    put(4, 2, s2)

    def forward_rest():
        ex.cot.start()
        second_w.wst.forward()
        for e in (second_w.sq, second_w.ext, second_w.we):
            e.forward()

    allreduce(4, 4, forward_rest)
    nred2 = norm(4, 0, 2, mid, inv_out, v_mid(vr2.rg), v_mid(vr2.rb))
    im2 = r.blk[2].im

    def build2(i, _):
        at = pl.multiple_of(i * 4 * so, 4 * so)
        m = tiled(r.mo[pl.ds(at, 4 * so), :], mid)
        w = silu(r.red2[pl.ds(at, 4 * so), :] * nred2.gs + nred2.sh) * m
        for dj in range(3):
            wj = w
            if dj == 0:
                wj = jnp.where(not_first, pltpu.roll(w, 1, 0), 0.0)
            if dj == 2:
                wj = jnp.where(not_last, pltpu.roll(w, 4 * so - 1, 0), 0.0)
            for di in range(3):
                im_put(im2, at, wj, di, dj, 1 - di)
        return 0

    lax.fori_loop(0, no // (4 * so), build2, 0)
    im_zero(im2, 0, False)
    im_zero(im2, 2, True)
    f2 = attention_forward(2, vr2, 5, (None, None, None))

    ex.cot.wait()

    def finish(at, carry):
        su, sv = carry
        rows = pl.ds(at, 16)
        m = tiled(r.mo[rows, :], co)
        v = r.blk[2].exp[rows, :]
        s = v * f2.nexp.gs + f2.nexp.sh + r.h[rows, :].astype(F32)
        q = sigmoid(s)
        u = r.cot[rows, :].astype(F32) * m * (q * (1.0 + s * (1.0 - q)))
        r.cot[rows, :] = (s * q * m).astype(BF16)
        r.g[rows, :] = u
        return su + sum8(u), sv + sum8(u * v)

    su, sv = loop(no, 16, finish, (zero8(co), zero8(co)))
    out_ex = Exchange(
        lambda s: r.cot.at[:, pl.ds(pl.multiple_of(s * z.cos, LANES), z.cos)],
        lambda s: made.out.at[pl.ds(pl.multiple_of(s * no, no), no), :],
        os_sem.at[0],
        or_sem.at[0],
    )
    out_ex.start()
    put(8, 0, fold(su))
    put(8, co // LANES, fold(sv))
    allreduce(8, 2 * co // LANES)

    def pack_rows(k, name, skip, v):
        group, at = z.lay[(k, name)]
        at, share = at + skip * z.mids, z.mids
        for s in range(nc):
            for t in range(v.shape[1] // LANES):
                r.group[group].pk[s // 2, s % 2, at + t * share : at + (t + 1) * share, :] = v[
                    s * share : (s + 1) * share, t * LANES : (t + 1) * LANES
                ].astype(BF16)

    def pack_lanes(k, name, s, v):
        group, at = z.lay[(k, name)]
        rows = v.shape[0]
        for t in range(v.shape[1] // LANES):
            r.group[group].pk[s // 2, s % 2, at + t * rows : at + (t + 1) * rows, :] = v[
                :, t * LANES : (t + 1) * LANES
            ].astype(BF16)

    class Reduction:
        def __init__(self, group):
            own = r.group[group]
            self.pk, self.r1, self.r2, self.r3 = own.pk, own.r1, own.r2, own.r3
            self.rows = z.rows[group]
            self.piece = self.rows // z.near
            self.r4 = own.r4
            self.near, self.mine = lax.rem(d, z.near), lax.div(d, z.near)
            self.res = made.res[group]
            self.sems = [own.q1, own.q2, own.q3s, own.q3r, own.q4s, own.q4r, own.q5s, own.q5r]
            self.across = lax.div(c, 2)

        def piece_at(self, n):
            return pl.ds(pl.multiple_of(n * self.piece, 16), self.piece)

        def copy1(self):
            return pltpu.make_async_remote_copy(
                src_ref=self.pk.at[:, 1 - odd], dst_ref=self.r1, send_sem=self.sems[0].at[0],
                recv_sem=self.sems[0].at[1], device_id=partner, device_id_type=MESH,
            )

        def copy2(self):
            return pltpu.make_async_remote_copy(
                src_ref=self.pk.at[1 - self.across, odd], dst_ref=self.r2,
                send_sem=self.sems[1].at[0], recv_sem=self.sems[1].at[1],
                device_id=(d, chan_at(2)), device_id_type=MESH,
            )

        def at_near(self, n):
            return (self.mine * z.near + n, c)

        def copy3(self, to, src):
            return pltpu.make_async_remote_copy(
                src_ref=self.pk.at[self.across, odd, self.piece_at(to), :],
                dst_ref=self.r3.at[src], send_sem=self.sems[2].at[to],
                recv_sem=self.sems[3].at[src], device_id=self.at_near(to), device_id_type=MESH,
            )

        def copy4(self, to, src):
            return pltpu.make_async_remote_copy(
                src_ref=self.r3.at[self.near], dst_ref=self.res.at[self.piece_at(src), :],
                send_sem=self.sems[4].at[to], recv_sem=self.sems[5].at[src],
                device_id=self.at_near(to), device_id_type=MESH,
            )

        def copy5(self, to, src):
            return pltpu.make_async_remote_copy(
                src_ref=self.r4.at[self.mine], dst_ref=self.r4.at[src],
                send_sem=self.sems[6].at[to], recv_sem=self.sems[7].at[src],
                device_id=(to * z.near + self.near, c), device_id_type=MESH,
            )

        def local4(self):
            return pltpu.make_async_copy(
                self.r3.at[self.near], self.res.at[self.piece_at(self.near), :],
                self.sems[5].at[self.near],
            )

        def others(self, body, me, n):
            def step(j, _):
                body(lax.rem(me + j, n), lax.rem(me - j + n, n))
                return 0

            lax.fori_loop(1, n, step, 0)

        def total(self, slots, n, to):
            def body(at, _):
                rows = pl.ds(at, 16)
                t = slots[0, rows, :].astype(F32)
                for k in range(1, n):
                    t = t + slots[k, rows, :].astype(F32)
                to[rows, :] = t.astype(BF16)
                return 0

            loop(self.piece, 16, body, 0)

        def add(self, which, other):
            def body(at, _):
                rows = pl.ds(at, 128)
                self.pk[which, odd, rows, :] = (
                    self.pk[which, odd, rows, :].astype(F32) + other(rows).astype(F32)
                ).astype(BF16)
                return 0

            loop(self.rows, 128, body, 0)

        def step1(self):
            self.copy1().start()

        def step2(self):
            self.copy1().wait()
            away = 1 - self.across
            self.add(away, lambda rows: self.r1[away, rows, :])
            self.copy2().start()
            self.add(self.across, lambda rows: self.r1[self.across, rows, :])

        def step3(self):
            self.copy2().wait_recv()
            self.add(self.across, lambda rows: self.r2[rows, :])
            self.others(lambda to, _: self.copy3(to, self.near).start(), self.near, z.near)
            self.copy2().wait_send()

        def step4(self):
            self.r3[self.near] = self.pk[self.across, odd, self.piece_at(self.near), :]

            def arrive(to, src):
                self.copy3(to, self.near).wait_send()
                self.copy3(src, src).wait_recv()

            self.others(arrive, self.near, z.near)
            mine = self.r3.at[self.near]
            if z.far == 1:
                self.total(self.r3, z.near, mine)
            else:
                self.total(self.r3, z.near, self.r4.at[self.mine])
                self.others(lambda to, _: self.copy5(to, self.mine).start(), self.mine, z.far)

                def arrive_far(to, src):
                    self.copy5(to, self.mine).wait_send()
                    self.copy5(src, src).wait_recv()

                self.others(arrive_far, self.mine, z.far)
                self.total(self.r4, z.far, mine)
            self.local4().start()
            self.others(lambda to, _: self.copy4(to, self.near).start(), self.near, z.near)

        def finish(self):
            self.local4().wait()

            def arrive(to, src):
                self.copy4(to, self.near).wait_send()
                self.copy4(src, src).wait_recv()

            self.others(arrive, self.near, z.near)

    sums_of = {group: Reduction(group) for group in GROUPS}

    def attention_backward(k, f, sync):
        srow = STO_ROWS[k]
        nexp, nsplit, natt = f.nexp, f.nsplit, f.natt
        first = k == 1
        cw = co // LANES
        su, sux, ea, eb = norm_grad(sync, 0, cw, co, inv_out, nexp)
        keep(srow.eb, su)
        keep(srow.eg, sux)
        if first:
            _, suxh, ha, hb = norm_grad(sync, 0, 2 * cw, co, inv_out, nshort)
            keep(srow.hg, suxh)

        def expand_grad(at, _):
            rows = pl.ds(at, 16)
            m = tiled(r.mo[rows, :], co)
            u = r.g[rows, :]
            r.eg[rows, :] = (nexp.gs * u - m * (ea + eb * r.blk[k].exp[rows, :])).astype(BF16)
            if first:
                r.shg[rows, :] = (
                    nshort.gs * u - m * (ha + hb * r.short[rows, :])
                ).astype(BF16)
            return 0

        loop(no, 16, expand_grad, 0)
        r.mg[...] = dot(r.eg[...], r.blk[k].we[...], NT)
        sa = r.blk[k].sa
        for img in range(b):
            def att_grad(at, s, img=img):
                rows = pl.ds(pl.multiple_of(at + img * po, 32), 32)
                return s + sum8(sa[rows, :] * tiled_pair(r.mg[rows, :]))

            r.ags[img : img + 1, :] = fold(loop(po, 32, att_grad, zero8(2 * mid)))
        ags, at_ref = r.ags, r.blk[k].att
        a0, a1 = at_ref[:, :mid], at_ref[:, mid:]
        g0, g1 = ags[:, :mid], ags[:, mid:]
        mean = a0 * g0 + a1 * g1
        l0, l1 = a0 * (g0 - mean), a1 * (g1 - mean)
        ext = r.blk[k].ext
        excited_grad = dot_exact(l0, ext[0]) + dot_exact(l1, ext[1])
        au = excited_grad * silu_slope(f.pre)
        put(sync + 1, 0, fold(au))
        put(sync + 1, 1, fold(au * f.xhat))
        put(sync + 1, 2, fold(l0))
        put(sync + 1, 4, fold(l1))

        def matrices():
            r.mixt[...] = jnp.transpose(r.blk[k].mix[...])
            for s in range(nc):
                share = slice(s * z.cos, (s + 1) * z.cos)
                pack_lanes(k, EXPAND, s, dot(r.mixt[...], r.eg[:, share]))
            pack_rows(k, EXCITE, 0, dot_exact(l0, f.excited, TN))
            pack_rows(k, EXCITE, 1, dot_exact(l1, f.excited, TN))
            if first:
                r.sgt[...] = jnp.transpose(r.pool[...])
                for s in range(nc):
                    share = slice(s * z.cos, (s + 1) * z.cos)
                    pack_lanes(k, SHORTCUT, s, dot(r.sgt[...], r.shg[:, share]))
                sums_of[2].step1()
                sums_of[1].step3()
                r.pg[...] = dot(r.shg[...], r.wsh[...], NT).astype(BF16)

            else:
                sums_of[0].step1()

        allreduce(sync + 1, 6, matrices)
        inv_images = 1.0 / (b * nc * nd)
        su, sux = total(sync + 1, 0, att), total(sync + 1, 1, att)
        keep(srow.qb, su)
        keep(srow.qg, sux)
        keep(srow.xb, total(sync + 1, 2, 2 * mid))
        sb = natt.gs * (au - su * inv_images - f.xhat * (sux * inv_images)) * live8
        sums_of[2 if first else 0].step2()
        r.mgr[...] = dot_exact(sb, r.blk[k].sq[...], NT) * tiled(inv_area, mid)
        sp = r.blk[k].sp
        carry = (zero8(2 * mid), zero8(2 * mid))
        for img in range(b):
            def split_up(at, carry, img=img):
                s1, s2 = carry
                rows = pl.ds(pl.multiple_of(at + img * po, 32), 32)
                m = tiled(r.mo[rows, :], 2 * mid)
                v = sp[rows, :]
                grad = tiled_pair(r.mg[rows, :]) * at_ref[img : img + 1, :] + tiled_pair(
                    r.mgr[img : img + 1, :]
                )
                u = grad * m * silu_slope(v * nsplit.gs + nsplit.sh)
                r.su[rows, :] = u
                return s1 + sum8(u), s2 + sum8(u * v)

            carry = loop(po, 32, split_up, carry)
        put(sync + 2, 0, fold(carry[0]))
        put(sync + 2, 4, fold(carry[1]))

        def squeeze_matrix():
            if first:
                sums_of[1].step4()
            pack_rows(k, SQUEEZE, 0, dot_exact(f.centred, sb, TN))

        allreduce(sync + 2, 8, squeeze_matrix)
        su, sux, ca, cb = norm_grad(sync + 2, 0, 4, 2 * mid, inv_out, nsplit)
        keep(srow.sb, su)
        keep(srow.sg, sux)

        def split_grad(at, _):
            rows = pl.ds(at, 32)
            m = tiled(r.mo[rows, :], 2 * mid)
            r.sgb[rows, :] = (
                nsplit.gs * r.su[rows, :] - m * (ca + cb * sp[rows, :])
            ).astype(BF16)
            return 0

        loop(no, 32, split_grad, 0)

    def tiled_pair(v):
        return jnp.concatenate([v, v], axis=1)

    def split_matrix(k):
        r.sgt[...] = jnp.transpose(r.sgb[...])
        for g in range(2):
            for t in range(3):
                v = dot(
                    r.sgt[g * mid : (g + 1) * mid, :],
                    r.blk[k].im[g, so : so + no, 3 * t * grp : 3 * (t + 1) * grp],
                )
                for u in range(3):
                    pack_rows(
                        k, SPLIT, (3 * t + u) * 2 + g, v[:, u * grp : (u + 1) * grp]
                    )

    dcol = r.dcol
    dcol[:so, :] = jnp.zeros((so, kk), F32)
    dcol[so + po :, :] = jnp.zeros((so, kk), F32)

    def columns(k, img, g):
        dcol[so : so + po, :] = dot(
            r.sgb[img * po : (img + 1) * po, g * mid : (g + 1) * mid], split_weights(k, g)
        )

    tile = 4 * so
    first_g, last_g = not_first[:, :grp], not_last[:, :grp]

    def tap(at, di, dj, shift):
        t = di * 3 + dj
        return dcol[pl.ds(pl.multiple_of(at + so - shift * so, so), tile), t * grp : (t + 1) * grp]

    def from_left(v):
        return jnp.where(first_g, pltpu.roll(v, 1, 0), 0.0)

    def from_right(v):
        return jnp.where(last_g, pltpu.roll(v, tile - 1, 0), 0.0)

    attention_backward(2, f2, 8)
    sums = []
    for g in range(2):
        carry = (zero8(grp), zero8(grp))
        lanes = slice(g * grp, (g + 1) * grp)
        for img in range(b):
            columns(2, img, g)

            def back2(at, carry, img=img, g=g, lanes=lanes):
                s1, s2 = carry
                cols = [
                    tap(at, 0, dj, -1) + tap(at, 1, dj, 0) + tap(at, 2, dj, 1) for dj in range(3)
                ]
                grad = cols[1] + from_right(cols[0]) + from_left(cols[2])
                rows = pl.ds(pl.multiple_of(at + img * po, tile), tile)
                v = r.red2[rows, lanes]
                u = (
                    grad
                    * tiled(r.mo[rows, :], grp)
                    * silu_slope(v * nred2.gs[:, lanes] + nred2.sh[:, lanes])
                )
                r.u2[rows, lanes] = u
                return s1 + sum8(u), s2 + sum8(u * v)

            carry = loop(po, tile, back2, carry)
        sums.append(carry)
    put(11, 0, jnp.concatenate([fold(s[0]) for s in sums], axis=1))
    put(11, 2, jnp.concatenate([fold(s[1]) for s in sums], axis=1))
    def split_matrix2():
        split_matrix(2)
        sums_of[1].step1()
        sums_of[0].step3()

    allreduce(11, 4, split_matrix2)
    sums_of[1].step2()
    su, sux, ca, cb = norm_grad(11, 0, 2, mid, inv_out, nred2)
    keep(STO_ROWS[2].rb, su)
    keep(STO_ROWS[2].rg, sux)

    def reduce_grad2(at, _):
        rows = pl.ds(at, 64)
        m = tiled(r.mo[rows, :], mid)
        r.rg1[rows, :] = (
            nred2.gs * r.u2[rows, :] - m * (ca + cb * r.red2[rows, :])
        ).astype(BF16)
        return 0

    loop(no, 64, reduce_grad2, 0)
    for n0 in range(0, co, 256):
        cols = slice(n0, n0 + 256)
        r.g[:, cols] = r.g[:, cols] + dot(r.rg1[:no, :], r.blk[2].wrt[:, cols])

    def first_up(at, carry):
        s1, s2, s3 = carry
        rows = pl.ds(at, 16)
        u = r.g[rows, :] * tiled(r.mo[rows, :], co) * silu_slope(summed1(rows))
        r.g[rows, :] = u
        return (
            s1 + sum8(u),
            s2 + sum8(u * r.blk[1].exp[rows, :]),
            s3 + sum8(u * r.short[rows, :]),
        )

    s1, s2, s3 = loop(no, 16, first_up, (zero8(co), zero8(co), zero8(co)))
    put(12, 0, fold(s1))
    put(12, co // LANES, fold(s2))
    put(12, 2 * co // LANES, fold(s3))

    def reduce_matrix2():
        r.rgt[:, :no] = jnp.transpose(r.rg1[:no, :])
        for n0 in range(0, co, 256):
            pack_rows(2, REDUCE, n0 // LANES, dot(r.rgt[:, :no], r.h[:, n0 : n0 + 256]))
        sums_of[0].step4()

    allreduce(12, 3 * co // LANES, reduce_matrix2)

    attention_backward(1, f1, 12)
    sums = []
    for g in range(2):
        carry = (zero8(grp), zero8(grp))
        lanes = slice(g * grp, (g + 1) * grp)
        for img in range(b):
            columns(1, img, g)

            def back1(at, carry, img=img, g=g, lanes=lanes):
                s1, s2 = carry
                rows = pl.ds(pl.multiple_of(at + img * po, tile), tile)
                m = tiled(r.mo[rows, :], grp)
                lead = pl.ds(pl.multiple_of(lax.div(at, so) + img * so, 4), 4)
                for p in range(2):
                    for q in range(2):
                        def col(dj):
                            if p == 0:
                                return tap(at, 1, dj, 0)
                            return tap(at, 0, dj, -1) + tap(at, 2, dj, 0)

                        grad = col(1) if q == 0 else col(2) + from_right(col(0))
                        v = phase_of(g, lead, p, q)
                        u = grad * m * silu_slope(v * nred1.gs[:, lanes] + nred1.sh[:, lanes])
                        r.u1[g, lead, p, pl.ds(q, so, stride=2), :] = u.reshape(4, so, grp)
                        s1, s2 = s1 + sum8(u), s2 + sum8(u * v)
                return s1, s2

            carry = loop(po, tile, back1, carry)
        sums.append(carry)
    put(15, 0, jnp.concatenate([fold(s[0]) for s in sums], axis=1))
    put(15, 2, jnp.concatenate([fold(s[1]) for s in sums], axis=1))

    def split_matrix1():
        split_matrix(1)
        sums_of[3].step1()

    allreduce(15, 4, split_matrix1)
    su, sux, ca, cb = norm_grad(15, 0, 2, mid, inv_in, nred1)
    keep(STO_ROWS[1].rb, su)
    keep(STO_ROWS[1].rg, sux)

    def reduce_grad1(i, _):
        rows = pl.ds(pl.multiple_of(i * 2 * si, 2 * si), 2 * si)
        m = tiled(r.mi[rows, :].astype(F32), mid)
        u, v = row_pair(r.u1, i), row_pair(red1, i)
        r.rg1[rows, :] = (nred1.gs * u - m * (ca + cb * v)).astype(BF16)
        return 0

    spread = pool_matrix(1)
    grads = (r.h, r.eg)
    last = []
    for q in range(nq):
        rows = slice(q * part, (q + 1) * part)
        lead = part // (2 * si)
        lax.fori_loop(q * lead, (q + 1) * lead, reduce_grad1, 0)
        m = tiled(r.mi[rows, :].astype(F32), 256)
        for n0 in range(0, ci, 256):
            cols = slice(n0, n0 + 256)
            v = dot(r.rg1[rows, :], r.blk[1].wrt[:, cols]) + dot(
                spread, r.pg[q * pool_rows : (q + 1) * pool_rows, cols]
            )
            at = (q % 2) * ci + n0
            grads[q // 2][:, at : at + 256] = (v * m).astype(BF16)
        e = Exchange(
            lambda s, q=q: grads[q // 2].at[
                :, pl.ds(pl.multiple_of((q % 2) * ci + s * z.cis, LANES), z.cis)
            ],
            lambda s, q=q: made.gx.at[
                pl.ds(pl.multiple_of(s * ni + q * part, part), part), :
            ],
            os_sem.at[1 + q],
            or_sem.at[1 + q],
        )
        e.start()
        last.append(e)
        if q == 0:
            sums_of[3].step2()
            sums_of[2].step3()
    r.rgt[...] = jnp.transpose(r.rg1[...])
    for n0 in range(0, ci, 256):
        pack_rows(1, REDUCE, n0 // LANES, dot(r.rgt[...], r.x[:, n0 : n0 + 256]))
    sums_of[4].step1()
    sums_of[2].step4()
    sums_of[4].step2()
    sums_of[3].step3()
    sums_of[4].step3()
    sums_of[3].step4()
    sums_of[4].step4()
    out_ex.wait()
    for e in last:
        e.wait()
    for sums in sums_of.values():
        sums.finish()


class Weights:
    def __init__(self, values):
        (
            self.reduce, self.reducegain, self.reducebias,
            self.split, self.splitgain, self.splitbias,
            self.squeeze, self.squeezegain, self.squeezebias,
            self.excite, self.excitebias,
            self.expand, self.expandgain, self.expandbias,
        ) = values[:14]
        self.extra = values[14:]


def doubled(v):
    return jnp.concatenate([v, v], axis=-1).reshape(-1, LANES)


def per_device(mesh, images, cotangent, groups, *weights):
    first, second = Weights(weights[:17]), Weights(weights[17:])
    z = Sizes(mesh, images, first.reduce, first.expand, first.squeeze)

    def vectors(w):
        parts = (w.reducegain, w.reducebias, w.splitgain, w.splitbias, w.excitebias)
        parts += (w.expandgain, w.expandbias) + w.extra[1:] + (w.squeezegain, w.squeezebias)
        return [v if v.ndim == 2 else v.reshape(1, -1) for v in parts]

    def block(w):
        return dict(
            wrt=w.reduce.T,
            wst=jnp.transpose(w.split, (0, 1, 3, 4, 2)).reshape(TAPS, 2, z.mids, z.grp),
            sq=w.squeeze,
            ext=jnp.transpose(w.excite, (1, 2, 0)),
            we=w.expand,
        )

    inputs = dict(
        images=images.reshape(-1, z.cis),
        cot=cotangent.reshape(-1, z.cos),
        groups=groups,
        vec=vectors(first) + vectors(second),
        wsh=first.extra[0],
        blk={1: block(first), 2: block(second)},
    )
    in_specs = jax.tree.map(lambda v: pl.BlockSpec(memory_space=pl.ANY), inputs)
    in_specs.update(groups=pl.BlockSpec(memory_space=pltpu.SMEM))
    outs = dict(
        out=jax.ShapeDtypeStruct((z.nc * z.no, z.cos), BF16),
        gx=jax.ShapeDtypeStruct((z.nc * z.ni, z.cis), BF16),
        sto=jax.ShapeDtypeStruct((NSTO, LANES), F32),
        res={n: jax.ShapeDtypeStruct((rows, LANES), BF16) for n, rows in z.rows.items()},
    )
    out_specs = jax.tree.map(lambda v: pl.BlockSpec(memory_space=pl.ANY), outs)
    out_specs.update(sto=pl.BlockSpec(memory_space=pltpu.VMEM))
    scratch = scratch_tree(z, vectors(first) + vectors(second))
    tree = jax.tree.structure((inputs, outs, scratch))
    results = pl.pallas_call(
        functools.partial(mega_kernel, z, tree),
        out_shape=jax.tree.leaves(outs),
        in_specs=jax.tree.leaves(in_specs),
        out_specs=jax.tree.leaves(out_specs),
        scratch_shapes=jax.tree.leaves(scratch),
        compiler_params=pltpu.CompilerParams(
            collective_id=0, has_side_effects=True, vmem_limit_bytes=63 << 20
        ),
        name="two_blocks",
    )(*jax.tree.leaves(inputs))
    return unpack(z, jax.tree.unflatten(jax.tree.structure(outs), results))


def unpack_kernel(z, plan, tree, *refs):
    given, (out_image, gx, *outs) = jax.tree.unflatten(tree, refs)
    given = space(given)
    out_in, gx_in, sto, res = given.out, given.gx, given.sto, given.res
    c = lax.axis_index(CHAN)
    out_image[...] = out_in[...].astype(F32)
    gx[...] = gx_in[...].astype(F32)

    def mid_share(row):
        v = sto[pl.ds(row + lax.div(c, 2), 1), :]
        return jnp.where(lax.rem(c, 2) == 0, v[:, : z.mids], v[:, z.mids :])

    @pl.when(pl.program_id(0) == 0)
    def _():
        for (kind, k, name), o in zip(plan, outs):
            if kind == MATRIX:
                group, at = z.lay[(k, name)]
                rows = o.shape[0]
                for t in range(o.shape[1] // LANES):
                    o[:, t * LANES : (t + 1) * LANES] = res[group][
                        at + t * rows : at + (t + 1) * rows, :
                    ].astype(F32)
                continue
            row = name
            if kind == MID_VECTOR:
                o[...] = mid_share(row)
            elif kind == PAIR_VECTOR:
                o[0:1, :] = mid_share(row)
                o[1:2, :] = mid_share(row + z.mid // LANES)
            elif kind == ATT_VECTOR:
                o[...] = sto[row : row + 1, :]
            else:
                n = z.cos // LANES
                for t in range(n):
                    o[:, t * LANES : (t + 1) * LANES] = sto[pl.ds(row + c * n + t, 1), :]


def unpack(z, results):
    plan = []
    for k in (1, 2):
        v = STO_ROWS[k]
        plan += [
            (MATRIX, k, REDUCE), (MID_VECTOR, k, v.rg), (MID_VECTOR, k, v.rb),
            (MATRIX, k, SPLIT), (PAIR_VECTOR, k, v.sg), (PAIR_VECTOR, k, v.sb),
            (MATRIX, k, SQUEEZE), (ATT_VECTOR, k, v.qg), (ATT_VECTOR, k, v.qb),
            (MATRIX, k, EXCITE), (PAIR_VECTOR, k, v.xb),
            (MATRIX, k, EXPAND), (OUT_VECTOR, k, v.eg), (OUT_VECTOR, k, v.eb),
        ]
        if k == 1:
            plan += [(MATRIX, k, SHORTCUT), (OUT_VECTOR, k, v.hg), (OUT_VECTOR, k, v.eb)]

    def shape_of(kind, k, name):
        if kind == MATRIX:
            return (
                (z.mids, z.ci if k == 1 else z.co),
                (2 * TAPS * z.mids, LANES),
                (z.mids, z.att),
                (2 * z.mids, z.att),
                (z.mid, z.cos),
                (z.ci, z.cos),
            )[name]
        return (None, (1, z.mids), (2, z.mids), (1, z.att), (1, z.cos))[kind]

    shapes = [shape_of(*entry) for entry in plan]
    steps = 8
    whole = lambda shape: pl.BlockSpec(shape, lambda i: (0, 0))
    slab = lambda v: pl.BlockSpec((v.shape[0] // steps, v.shape[1]), lambda i: (i, 0))
    in_specs = {n: slab(v) if n in ("out", "gx") else jax.tree.map(lambda a: whole(a.shape), v)
                for n, v in results.items()}
    images = [results["out"], results["gx"]]
    outs = [jax.ShapeDtypeStruct(v.shape, F32) for v in images]
    outs += [jax.ShapeDtypeStruct(s, F32) for s in shapes]
    flat = pl.pallas_call(
        functools.partial(unpack_kernel, z, plan, jax.tree.structure((results, outs))),
        grid=(steps,),
        out_shape=outs,
        in_specs=jax.tree.leaves(in_specs),
        out_specs=[slab(v) for v in images] + [whole(s) for s in shapes],
        compiler_params=pltpu.CompilerParams(vmem_limit_bytes=62 << 20),
        name="unpack",
    )(*jax.tree.leaves(results))
    final = [
        flat[0].reshape(z.nc * z.b, z.so, z.so, z.cos),
        flat[1].reshape(z.nc * z.b, z.si, z.si, z.cis),
    ]
    for (kind, _, name), v in zip(plan, flat[2:]):
        if (kind, name) == (MATRIX, REDUCE):
            v = v.T
        elif (kind, name) == (MATRIX, SPLIT):
            v = jnp.transpose(v.reshape(3, 3, 2, z.mids, z.grp), (0, 1, 4, 2, 3))
        elif (kind, name) == (MATRIX, EXCITE):
            v = jnp.transpose(v.reshape(2, z.mids, z.att), (2, 0, 1))
        elif kind in (MID_VECTOR, ATT_VECTOR, OUT_VECTOR):
            v = v.reshape(-1)
        final.append(v)
    return tuple(final)


def specs():
    block = [
        P(None, CHAN), P(CHAN), P(CHAN),
        P(None, None, None, None, CHAN), P(None, CHAN), P(None, CHAN),
        P(CHAN, None), P(), P(), P(None, None, CHAN), P(None, CHAN),
        P(None, CHAN), P(CHAN), P(CHAN),
    ]
    short = [P(None, CHAN), P(CHAN), P(CHAN)]
    return block + short + block


def solution(mesh):
    image = P(DP, None, None, CHAN)
    return jax.shard_map(
        functools.partial(per_device, mesh),
        mesh=mesh,
        in_specs=tuple([image, image, P(DP)] + specs()),
        out_specs=tuple([image, image] + specs()),
        check_vma=False,
    )
```

```python
import functools
from types import SimpleNamespace

import jax
import jax.numpy as jnp
from jax import lax
from jax.experimental import pallas as pl
from jax.experimental.pallas import tpu as pltpu
from jax.sharding import PartitionSpec as P

EPSILON = 1e-05
F32, BF16 = jnp.float32, jnp.bfloat16
HIGHEST = lax.Precision.HIGHEST
MESH = pl.DeviceIdType.MESH
LANES = 128
TAPS = 9
DP, CHAN = "dp", "chan"
REDUCE, SPLIT, SQUEEZE, EXCITE, EXPAND, SHORTCUT = range(6)
MATRIX, MID_VECTOR, PAIR_VECTOR, ATT_VECTOR, OUT_VECTOR = range(5)
SYNC_ROWS = (8, 8, 8, 32, 8, 8, 8, 16, 16, 8, 8, 8, 24, 8, 8, 8)

NT = (((1,), (1,)), ((), ()))
NN = (((1,), (0,)), ((), ()))
TN = (((0,), (0,)), ((), ()))


def dot(a, b, dims=NN):
    return lax.dot_general(a, b, dims, preferred_element_type=F32)


def dot_exact(a, b, dims=NN):
    return lax.dot_general(
        a.astype(F32), b.astype(F32), dims, precision=HIGHEST, preferred_element_type=F32
    )


def sigmoid(v):
    return 0.5 * jnp.tanh(0.5 * v) + 0.5


def silu(v):
    return v * sigmoid(v)


def silu_slope(v):
    q = sigmoid(v)
    return q * (1.0 + v * (1.0 - q))


def tiled(v, width):
    return jnp.concatenate([v] * (width // LANES), axis=1) if width > LANES else v


def sum8(v):
    return jnp.sum(v.reshape(v.shape[0] // 8, 8, v.shape[1]), axis=0)


def fold(v):
    return jnp.sum(v, axis=0, keepdims=True)


def span(start, size):
    if isinstance(start, int):
        return pl.ds(start, size)
    return pl.ds(pl.multiple_of(start, size), size)


class Sizes:
    def __init__(self, mesh, images, reduce_w, expand_w, squeeze_w):
        self.nd, self.nc = mesh.shape[DP], mesh.shape[CHAN]
        self.near = min(self.nd, 8)
        self.far = self.nd // self.near
        self.b = images.shape[0] // self.nc
        self.si = images.shape[1]
        self.so = self.si // 2
        self.cis = images.shape[3]
        self.ci = self.cis * self.nc
        self.mids = reduce_w.shape[1]
        self.mid = self.mids * self.nc
        self.cos = expand_w.shape[1]
        self.co = self.cos * self.nc
        self.att = squeeze_w.shape[1]
        self.po = self.so * self.so
        self.pi = self.si * self.si
        self.no = self.b * self.po
        self.ni = self.b * self.pi
        self.grp = self.mid // 2
        self.kk = TAPS * self.grp
        cin = {1: self.ci, 2: self.co}
        self.piece_rows = {
            (k, name): rows
            for k in (1, 2)
            for name, rows in (
                (REDUCE, cin[k] // LANES * self.mids),
                (SPLIT, 2 * TAPS * self.mids),
                (SQUEEZE, self.mids),
                (EXCITE, 2 * self.mids),
                (EXPAND, self.cos // LANES * self.mid),
                (SHORTCUT, self.cos // LANES * self.ci),
            )
        }
        self.lay, self.rows = {}, {}
        for group, members in GROUPS.items():
            at = 0
            for key in members:
                self.lay[key] = (group, at)
                at += self.piece_rows[key]
            self.rows[group] = -(-at // (16 * self.near)) * 16 * self.near


GROUPS = {
    0: ((2, EXPAND), (2, EXCITE)),
    1: ((2, SPLIT), (2, SQUEEZE)),
    2: ((1, EXPAND), (1, EXCITE), (1, SHORTCUT)),
    3: ((1, SPLIT), (1, SQUEEZE)),
    4: ((1, REDUCE),),
    5: ((2, REDUCE),),
}
VEC_ROWS = {
    1: SimpleNamespace(rg=0, rb=1, sg=2, sb=4, xb=6, eg=8, eb=10, hg=12, hb=14, qg=16, qb=17),
    2: SimpleNamespace(rg=18, rb=19, sg=20, sb=22, xb=24, eg=26, eb=28, qg=30, qb=31),
}
NVEC = 32
STO_ROWS = {
    2: SimpleNamespace(eb=0, eg=8, qb=16, qg=17, sb=18, sg=22, rb=26, rg=28, xb=30),
    1: SimpleNamespace(eb=34, eg=42, qb=50, qg=51, sb=52, sg=56, rb=60, rg=62, xb=64, hg=68),
}
NSTO = 80
QUARTERS = 4
OUT_PARTS = 4


def space(tree):
    if not isinstance(tree, dict):
        return tree
    inner = {k: space(v) for k, v in tree.items()}
    return SimpleNamespace(**inner) if all(isinstance(k, str) for k in inner) else inner


def scratch_tree(z, vec):
    def f32(*shape):
        return pltpu.VMEM(shape, F32)

    def bf16(*shape):
        return pltpu.VMEM(shape, BF16)

    def sem(*shape):
        return pltpu.SemaphoreType.DMA(shape)

    ns = z.nd * z.nc // 2
    return dict(
        x=bf16(z.ni, z.ci),
        cot=bf16(z.no, z.co),
        wsh=bf16(z.ci, z.co),
        vv=f32(z.nc, NVEC, LANES),
        vmine=f32(NVEC, LANES),
        vraw=[f32(*v.shape) for v in vec],
        vsem=sem(len(vec)),
        mo=f32(z.no, LANES),
        mi=bf16(z.ni, LANES),
        red1=f32(z.mid // LANES, z.b * z.so, 2, z.si, LANES),
        u1=f32(z.mid // LANES, z.b * z.so, 2, z.si, LANES),
        pool=bf16(z.no, z.ci),
        short=f32(z.no, z.co),
        h=bf16(z.no, z.co),
        red2=f32(z.no, z.mid),
        u2=f32(z.no, z.mid),
        g=f32(z.no, z.co),
        eg=bf16(z.no, z.co),
        shg=bf16(z.no, z.co),
        mg=f32(z.no, z.mid),
        su=f32(z.no, 2 * z.mid),
        sgb=bf16(z.no, 2 * z.mid),
        sgt=bf16(2 * z.mid, z.no),
        mixt=bf16(z.mid, z.no),
        dcol=f32(z.po + 2 * z.so, z.kk),
        rg1=bf16(z.ni, z.mid),
        rgt=bf16(z.mid, z.ni),
        pg=bf16(z.no, z.ci),
        ags=f32(8, 2 * z.mid),
        mgr=f32(8, z.mid),
        blk={
            k: dict(
                wrt=bf16(z.mid, z.ci if k == 1 else z.co),
                wst=bf16(TAPS, 2, z.mid, z.grp),
                sq=bf16(z.mid, z.att),
                ext=bf16(2, z.mid, z.att),
                we=bf16(z.mid, z.co),
                im=bf16(2, z.no + 2 * z.so, z.kk),
                sp=f32(z.no, 2 * z.mid),
                sa=f32(z.no, 2 * z.mid),
                mix=bf16(z.no, z.mid),
                exp=f32(z.no, z.co),
                att=f32(8, 2 * z.mid),
                pm=f32(8, z.mid),
            )
            for k in (1, 2)
        },
        group={
            n: dict(
                pk=bf16(z.nc // 2, 2, rows, LANES),
                r1=bf16(z.nc // 2, rows, LANES),
                r2=bf16(rows, LANES),
                r3=bf16(z.near, rows // z.near, LANES),
                r4=bf16(z.far, rows // z.near, LANES),
                q1=sem(2),
                q2=sem(2),
                q3s=sem(z.near),
                q3r=sem(z.near),
                q4s=sem(z.near),
                q4r=sem(z.near),
                q5s=sem(z.far),
                q5r=sem(z.far),
                ry=bf16(rows // 2 if n == 2 else 16, LANES),
                q6=sem(4),
            )
            for n, rows in z.rows.items()
        },
        sync={
            k: dict(sa=f32(rows, LANES), sb=f32(rows, LANES), st=f32(rows, LANES))
            for k, rows in enumerate(SYNC_ROWS)
        },
        slots={p: f32(ns, max(SYNC_ROWS), LANES) for p in range(2)},
        gather_send=sem(13, z.nc),
        gather_recv=sem(13, z.nc),
        image_send=sem(QUARTERS, z.nc),
        image_recv=sem(QUARTERS, z.nc),
        out_send=sem(OUT_PARTS + QUARTERS, z.nc),
        out_got=sem(OUT_PARTS + QUARTERS, z.nc),
        s0s=sem(1),
        s0r=sem(2),
        s1s=sem(1),
        s1r=sem(2),
    )


def mega_kernel(z, tree, *refs):
    given, made, r = (space(t) for t in jax.tree.unflatten(tree, refs))
    nc, nd = z.nc, z.nd
    b, so, si, po, pi_, no, ni = z.b, z.so, z.si, z.po, z.pi, z.no, z.ni
    mid, co, ci, att, grp, kk = z.mid, z.co, z.ci, z.att, z.grp, z.kk
    d, c = lax.axis_index(DP), lax.axis_index(CHAN)
    ns = nd * nc // 2
    me = d * (nc // 2) + lax.div(c, 2)
    odd = lax.rem(c, 2)

    def chan_at(i):
        return lax.rem(c + i, nc)

    def place(s):
        return (lax.div(s, nc // 2), lax.rem(s, nc // 2) * 2 + odd)

    partner = (d, c + 1 - 2 * odd)
    far_first = []
    if ns <= 16:
        for n in range(ns - 1):
            far_first.append(place(lax.rem(me + (n + ns // 3) % (ns - 1) + 1, ns)))

    barrier = pltpu.get_barrier_semaphore()
    for i in range(1, nc):
        pl.semaphore_signal(barrier, inc=1, device_id=(d, chan_at(i)), device_id_type=MESH)

    def greet(j, _):
        pl.semaphore_signal(
            barrier, inc=1, device_id=place(lax.rem(me + j, ns)), device_id_type=MESH
        )
        return 0

    lax.fori_loop(1, ns, greet, 0)
    pl.semaphore_wait(barrier, nc - 1 + ns - 1)

    class Exchange:
        def __init__(self, src, dst, send, recv):
            self.src, self.dst, self.send, self.recv = src, dst, send, recv

        def copy(self, i):
            to = chan_at(i)
            return pltpu.make_async_remote_copy(
                src_ref=self.src(to), dst_ref=self.dst(c), send_sem=self.send.at[i],
                recv_sem=self.recv.at[i], device_id=(d, to), device_id_type=MESH,
            )

        def local(self):
            return pltpu.make_async_copy(self.src(c), self.dst(c), self.recv.at[0])

        def start(self):
            for i in (2, 1, 3) if nc == 4 else range(1, nc):
                self.copy(i).start()
            self.local().start()

        def wait(self):
            self.local().wait()
            for i in range(1, nc):
                frm = lax.rem(c - i + nc, nc)
                pltpu.make_async_remote_copy(
                    src_ref=self.src(c), dst_ref=self.dst(frm), send_sem=self.send.at[i],
                    recv_sem=self.recv.at[i], device_id=(d, frm), device_id_type=MESH,
                ).wait_recv()
                self.copy(i).wait_send()

    class Relay:
        def __init__(self, src, dst, send, recv):
            self.src, self.dst, self.send, self.recv = src, dst, send, recv
            self.far = chan_at(2)

        def copy(self, n, src, which, to):
            return pltpu.make_async_remote_copy(
                src_ref=src, dst_ref=self.dst(which), send_sem=self.send.at[n],
                recv_sem=self.recv.at[n], device_id=to, device_id_type=MESH,
            )

        def across(self, which):
            return self.copy(1, self.src(c), which, (d, self.far))

        def beside(self, which):
            return self.copy(2, self.src(c), which, partner)

        def onward(self, which):
            return self.copy(3, self.dst(self.far), which, partner)

        def local(self):
            return pltpu.make_async_copy(self.src(c), self.dst(c), self.recv.at[0])

        def start(self):
            self.across(c).start()
            self.beside(c).start()
            self.local().start()

        def forward(self):
            self.across(self.far).wait_recv()
            self.onward(self.far).start()

        def wait(self):
            self.local().wait()
            self.across(c).wait_send()
            self.beside(c).wait_send()
            self.onward(self.far).wait_send()
            self.beside(partner[1]).wait_recv()
            self.onward(lax.rem(partner[1] + 2, nc)).wait_recv()

    gs_sem, gr_sem = r.gather_send, r.gather_recv
    xs_sem, xr_sem = r.image_send, r.image_recv
    os_sem, or_sem = r.out_send, r.out_got

    def lanes_of(ref, width):
        return lambda s: ref.at[:, pl.ds(pl.multiple_of(s * width, LANES), width)]

    def rows_of(ref, size):
        return lambda s: ref.at[pl.ds(pl.multiple_of(s * size, size), size), :]

    def mids_of(ref, size):
        return lambda s: ref.at[:, pl.ds(pl.multiple_of(s * size, size), size), :]

    def taps_of(ref, size):
        return lambda s: ref.at[:, :, pl.ds(pl.multiple_of(s * size, size), size), :]

    whole = lambda ref: (lambda s: ref)
    ms = z.mids
    sem_rows = iter(range(13))

    def gathered(src, dst, kind=Relay):
        e = next(sem_rows)
        return kind(src, dst, gs_sem.at[e], gr_sem.at[e])

    ex = SimpleNamespace(
        vec=gathered(whole(r.vmine), lambda s: r.vv.at[s], Exchange),
        wsh=gathered(whole(given.wsh), lanes_of(r.wsh, z.cos)),
        cot=gathered(rows_of(given.cot, no), lanes_of(r.cot, z.cos), Exchange),
        blk={
            k: SimpleNamespace(
                wrt=gathered(whole(given.blk[k].wrt), rows_of(r.blk[k].wrt, ms)),
                wst=gathered(whole(given.blk[k].wst), taps_of(r.blk[k].wst, ms)),
                sq=gathered(whole(given.blk[k].sq), rows_of(r.blk[k].sq, ms)),
                ext=gathered(whole(given.blk[k].ext), mids_of(r.blk[k].ext, ms)),
                we=gathered(whole(given.blk[k].we), lanes_of(r.blk[k].we, z.cos)),
            )
            for k in (1, 2)
        },
        x=[],
    )
    nq = QUARTERS
    part = ni // nq
    for q in range(nq):
        ex.x.append(Exchange(
            lambda s, q=q: given.images.at[pl.ds(pl.multiple_of(s * ni + q * part, part), part), :],
            lambda s, q=q: r.x.at[
                pl.ds(q * part, part), pl.ds(pl.multiple_of(s * z.cis, LANES), z.cis)
            ],
            xs_sem.at[q],
            xr_sem.at[q],
        ))
    first_w, second_w = ex.blk[1], ex.blk[2]
    first_w.wrt.start()
    raw = [
        pltpu.make_async_copy(v, to, r.vsem.at[n]) for n, (v, to) in enumerate(zip(given.vec, r.vraw))
    ]
    for copy in raw:
        copy.start()
    ex.x[0].start()
    for q in range(1, nq):
        ex.x[q].start()
    row = 0
    for copy, v in zip(raw, r.vraw):
        copy.wait()
        rows, width = v.shape
        for k in range(rows):
            one = v[k : k + 1, :]
            if width < LANES:
                one = jnp.concatenate([one, one], axis=1)
            for t in range(one.shape[1] // LANES):
                r.vmine[row : row + 1, :] = one[:, t * LANES : (t + 1) * LANES]
                row += 1
    ex.vec.start()

    ss0, rs0, ss1, rs1 = r.s0s, r.s0r, r.s1s, r.s1r

    def put(k, row, v):
        for t in range(v.shape[1] // LANES):
            r.sync[k].sa[row + t : row + t + 1, :] = v[:, t * LANES : (t + 1) * LANES]

    def allreduce(k, used, meanwhile=None):
        sa, sb, st = r.sync[k].sa, r.sync[k].sb, r.sync[k].st
        rows = SYNC_ROWS[k]
        sc = r.slots[k % 2].at[:, :rows, :]
        if used < rows:
            sa[used:rows, :] = jnp.zeros((rows - used, LANES), F32)
        first = pltpu.make_async_remote_copy(
            src_ref=sa, dst_ref=sb, send_sem=ss0.at[0], recv_sem=rs0.at[k % 2],
            device_id=partner, device_id_type=MESH,
        )
        first.start()
        first.wait()
        pair = sa[...] + sb[...]
        sc[me] = pair

        def send(to):
            pltpu.make_async_remote_copy(
                src_ref=sc.at[me], dst_ref=sc.at[me], send_sem=ss1.at[0],
                recv_sem=rs1.at[k % 2], device_id=to, device_id_type=MESH,
            ).start()

        if ns <= 16:
            for to in far_first:
                send(to)
        else:

            def send_one(j, _):
                send(place(lax.rem(me + j, ns)))
                return 0

            lax.fori_loop(1, ns, send_one, 0)
        if meanwhile is not None:
            meanwhile()
        others = sc.at[pl.ds(0, ns - 1)]
        pltpu.make_async_remote_copy(
            src_ref=others, dst_ref=others, send_sem=ss1.at[0], recv_sem=rs1.at[k % 2],
            device_id=partner, device_id_type=MESH,
        ).wait()
        if ns <= 16:
            total = sc[0]
            for s in range(1, ns):
                total = total + sc[s]
        else:
            total = lax.fori_loop(1, ns, lambda s, t: t + sc[s], sc[0])
        st[...] = total

    def total(k, row, width):
        st = r.sync[k].st
        return jnp.concatenate(
            [st[row + t : row + t + 1, :] for t in range(width // LANES)], axis=1
        )

    sto = made.sto

    def keep(row, v):
        for t in range(v.shape[1] // LANES):
            sto[row + t : row + t + 1, :] = v[:, t * LANES : (t + 1) * LANES]

    half = lambda rows: lax.broadcasted_iota(jnp.int32, (rows, LANES), 0)
    groups = given.groups
    sides = [(so - 4 + 2 * groups[c * b + k]) for k in range(b)]
    areas = [(s * s).astype(F32) for s in sides]
    for k in range(b):
        def fill_out(t, _, k=k):
            p = half(2 * so) + t * (2 * so)
            ok = (lax.div(p, so) < sides[k]) & (lax.rem(p, so) < sides[k])
            r.mo[span(k * po + t * (2 * so), 2 * so), :] = jnp.where(ok, 1.0, 0.0)
            return 0

        lax.fori_loop(0, po // (2 * so), fill_out, 0)

        def fill_in(t, _, k=k):
            p = half(2 * si) + t * (2 * si)
            ok = (lax.div(p, si) < 2 * sides[k]) & (lax.rem(p, si) < 2 * sides[k])
            r.mi[span(k * pi_ + t * (2 * si), 2 * si), :] = jnp.where(ok, 1.0, 0.0).astype(BF16)
            return 0

        lax.fori_loop(0, pi_ // (2 * si), fill_in, 0)
    row8 = lax.broadcasted_iota(jnp.int32, (8, LANES), 0)
    live8 = jnp.where(row8 < b, 1.0, 0.0)
    inv_area = jnp.zeros((8, LANES), F32)
    for k in range(b):
        inv_area = jnp.where(row8 == k, 1.0 / jnp.full((8, LANES), areas[k], F32), inv_area)
    for ref in (r.blk[1].pm, r.blk[2].pm, r.ags):
        ref[...] = jnp.zeros_like(ref)

    pool_rows = part // 4

    def pool_matrix(out_axis):
        shape = (pool_rows, part) if out_axis == 0 else (part, pool_rows)
        o = lax.broadcasted_iota(jnp.int32, shape, out_axis)
        p = lax.broadcasted_iota(jnp.int32, shape, 1 - out_axis)
        row, col = lax.div(p, si), lax.rem(p, si)
        hit = (lax.div(row, 2) * so + lax.div(col, 2)) == o
        return jnp.where(hit, 0.25, 0.0).astype(BF16)

    low_half = lax.broadcasted_iota(jnp.int32, (1, LANES), 1) < z.mids
    vv = r.vv

    def v_mid(row):
        return jnp.concatenate(
            [
                jnp.where(low_half, vv[s, row : row + 1, :], vv[s + 1, row : row + 1, :])
                for s in range(0, nc, 2)
            ],
            axis=1,
        )

    def v_split(row):
        return jnp.concatenate([v_mid(row), v_mid(row + 1)], axis=1)

    def v_co(row):
        return jnp.concatenate(
            [
                vv[s, row + t : row + t + 1, :]
                for s in range(nc)
                for t in range(z.cos // LANES)
            ],
            axis=1,
        )

    def norm(k, row1, row2, width, inv_n, gain, bias):
        n = tiled(inv_n, width)
        mean = total(k, row1, width) * n
        inv = lax.rsqrt(total(k, row2, width) * n - mean * mean + EPSILON)
        scale = gain * inv
        return SimpleNamespace(mean=mean, inv=inv, gs=scale, sh=bias - mean * scale)

    def norm_grad(k, rowu, rowv, width, inv_n, nm):
        n = tiled(inv_n, width)
        su = total(k, rowu, width)
        sux = nm.inv * (total(k, rowv, width) - nm.mean * su)
        t = sux * n
        return (
            su,
            sux,
            nm.gs * (su * n - nm.mean * nm.inv * t),
            nm.gs * nm.inv * t,
        )

    def loop(n, tile, body, init):
        def step(i, carry):
            return body(pl.multiple_of(i * tile, tile), carry)

        return lax.fori_loop(0, n // tile, step, init)

    def zero8(width):
        return jnp.zeros((8, width), F32)

    def moments(ref, rows, width, tile):
        def body(at, carry):
            s1, s2 = carry
            v = ref[pl.ds(at, tile), :]
            mv = v * tiled(r.mo[pl.ds(at, tile), :], width)
            return s1 + sum8(mv), s2 + sum8(mv * v)

        s1, s2 = loop(rows, tile, body, (zero8(width), zero8(width)))
        return fold(s1), fold(s2)

    red1 = r.red1

    def row_pair(ref, i):
        return jnp.concatenate(
            [ref[t, pl.ds(i, 1)].reshape(2 * si, LANES) for t in range(mid // LANES)], axis=1
        )

    def phase_of(t, lead, p, q):
        return red1[t, lead, p, pl.ds(q, so, stride=2), :].reshape(4 * so, LANES)

    pool_m = pool_matrix(0)
    first_w.wrt.forward()
    first_w.wrt.wait()
    r1, r2 = zero8(mid), zero8(mid)
    for q in range(nq):
        ex.x[q].wait()
        xv = r.x[q * part : (q + 1) * part, :]
        lead = part // (2 * si)
        reduced = dot(xv, r.blk[1].wrt[...], NT)
        for t in range(mid // LANES):
            red1[t, q * lead : (q + 1) * lead] = reduced[:, t * LANES : (t + 1) * LANES].reshape(
                lead, 2, si, LANES
            )

        def red_sums(i, carry, q=q, lead=lead):
            s1, s2 = carry
            v = row_pair(red1, q * lead + i)
            m = r.mi[span((q * lead + i) * 2 * si, 2 * si), :].astype(F32)
            mv = v * tiled(m, mid)
            return s1 + sum8(mv), s2 + sum8(mv * v)

        r1, r2 = lax.fori_loop(0, lead, red_sums, (r1, r2))
    first_w.wst.start()
    put(0, 0, fold(r1))
    put(0, mid // LANES, fold(r2))
    at = 2 * mid // LANES
    local_area = areas[0]
    for k in range(1, b):
        local_area = local_area + areas[k]
    put(0, at, jnp.full((1, LANES), local_area, F32))

    def pooling():
        for q in range(nq):
            r.pool[q * pool_rows : (q + 1) * pool_rows, :] = dot(
                pool_m, r.x[q * part : (q + 1) * part, :]
            ).astype(BF16)

    allreduce(0, at + 1, pooling)
    ex.vec.wait()
    count = total(0, at, LANES)
    inv_out = 1.0 / count
    inv_in = 0.25 * inv_out
    vr1, vr2 = VEC_ROWS[1], VEC_ROWS[2]
    nred1 = norm(0, 0, mid // LANES, mid, inv_in, v_mid(vr1.rg), v_mid(vr1.rb))
    lane16 = lax.rem(lax.broadcasted_iota(jnp.int32, (4 * so, mid), 0), so)
    not_first = lane16 > 0
    not_last = lane16 < so - 1

    def im_put(im, at, w, di, dj, shift):
        tap = di * 3 + dj
        low = w.astype(BF16)
        for g in range(2):
            im[g, pl.ds(pl.multiple_of(at + so + shift * so, so), 4 * so), tap * grp : (tap + 1) * grp] = (
                low[:, g * grp : (g + 1) * grp]
            )

    def im_zero(im, di, last):
        for k in range(b):
            row = so + k * po + (po - so if last else 0)
            for g in range(2):
                im[g, row : row + so, di * 3 * grp : (di + 1) * 3 * grp] = jnp.zeros(
                    (so, 3 * grp), BF16
                )

    im1 = r.blk[1].im

    def build1(i, _):
        at = pl.multiple_of(i * 4 * so, 4 * so)
        m = tiled(r.mo[pl.ds(at, 4 * so), :], mid)
        for p in range(2):
            for q in range(2):
                v = jnp.concatenate(
                    [phase_of(t, pl.ds(i * 4, 4), p, q) for t in range(mid // LANES)], axis=1
                )
                w = silu(v * nred1.gs + nred1.sh) * m
                for dj in ((1,) if q == 0 else (2, 0)):
                    wj = w
                    if dj == 0:
                        wj = jnp.where(not_first, pltpu.roll(w, 1, 0), 0.0)
                    for di in ((1,) if p == 0 else (2, 0)):
                        im_put(im1, at, wj, di, dj, 1 if di == 0 else 0)
        return 0

    for e in (first_w.sq, first_w.ext, first_w.we, ex.wsh):
        e.start()
    lax.fori_loop(0, no // (4 * so), build1, 0)
    first_w.wst.forward()
    im_zero(im1, 0, False)

    def split_weights(k, g):
        return jnp.concatenate([r.blk[k].wst[t, g] for t in range(TAPS)], axis=1)

    def split_conv(k):
        ex.blk[k].wst.wait()
        for g in range(2):
            r.blk[k].sp[:, g * mid : (g + 1) * mid] = dot(
                r.blk[k].im[g, so : so + no, :], split_weights(k, g), NT
            )
        return moments(r.blk[k].sp, no, 2 * mid, 32)

    def attention_forward(k, vr, sync, fills):
        s1, s2 = split_conv(k)
        put(sync, 0, s1)
        put(sync, 4, s2)
        allreduce(sync, 8, fills[0])
        nsplit = norm(sync, 0, 4, 2 * mid, inv_out, v_split(vr.sg), v_split(vr.sb))
        sp, sa, pm = r.blk[k].sp, r.blk[k].sa, r.blk[k].pm
        for img in range(b):
            def act(at, s, img=img):
                rows = pl.ds(pl.multiple_of(at + img * po, 32), 32)
                v = silu(sp[rows, :] * nsplit.gs + nsplit.sh)
                v = v * tiled(r.mo[rows, :], 2 * mid)
                sa[rows, :] = v
                return s + sum8(v)

            s = fold(loop(po, 32, act, zero8(2 * mid)))
            pm[img : img + 1, :] = (s[:, :mid] + s[:, mid:]) * tiled(inv_area[img : img + 1, :], mid)
        ex.blk[k].sq.wait()
        squeezed = dot_exact(pm[...], r.blk[k].sq[...])
        put(sync + 1, 0, fold(squeezed))
        put(sync + 1, 1, fold(squeezed * squeezed))
        put(sync + 1, 2, fold(pm[...]))
        allreduce(sync + 1, 4, fills[1])
        inv_images = jnp.full((1, LANES), 1.0 / (b * nc * nd), F32)
        natt = norm(
            sync + 1, 0, 1, att, inv_images, vv[0, vr.qg : vr.qg + 1, :],
            vv[0, vr.qb : vr.qb + 1, :],
        )
        xhat = (squeezed - natt.mean) * natt.inv
        centred = pm[...] - total(sync + 1, 2, mid) * tiled(inv_images, mid)
        pre = squeezed * natt.gs + natt.sh
        excited = silu(pre) * live8
        ex.blk[k].ext.wait()
        halves = []
        for g in range(2):
            bias = v_mid(vr.xb + g)
            halves.append(dot_exact(excited, r.blk[k].ext[g], NT) + bias)
        top = jnp.maximum(halves[0], halves[1])
        e0, e1 = jnp.exp(halves[0] - top), jnp.exp(halves[1] - top)
        whole_sum = e0 + e1
        at_ref = r.blk[k].att
        at_ref[:, :mid] = e0 / whole_sum
        at_ref[:, mid:] = e1 / whole_sum
        for img in range(b):
            def mix(at, _, img=img):
                rows = pl.ds(pl.multiple_of(at + img * po, 32), 32)
                v = sa[rows, :] * at_ref[img : img + 1, :]
                r.blk[k].mix[rows, :] = (v[:, :mid] + v[:, mid:]).astype(BF16)
                return 0

            loop(po, 32, mix, 0)
        ex.blk[k].we.wait()
        for n0 in range(0, co, 256):
            r.blk[k].exp[:, n0 : n0 + 256] = dot(r.blk[k].mix[...], r.blk[k].we[:, n0 : n0 + 256])
        s1, s2 = moments(r.blk[k].exp, no, co, 16)
        put(sync + 2, 0, s1)
        put(sync + 2, co // LANES, s2)
        if k == 1:
            for n, v in enumerate(short_sums):
                put(sync + 2, (2 + n) * co // LANES, v)
        allreduce(sync + 2, (4 if k == 1 else 2) * co // LANES, fills[2])
        nexp = norm(sync + 2, 0, co // LANES, co, inv_out, v_co(vr.eg), v_co(vr.eb))
        return SimpleNamespace(nsplit=nsplit, natt=natt, xhat=xhat, pre=pre, excited=excited, nexp=nexp, centred=centred)

    short_sums = []

    def shortcut_forward():
        ex.wsh.wait()
        for n0 in range(0, co, 256):
            r.short[:, n0 : n0 + 256] = dot(r.pool[...], r.wsh[:, n0 : n0 + 256])
        short_sums.extend(moments(r.short, no, co, 16))

    def forward_first():
        for e in (first_w.sq, first_w.ext, first_w.we):
            e.forward()
        second_w.wrt.start()

    def between():
        ex.wsh.forward()
        second_w.wst.start()
        shortcut_forward()

    def forward_second():
        second_w.wrt.forward()
        for e in (second_w.sq, second_w.ext, second_w.we):
            e.start()

    f1 = attention_forward(1, vr1, 1, (forward_first, between, forward_second))
    nshort = norm(
        3, 2 * co // LANES, 3 * co // LANES, co, inv_out, v_co(vr1.hg), v_co(vr1.hb)
    )

    def summed1(rows):
        return (
            r.blk[1].exp[rows, :] * f1.nexp.gs
            + f1.nexp.sh
            + r.short[rows, :] * nshort.gs
            + nshort.sh
        )

    def hidden(at, _):
        rows = pl.ds(at, 16)
        r.h[rows, :] = (silu(summed1(rows)) * tiled(r.mo[rows, :], co)).astype(BF16)
        return 0

    loop(no, 16, hidden, 0)

    ex.blk[2].wrt.wait()
    r.red2[...] = dot(r.h[...], r.blk[2].wrt[...], NT)
    s1, s2 = moments(r.red2, no, mid, 64)
    put(4, 0, s1)
    put(4, 2, s2)

    def forward_rest():
        ex.cot.start()
        second_w.wst.forward()
        for e in (second_w.sq, second_w.ext, second_w.we):
            e.forward()

    allreduce(4, 4, forward_rest)
    nred2 = norm(4, 0, 2, mid, inv_out, v_mid(vr2.rg), v_mid(vr2.rb))
    im2 = r.blk[2].im

    def build2(i, _):
        at = pl.multiple_of(i * 4 * so, 4 * so)
        m = tiled(r.mo[pl.ds(at, 4 * so), :], mid)
        w = silu(r.red2[pl.ds(at, 4 * so), :] * nred2.gs + nred2.sh) * m
        for dj in range(3):
            wj = w
            if dj == 0:
                wj = jnp.where(not_first, pltpu.roll(w, 1, 0), 0.0)
            if dj == 2:
                wj = jnp.where(not_last, pltpu.roll(w, 4 * so - 1, 0), 0.0)
            for di in range(3):
                im_put(im2, at, wj, di, dj, 1 - di)
        return 0

    lax.fori_loop(0, no // (4 * so), build2, 0)
    im_zero(im2, 0, False)
    im_zero(im2, 2, True)
    f2 = attention_forward(2, vr2, 5, (None, None, None))

    ex.cot.wait()

    def finish(at, carry):
        su, sv = carry
        rows = pl.ds(at, 16)
        m = tiled(r.mo[rows, :], co)
        v = r.blk[2].exp[rows, :]
        s = v * f2.nexp.gs + f2.nexp.sh + r.h[rows, :].astype(F32)
        q = sigmoid(s)
        u = r.cot[rows, :].astype(F32) * m * (q * (1.0 + s * (1.0 - q)))
        r.cot[rows, :] = (s * q * m).astype(BF16)
        r.g[rows, :] = u
        return su + sum8(u), sv + sum8(u * v)

    su, sv = loop(no, 16, finish, (zero8(co), zero8(co)))
    out_part = no // OUT_PARTS
    out_ex = [
        Exchange(
            lambda s, n=n: r.cot.at[
                pl.ds(n * out_part, out_part), pl.ds(pl.multiple_of(s * z.cos, LANES), z.cos)
            ],
            lambda s, n=n: made.out.at[
                pl.ds(pl.multiple_of(s * no + n * out_part, out_part), out_part), :
            ],
            os_sem.at[n],
            or_sem.at[n],
        )
        for n in range(OUT_PARTS)
    ]
    put(8, 0, fold(su))
    put(8, co // LANES, fold(sv))
    allreduce(8, 2 * co // LANES)
    out_ex[0].start()

    def pack_rows(k, name, skip, v):
        group, at = z.lay[(k, name)]
        at, share = at + skip * z.mids, z.mids
        for s in range(nc):
            for t in range(v.shape[1] // LANES):
                r.group[group].pk[s // 2, s % 2, at + t * share : at + (t + 1) * share, :] = v[
                    s * share : (s + 1) * share, t * LANES : (t + 1) * LANES
                ].astype(BF16)

    def pack_lanes(k, name, s, v):
        group, at = z.lay[(k, name)]
        rows = v.shape[0]
        for t in range(v.shape[1] // LANES):
            r.group[group].pk[s // 2, s % 2, at + t * rows : at + (t + 1) * rows, :] = v[
                :, t * LANES : (t + 1) * LANES
            ].astype(BF16)

    class Reduction:
        def __init__(self, group):
            own = r.group[group]
            self.pk, self.r1, self.r2, self.r3 = own.pk, own.r1, own.r2, own.r3
            self.rows = z.rows[group]
            self.piece = self.rows // z.near
            self.r4 = own.r4
            self.near, self.mine = lax.rem(d, z.near), lax.div(d, z.near)
            self.res = made.res[group]
            self.sems = [own.q1, own.q2, own.q3s, own.q3r, own.q4s, own.q4r, own.q5s, own.q5r]
            self.across = lax.div(c, 2)

        def piece_at(self, n):
            return pl.ds(pl.multiple_of(n * self.piece, 16), self.piece)

        def copy1(self):
            return pltpu.make_async_remote_copy(
                src_ref=self.pk.at[:, 1 - odd], dst_ref=self.r1, send_sem=self.sems[0].at[0],
                recv_sem=self.sems[0].at[1], device_id=partner, device_id_type=MESH,
            )

        def copy2(self):
            return pltpu.make_async_remote_copy(
                src_ref=self.pk.at[1 - self.across, odd], dst_ref=self.r2,
                send_sem=self.sems[1].at[0], recv_sem=self.sems[1].at[1],
                device_id=(d, chan_at(2)), device_id_type=MESH,
            )

        def at_near(self, n):
            return (self.mine * z.near + n, c)

        def copy3(self, to, src):
            return pltpu.make_async_remote_copy(
                src_ref=self.pk.at[self.across, odd, self.piece_at(to), :],
                dst_ref=self.r3.at[src], send_sem=self.sems[2].at[to],
                recv_sem=self.sems[3].at[src], device_id=self.at_near(to), device_id_type=MESH,
            )

        def copy4(self, to, src):
            return pltpu.make_async_remote_copy(
                src_ref=self.r3.at[self.near], dst_ref=self.res.at[self.piece_at(src), :],
                send_sem=self.sems[4].at[to], recv_sem=self.sems[5].at[src],
                device_id=self.at_near(to), device_id_type=MESH,
            )

        def copy5(self, to, src):
            return pltpu.make_async_remote_copy(
                src_ref=self.r4.at[self.mine], dst_ref=self.r4.at[src],
                send_sem=self.sems[6].at[to], recv_sem=self.sems[7].at[src],
                device_id=(to * z.near + self.near, c), device_id_type=MESH,
            )

        def local4(self):
            return pltpu.make_async_copy(
                self.r3.at[self.near], self.res.at[self.piece_at(self.near), :],
                self.sems[5].at[self.near],
            )

        def others(self, body, me, n):
            def step(j, _):
                body(lax.rem(me + j, n), lax.rem(me - j + n, n))
                return 0

            lax.fori_loop(1, n, step, 0)

        def total(self, slots, n, to):
            def body(at, _):
                rows = pl.ds(at, 16)
                t = slots[0, rows, :].astype(F32)
                for k in range(1, n):
                    t = t + slots[k, rows, :].astype(F32)
                to[rows, :] = t.astype(BF16)
                return 0

            loop(self.piece, 16, body, 0)

        def add(self, which, other):
            def body(at, _):
                rows = pl.ds(at, 128)
                self.pk[which, odd, rows, :] = (
                    self.pk[which, odd, rows, :].astype(F32) + other(rows).astype(F32)
                ).astype(BF16)
                return 0

            loop(self.rows, 128, body, 0)

        def step1(self):
            self.copy1().start()

        def ready2(self):
            self.copy1().wait()
            for which in (1 - self.across, self.across):
                self.add(which, lambda rows, which=which: self.r1[which, rows, :])

        def step2(self):
            self.copy2().start()

        def ready3(self):
            self.copy2().wait()
            self.add(self.across, lambda rows: self.r2[rows, :])

        def step3(self):
            self.others(lambda to, _: self.copy3(to, self.near).start(), self.near, z.near)

        def ready4(self):
            self.r3[self.near] = self.pk[self.across, odd, self.piece_at(self.near), :]

            def arrive(to, src):
                self.copy3(to, self.near).wait_send()
                self.copy3(src, src).wait_recv()

            self.others(arrive, self.near, z.near)
            mine = self.r3.at[self.near]
            if z.far == 1:
                self.total(self.r3, z.near, mine)
            else:
                self.total(self.r3, z.near, self.r4.at[self.mine])
                self.others(lambda to, _: self.copy5(to, self.mine).start(), self.mine, z.far)

                def arrive_far(to, src):
                    self.copy5(to, self.mine).wait_send()
                    self.copy5(src, src).wait_recv()

                self.others(arrive_far, self.mine, z.far)
                self.total(self.r4, z.far, mine)

        def step4(self):
            self.local4().start()
            self.others(lambda to, _: self.copy4(to, self.near).start(), self.near, z.near)

        def finish(self):
            self.local4().wait()

            def arrive(to, src):
                self.copy4(to, self.near).wait_send()
                self.copy4(src, src).wait_recv()

            self.others(arrive, self.near, z.near)

    class SplitReduction(Reduction):
        def __init__(self, group):
            super().__init__(group)
            self.ry, self.q6 = r.group[group].ry, r.group[group].q6
            self.half = self.rows // 2
            self.par, self.far_at = lax.rem(self.near, 2), lax.div(self.near, 2)
            self.quad = z.near // 2
            self.mate = self.at_near(self.near + 1 - 2 * self.par)

        def half_at(self, par):
            return pl.ds(pl.multiple_of(par * self.half, 16), self.half)

        def piece_at(self, n):
            at = lax.rem(n, 2) * self.half + lax.div(n, 2) * self.piece
            return pl.ds(pl.multiple_of(at, 16), self.piece)

        def copy_half(self):
            return pltpu.make_async_remote_copy(
                src_ref=self.pk.at[self.across, odd, self.half_at(1 - self.par), :],
                dst_ref=self.ry, send_sem=self.q6.at[0], recv_sem=self.q6.at[1],
                device_id=self.mate, device_id_type=MESH,
            )

        def copy_back(self, par):
            rows = self.half_at(par)
            return pltpu.make_async_remote_copy(
                src_ref=self.res.at[rows, :], dst_ref=self.res.at[rows, :],
                send_sem=self.q6.at[2], recv_sem=self.q6.at[3],
                device_id=self.mate, device_id_type=MESH,
            )

        def slot3(self, to, src):
            n = 2 * to + self.par
            return pltpu.make_async_remote_copy(
                src_ref=self.pk.at[self.across, odd, self.piece_at(n), :],
                dst_ref=self.r3.at[src], send_sem=self.sems[2].at[to],
                recv_sem=self.sems[3].at[src], device_id=self.at_near(n), device_id_type=MESH,
            )

        def slot4(self, to, src):
            return pltpu.make_async_remote_copy(
                src_ref=self.r3.at[self.far_at],
                dst_ref=self.res.at[self.piece_at(2 * src + self.par), :],
                send_sem=self.sems[4].at[to], recv_sem=self.sems[5].at[src],
                device_id=self.at_near(2 * to + self.par), device_id_type=MESH,
            )

        def local5(self):
            return pltpu.make_async_copy(
                self.r3.at[self.far_at], self.res.at[self.piece_at(self.near), :],
                self.sems[5].at[self.far_at],
            )

        def step3(self):
            self.copy_half().start()

        def ready4(self):
            self.copy_half().wait()

            def body(at, _):
                rows = pl.ds(pl.multiple_of(self.par * self.half + at, 16), 16)
                self.pk[self.across, odd, rows, :] = (
                    self.pk[self.across, odd, rows, :].astype(F32)
                    + self.ry[pl.ds(at, 16), :].astype(F32)
                ).astype(BF16)
                return 0

            loop(self.half, 16, body, 0)

        def step4(self):
            self.others(lambda to, _: self.slot3(to, self.far_at).start(), self.far_at, self.quad)

        def ready5(self):
            self.r3[self.far_at] = self.pk[self.across, odd, self.piece_at(self.near), :]

            def arrive(to, src):
                self.slot3(to, self.far_at).wait_send()
                self.slot3(src, src).wait_recv()

            self.others(arrive, self.far_at, self.quad)
            mine = self.r3.at[self.far_at]
            if z.far == 1:
                self.total(self.r3, self.quad, mine)
            else:
                self.total(self.r3, self.quad, self.r4.at[self.mine])
                self.others(lambda to, _: self.copy5(to, self.mine).start(), self.mine, z.far)

                def arrive_far(to, src):
                    self.copy5(to, self.mine).wait_send()
                    self.copy5(src, src).wait_recv()

                self.others(arrive_far, self.mine, z.far)
                self.total(self.r4, z.far, mine)

        def step5(self):
            self.local5().start()
            self.others(lambda to, _: self.slot4(to, self.far_at).start(), self.far_at, self.quad)

        def ready6(self):
            self.local5().wait()

            def arrive(to, src):
                self.slot4(to, self.far_at).wait_send()
                self.slot4(src, src).wait_recv()

            self.others(arrive, self.far_at, self.quad)

        def step6(self):
            self.copy_back(self.par).start()

        def finish(self):
            self.copy_back(self.par).wait_send()
            self.copy_back(1 - self.par).wait_recv()

    sums_of = {group: (SplitReduction if group == 2 else Reduction)(group) for group in GROUPS}

    def attention_backward(k, f, sync):
        srow = STO_ROWS[k]
        nexp, nsplit, natt = f.nexp, f.nsplit, f.natt
        first = k == 1
        cw = co // LANES
        su, sux, ea, eb = norm_grad(sync, 0, cw, co, inv_out, nexp)
        keep(srow.eb, su)
        keep(srow.eg, sux)
        if first:
            _, suxh, ha, hb = norm_grad(sync, 0, 2 * cw, co, inv_out, nshort)
            keep(srow.hg, suxh)

        def expand_grad(at, _):
            rows = pl.ds(at, 16)
            m = tiled(r.mo[rows, :], co)
            u = r.g[rows, :]
            r.eg[rows, :] = (nexp.gs * u - m * (ea + eb * r.blk[k].exp[rows, :])).astype(BF16)
            if first:
                r.shg[rows, :] = (
                    nshort.gs * u - m * (ha + hb * r.short[rows, :])
                ).astype(BF16)
            return 0

        loop(no, 16, expand_grad, 0)
        r.mg[...] = dot(r.eg[...], r.blk[k].we[...], NT)
        sa = r.blk[k].sa
        for img in range(b):
            def att_grad(at, s, img=img):
                rows = pl.ds(pl.multiple_of(at + img * po, 32), 32)
                return s + sum8(sa[rows, :] * tiled_pair(r.mg[rows, :]))

            r.ags[img : img + 1, :] = fold(loop(po, 32, att_grad, zero8(2 * mid)))
        ags, at_ref = r.ags, r.blk[k].att
        a0, a1 = at_ref[:, :mid], at_ref[:, mid:]
        g0, g1 = ags[:, :mid], ags[:, mid:]
        mean = a0 * g0 + a1 * g1
        l0, l1 = a0 * (g0 - mean), a1 * (g1 - mean)
        ext = r.blk[k].ext
        excited_grad = dot_exact(l0, ext[0]) + dot_exact(l1, ext[1])
        au = excited_grad * silu_slope(f.pre)
        put(sync + 1, 0, fold(au))
        put(sync + 1, 1, fold(au * f.xhat))
        put(sync + 1, 2, fold(l0))
        put(sync + 1, 4, fold(l1))

        def matrices():
            r.mixt[...] = jnp.transpose(r.blk[k].mix[...])
            for s in range(nc):
                share = slice(s * z.cos, (s + 1) * z.cos)
                pack_lanes(k, EXPAND, s, dot(r.mixt[...], r.eg[:, share]))
            pack_rows(k, EXCITE, 0, dot_exact(l0, f.excited, TN))
            pack_rows(k, EXCITE, 1, dot_exact(l1, f.excited, TN))
            if first:
                r.sgt[...] = jnp.transpose(r.pool[...])
                for s in range(nc):
                    share = slice(s * z.cos, (s + 1) * z.cos)
                    pack_lanes(k, SHORTCUT, s, dot(r.sgt[...], r.shg[:, share]))
                sums_of[2].step1()
                sums_of[5].ready2()
                sums_of[1].ready3()
                r.pg[...] = dot(r.shg[...], r.wsh[...], NT).astype(BF16)

            else:
                sums_of[0].step1()

        allreduce(sync + 1, 6, matrices)
        inv_images = 1.0 / (b * nc * nd)
        su, sux = total(sync + 1, 0, att), total(sync + 1, 1, att)
        keep(srow.qb, su)
        keep(srow.qg, sux)
        keep(srow.xb, total(sync + 1, 2, 2 * mid))
        sb = natt.gs * (au - su * inv_images - f.xhat * (sux * inv_images)) * live8
        if first:
            sums_of[1].step3()
            sums_of[2].ready2()
            sums_of[2].step2()
        else:
            out_ex[1].start()
        r.mgr[...] = dot_exact(sb, r.blk[k].sq[...], NT) * tiled(inv_area, mid)
        sp = r.blk[k].sp
        carry = (zero8(2 * mid), zero8(2 * mid))
        for img in range(b):
            def split_up(at, carry, img=img):
                s1, s2 = carry
                rows = pl.ds(pl.multiple_of(at + img * po, 32), 32)
                m = tiled(r.mo[rows, :], 2 * mid)
                v = sp[rows, :]
                grad = tiled_pair(r.mg[rows, :]) * at_ref[img : img + 1, :] + tiled_pair(
                    r.mgr[img : img + 1, :]
                )
                u = grad * m * silu_slope(v * nsplit.gs + nsplit.sh)
                r.su[rows, :] = u
                return s1 + sum8(u), s2 + sum8(u * v)

            carry = loop(po, 32, split_up, carry)
        put(sync + 2, 0, fold(carry[0]))
        put(sync + 2, 4, fold(carry[1]))

        def squeeze_matrix():
            pack_rows(k, SQUEEZE, 0, dot_exact(f.centred, sb, TN))
            if first:
                sums_of[1].ready4()
            else:
                sums_of[0].ready2()

        allreduce(sync + 2, 8, squeeze_matrix)
        if first:
            sums_of[1].step4()
            sums_of[5].step2()
        else:
            sums_of[0].step2()
            out_ex[2].start()
        su, sux, ca, cb = norm_grad(sync + 2, 0, 4, 2 * mid, inv_out, nsplit)
        keep(srow.sb, su)
        keep(srow.sg, sux)

        def split_grad(at, _):
            rows = pl.ds(at, 32)
            m = tiled(r.mo[rows, :], 2 * mid)
            r.sgb[rows, :] = (
                nsplit.gs * r.su[rows, :] - m * (ca + cb * sp[rows, :])
            ).astype(BF16)
            return 0

        loop(no, 32, split_grad, 0)

    def tiled_pair(v):
        return jnp.concatenate([v, v], axis=1)

    def split_matrix(k):
        r.sgt[...] = jnp.transpose(r.sgb[...])
        for g in range(2):
            for t in range(3):
                v = dot(
                    r.sgt[g * mid : (g + 1) * mid, :],
                    r.blk[k].im[g, so : so + no, 3 * t * grp : 3 * (t + 1) * grp],
                )
                for u in range(3):
                    pack_rows(
                        k, SPLIT, (3 * t + u) * 2 + g, v[:, u * grp : (u + 1) * grp]
                    )

    dcol = r.dcol
    dcol[:so, :] = jnp.zeros((so, kk), F32)
    dcol[so + po :, :] = jnp.zeros((so, kk), F32)

    def columns(k, img, g):
        dcol[so : so + po, :] = dot(
            r.sgb[img * po : (img + 1) * po, g * mid : (g + 1) * mid], split_weights(k, g)
        )

    tile = 4 * so
    first_g, last_g = not_first[:, :grp], not_last[:, :grp]

    def tap(at, di, dj, shift):
        t = di * 3 + dj
        return dcol[pl.ds(pl.multiple_of(at + so - shift * so, so), tile), t * grp : (t + 1) * grp]

    def from_left(v):
        return jnp.where(first_g, pltpu.roll(v, 1, 0), 0.0)

    def from_right(v):
        return jnp.where(last_g, pltpu.roll(v, tile - 1, 0), 0.0)

    attention_backward(2, f2, 8)
    sums = []
    for g in range(2):
        carry = (zero8(grp), zero8(grp))
        lanes = slice(g * grp, (g + 1) * grp)
        for img in range(b):
            columns(2, img, g)

            def back2(at, carry, img=img, g=g, lanes=lanes):
                s1, s2 = carry
                cols = [
                    tap(at, 0, dj, -1) + tap(at, 1, dj, 0) + tap(at, 2, dj, 1) for dj in range(3)
                ]
                grad = cols[1] + from_right(cols[0]) + from_left(cols[2])
                rows = pl.ds(pl.multiple_of(at + img * po, tile), tile)
                v = r.red2[rows, lanes]
                u = (
                    grad
                    * tiled(r.mo[rows, :], grp)
                    * silu_slope(v * nred2.gs[:, lanes] + nred2.sh[:, lanes])
                )
                r.u2[rows, lanes] = u
                return s1 + sum8(u), s2 + sum8(u * v)

            carry = loop(po, tile, back2, carry)
        sums.append(carry)
    put(11, 0, jnp.concatenate([fold(s[0]) for s in sums], axis=1))
    put(11, 2, jnp.concatenate([fold(s[1]) for s in sums], axis=1))
    def split_matrix2():
        split_matrix(2)
        sums_of[1].step1()
        sums_of[0].ready3()

    allreduce(11, 4, split_matrix2)
    sums_of[0].step3()
    out_ex[3].start()
    su, sux, ca, cb = norm_grad(11, 0, 2, mid, inv_out, nred2)
    keep(STO_ROWS[2].rb, su)
    keep(STO_ROWS[2].rg, sux)

    def reduce_grad2(at, _):
        rows = pl.ds(at, 64)
        m = tiled(r.mo[rows, :], mid)
        r.rg1[rows, :] = (
            nred2.gs * r.u2[rows, :] - m * (ca + cb * r.red2[rows, :])
        ).astype(BF16)
        return 0

    loop(no, 64, reduce_grad2, 0)
    for n0 in range(0, co, 256):
        cols = slice(n0, n0 + 256)
        r.g[:, cols] = r.g[:, cols] + dot(r.rg1[:no, :], r.blk[2].wrt[:, cols])

    def first_up(at, carry):
        s1, s2, s3 = carry
        rows = pl.ds(at, 16)
        u = r.g[rows, :] * tiled(r.mo[rows, :], co) * silu_slope(summed1(rows))
        r.g[rows, :] = u
        return (
            s1 + sum8(u),
            s2 + sum8(u * r.blk[1].exp[rows, :]),
            s3 + sum8(u * r.short[rows, :]),
        )

    s1, s2, s3 = loop(no, 16, first_up, (zero8(co), zero8(co), zero8(co)))
    put(12, 0, fold(s1))
    put(12, co // LANES, fold(s2))
    put(12, 2 * co // LANES, fold(s3))

    def reduce_matrix2():
        r.rgt[:, :no] = jnp.transpose(r.rg1[:no, :])
        for n0 in range(0, co, 256):
            pack_rows(2, REDUCE, n0 // LANES, dot(r.rgt[:, :no], r.h[:, n0 : n0 + 256]))
        sums_of[5].step1()
        sums_of[1].ready2()
        sums_of[0].ready4()

    allreduce(12, 3 * co // LANES, reduce_matrix2)
    sums_of[1].step2()
    sums_of[0].step4()

    attention_backward(1, f1, 12)
    sums = []
    for g in range(2):
        carry = (zero8(grp), zero8(grp))
        lanes = slice(g * grp, (g + 1) * grp)
        for img in range(b):
            columns(1, img, g)

            def back1(at, carry, img=img, g=g, lanes=lanes):
                s1, s2 = carry
                rows = pl.ds(pl.multiple_of(at + img * po, tile), tile)
                m = tiled(r.mo[rows, :], grp)
                lead = pl.ds(pl.multiple_of(lax.div(at, so) + img * so, 4), 4)
                for p in range(2):
                    for q in range(2):
                        def col(dj):
                            if p == 0:
                                return tap(at, 1, dj, 0)
                            return tap(at, 0, dj, -1) + tap(at, 2, dj, 0)

                        grad = col(1) if q == 0 else col(2) + from_right(col(0))
                        v = phase_of(g, lead, p, q)
                        u = grad * m * silu_slope(v * nred1.gs[:, lanes] + nred1.sh[:, lanes])
                        r.u1[g, lead, p, pl.ds(q, so, stride=2), :] = u.reshape(4, so, grp)
                        s1, s2 = s1 + sum8(u), s2 + sum8(u * v)
                return s1, s2

            carry = loop(po, tile, back1, carry)
        sums.append(carry)
    put(15, 0, jnp.concatenate([fold(s[0]) for s in sums], axis=1))
    put(15, 2, jnp.concatenate([fold(s[1]) for s in sums], axis=1))

    def split_matrix1():
        split_matrix(1)
        sums_of[3].step1()
        sums_of[2].ready3()
        sums_of[2].step3()
        sums_of[3].ready2()
        sums_of[5].ready3()

    allreduce(15, 4, split_matrix1)
    sums_of[5].step3()
    su, sux, ca, cb = norm_grad(15, 0, 2, mid, inv_in, nred1)
    keep(STO_ROWS[1].rb, su)
    keep(STO_ROWS[1].rg, sux)

    def reduce_grad1(i, _):
        rows = pl.ds(pl.multiple_of(i * 2 * si, 2 * si), 2 * si)
        m = tiled(r.mi[rows, :].astype(F32), mid)
        u, v = row_pair(r.u1, i), row_pair(red1, i)
        r.rg1[rows, :] = (nred1.gs * u - m * (ca + cb * v)).astype(BF16)
        return 0

    spread = pool_matrix(1)
    grads = (r.h, r.eg)
    last = []

    def send_quarter(q):
        rows = slice(q * part, (q + 1) * part)
        m = tiled(r.mi[rows, :].astype(F32), 256)
        for n0 in range(0, ci, 256):
            cols = slice(n0, n0 + 256)
            v = dot(r.rg1[rows, :], r.blk[1].wrt[:, cols]) + dot(
                spread, r.pg[q * pool_rows : (q + 1) * pool_rows, cols]
            )
            at = (q % 2) * ci + n0
            grads[q // 2][:, at : at + 256] = (v * m).astype(BF16)
        e = Exchange(
            lambda s, q=q: grads[q // 2].at[
                :, pl.ds(pl.multiple_of((q % 2) * ci + s * z.cis, LANES), z.cis)
            ],
            lambda s, q=q: made.gx.at[
                pl.ds(pl.multiple_of(s * ni + q * part, part), part), :
            ],
            os_sem.at[OUT_PARTS + q],
            or_sem.at[OUT_PARTS + q],
        )
        e.start()
        last.append(e)

    lead = part // (2 * si)
    lax.fori_loop(0, lead, reduce_grad1, 0)
    send_quarter(0)
    sums_of[3].step2()
    sums_of[2].ready4()
    sums_of[2].step4()
    lax.fori_loop(lead, nq * lead, reduce_grad1, 0)
    r.rgt[...] = jnp.transpose(r.rg1[...])
    for n0 in range(0, ci, 256):
        pack_rows(1, REDUCE, n0 // LANES, dot(r.rgt[...], r.x[:, n0 : n0 + 256]))
    sums_of[4].step1()
    send_quarter(1)
    sums_of[4].ready2()
    sums_of[4].step2()
    for q in range(2, nq):
        send_quarter(q)
    sums_of[5].ready4()
    sums_of[5].step4()
    sums_of[2].ready5()
    sums_of[2].step5()
    sums_of[3].ready3()
    sums_of[3].step3()
    sums_of[4].ready3()
    sums_of[4].step3()
    sums_of[2].ready6()
    sums_of[2].step6()
    sums_of[3].ready4()
    sums_of[3].step4()
    sums_of[4].ready4()
    sums_of[4].step4()
    for e in out_ex + last:
        e.wait()
    for sums in sums_of.values():
        sums.finish()


class Weights:
    def __init__(self, values):
        (
            self.reduce, self.reducegain, self.reducebias,
            self.split, self.splitgain, self.splitbias,
            self.squeeze, self.squeezegain, self.squeezebias,
            self.excite, self.excitebias,
            self.expand, self.expandgain, self.expandbias,
        ) = values[:14]
        self.extra = values[14:]


def doubled(v):
    return jnp.concatenate([v, v], axis=-1).reshape(-1, LANES)


def per_device(mesh, images, cotangent, groups, *weights):
    first, second = Weights(weights[:17]), Weights(weights[17:])
    z = Sizes(mesh, images, first.reduce, first.expand, first.squeeze)

    def vectors(w):
        parts = (w.reducegain, w.reducebias, w.splitgain, w.splitbias, w.excitebias)
        parts += (w.expandgain, w.expandbias) + w.extra[1:] + (w.squeezegain, w.squeezebias)
        return [v if v.ndim == 2 else v.reshape(1, -1) for v in parts]

    def block(w):
        return dict(
            wrt=w.reduce.T,
            wst=jnp.transpose(w.split, (0, 1, 3, 4, 2)).reshape(TAPS, 2, z.mids, z.grp),
            sq=w.squeeze,
            ext=jnp.transpose(w.excite, (1, 2, 0)),
            we=w.expand,
        )

    inputs = dict(
        images=images.reshape(-1, z.cis),
        cot=cotangent.reshape(-1, z.cos),
        groups=groups,
        vec=vectors(first) + vectors(second),
        wsh=first.extra[0],
        blk={1: block(first), 2: block(second)},
    )
    in_specs = jax.tree.map(lambda v: pl.BlockSpec(memory_space=pl.ANY), inputs)
    in_specs.update(groups=pl.BlockSpec(memory_space=pltpu.SMEM))
    outs = dict(
        out=jax.ShapeDtypeStruct((z.nc * z.no, z.cos), BF16),
        gx=jax.ShapeDtypeStruct((z.nc * z.ni, z.cis), BF16),
        sto=jax.ShapeDtypeStruct((NSTO, LANES), F32),
        res={n: jax.ShapeDtypeStruct((rows, LANES), BF16) for n, rows in z.rows.items()},
    )
    out_specs = jax.tree.map(lambda v: pl.BlockSpec(memory_space=pl.ANY), outs)
    out_specs.update(sto=pl.BlockSpec(memory_space=pltpu.VMEM))
    scratch = scratch_tree(z, vectors(first) + vectors(second))
    tree = jax.tree.structure((inputs, outs, scratch))
    results = pl.pallas_call(
        functools.partial(mega_kernel, z, tree),
        out_shape=jax.tree.leaves(outs),
        in_specs=jax.tree.leaves(in_specs),
        out_specs=jax.tree.leaves(out_specs),
        scratch_shapes=jax.tree.leaves(scratch),
        compiler_params=pltpu.CompilerParams(
            collective_id=0, has_side_effects=True, vmem_limit_bytes=63 << 20
        ),
        name="two_blocks",
    )(*jax.tree.leaves(inputs))
    return unpack(z, jax.tree.unflatten(jax.tree.structure(outs), results))


def unpack_kernel(z, plan, tree, *refs):
    given, (out_image, gx, *outs) = jax.tree.unflatten(tree, refs)
    given = space(given)
    out_in, gx_in, sto, res = given.out, given.gx, given.sto, given.res
    c = lax.axis_index(CHAN)
    out_image[...] = out_in[...].astype(F32)
    gx[...] = gx_in[...].astype(F32)

    def mid_share(row):
        v = sto[pl.ds(row + lax.div(c, 2), 1), :]
        return jnp.where(lax.rem(c, 2) == 0, v[:, : z.mids], v[:, z.mids :])

    @pl.when(pl.program_id(0) == 0)
    def _():
        for (kind, k, name), o in zip(plan, outs):
            if kind == MATRIX:
                group, at = z.lay[(k, name)]
                rows = o.shape[0]
                for t in range(o.shape[1] // LANES):
                    o[:, t * LANES : (t + 1) * LANES] = res[group][
                        at + t * rows : at + (t + 1) * rows, :
                    ].astype(F32)
                continue
            row = name
            if kind == MID_VECTOR:
                o[...] = mid_share(row)
            elif kind == PAIR_VECTOR:
                o[0:1, :] = mid_share(row)
                o[1:2, :] = mid_share(row + z.mid // LANES)
            elif kind == ATT_VECTOR:
                o[...] = sto[row : row + 1, :]
            else:
                n = z.cos // LANES
                for t in range(n):
                    o[:, t * LANES : (t + 1) * LANES] = sto[pl.ds(row + c * n + t, 1), :]


def unpack(z, results):
    plan = []
    for k in (1, 2):
        v = STO_ROWS[k]
        plan += [
            (MATRIX, k, REDUCE), (MID_VECTOR, k, v.rg), (MID_VECTOR, k, v.rb),
            (MATRIX, k, SPLIT), (PAIR_VECTOR, k, v.sg), (PAIR_VECTOR, k, v.sb),
            (MATRIX, k, SQUEEZE), (ATT_VECTOR, k, v.qg), (ATT_VECTOR, k, v.qb),
            (MATRIX, k, EXCITE), (PAIR_VECTOR, k, v.xb),
            (MATRIX, k, EXPAND), (OUT_VECTOR, k, v.eg), (OUT_VECTOR, k, v.eb),
        ]
        if k == 1:
            plan += [(MATRIX, k, SHORTCUT), (OUT_VECTOR, k, v.hg), (OUT_VECTOR, k, v.eb)]

    def shape_of(kind, k, name):
        if kind == MATRIX:
            return (
                (z.mids, z.ci if k == 1 else z.co),
                (2 * TAPS * z.mids, LANES),
                (z.mids, z.att),
                (2 * z.mids, z.att),
                (z.mid, z.cos),
                (z.ci, z.cos),
            )[name]
        return (None, (1, z.mids), (2, z.mids), (1, z.att), (1, z.cos))[kind]

    shapes = [shape_of(*entry) for entry in plan]
    steps = 4
    whole = lambda shape: pl.BlockSpec(shape, lambda i: (0, 0))
    slab = lambda v: pl.BlockSpec((v.shape[0] // steps, v.shape[1]), lambda i: (i, 0))
    in_specs = {n: slab(v) if n in ("out", "gx") else jax.tree.map(lambda a: whole(a.shape), v)
                for n, v in results.items()}
    images = [results["out"], results["gx"]]
    outs = [jax.ShapeDtypeStruct(v.shape, F32) for v in images]
    outs += [jax.ShapeDtypeStruct(s, F32) for s in shapes]
    flat = pl.pallas_call(
        functools.partial(unpack_kernel, z, plan, jax.tree.structure((results, outs))),
        grid=(steps,),
        out_shape=outs,
        in_specs=jax.tree.leaves(in_specs),
        out_specs=[slab(v) for v in images] + [whole(s) for s in shapes],
        compiler_params=pltpu.CompilerParams(vmem_limit_bytes=62 << 20),
        name="unpack",
    )(*jax.tree.leaves(results))
    final = [
        flat[0].reshape(z.nc * z.b, z.so, z.so, z.cos),
        flat[1].reshape(z.nc * z.b, z.si, z.si, z.cis),
    ]
    for (kind, _, name), v in zip(plan, flat[2:]):
        if (kind, name) == (MATRIX, REDUCE):
            v = v.T
        elif (kind, name) == (MATRIX, SPLIT):
            v = jnp.transpose(v.reshape(3, 3, 2, z.mids, z.grp), (0, 1, 4, 2, 3))
        elif (kind, name) == (MATRIX, EXCITE):
            v = jnp.transpose(v.reshape(2, z.mids, z.att), (2, 0, 1))
        elif kind in (MID_VECTOR, ATT_VECTOR, OUT_VECTOR):
            v = v.reshape(-1)
        final.append(v)
    return tuple(final)


def specs():
    block = [
        P(None, CHAN), P(CHAN), P(CHAN),
        P(None, None, None, None, CHAN), P(None, CHAN), P(None, CHAN),
        P(CHAN, None), P(), P(), P(None, None, CHAN), P(None, CHAN),
        P(None, CHAN), P(CHAN), P(CHAN),
    ]
    short = [P(None, CHAN), P(CHAN), P(CHAN)]
    return block + short + block


def solution(mesh):
    image = P(DP, None, None, CHAN)
    return jax.shard_map(
        functools.partial(per_device, mesh),
        mesh=mesh,
        in_specs=tuple([image, image, P(DP)] + specs()),
        out_specs=tuple([image, image] + specs()),
        check_vma=False,
    )
```

```python
import functools
from types import SimpleNamespace

import jax
import jax.numpy as jnp
from jax import lax
from jax.experimental import pallas as pl
from jax.experimental.pallas import tpu as pltpu
from jax.sharding import PartitionSpec as P

EPSILON = 1e-05
F32, BF16 = jnp.float32, jnp.bfloat16
HIGHEST = lax.Precision.HIGHEST
MESH = pl.DeviceIdType.MESH
LANES = 128
TAPS = 9
DP, CHAN = "dp", "chan"
REDUCE, SPLIT, SQUEEZE, EXCITE, EXPAND, SHORTCUT = range(6)
MATRIX, MID_VECTOR, PAIR_VECTOR, ATT_VECTOR, OUT_VECTOR = range(5)
SYNC_ROWS = (8, 8, 8, 32, 8, 8, 8, 16, 16, 16, 8, 24, 16, 8)

NT = (((1,), (1,)), ((), ()))
NN = (((1,), (0,)), ((), ()))
TN = (((0,), (0,)), ((), ()))


def dot(a, b, dims=NN):
    return lax.dot_general(a, b, dims, preferred_element_type=F32)


def dot_exact(a, b, dims=NN):
    return lax.dot_general(
        a.astype(F32), b.astype(F32), dims, precision=HIGHEST, preferred_element_type=F32
    )


def sigmoid(v):
    return 0.5 * jnp.tanh(0.5 * v) + 0.5


def silu(v):
    return v * sigmoid(v)


def silu_slope(v):
    q = sigmoid(v)
    return q * (1.0 + v * (1.0 - q))


def tiled(v, width):
    return jnp.concatenate([v] * (width // LANES), axis=1) if width > LANES else v


def sum8(v):
    return jnp.sum(v.reshape(v.shape[0] // 8, 8, v.shape[1]), axis=0)


def fold(v):
    return jnp.sum(v, axis=0, keepdims=True)


def span(start, size):
    if isinstance(start, int):
        return pl.ds(start, size)
    return pl.ds(pl.multiple_of(start, size), size)


def tile_of(rows):
    return next(t for t in (256, 128, 64, 32, 16) if rows % t == 0)


class Sizes:
    def __init__(self, mesh, images, reduce_w, expand_w, squeeze_w):
        self.nd, self.nc = mesh.shape[DP], mesh.shape[CHAN]
        self.near = min(self.nd, 8)
        self.far = self.nd // self.near
        self.b = images.shape[0] // self.nc
        self.si = images.shape[1]
        self.so = self.si // 2
        self.cis = images.shape[3]
        self.ci = self.cis * self.nc
        self.mids = reduce_w.shape[1]
        self.mid = self.mids * self.nc
        self.cos = expand_w.shape[1]
        self.co = self.cos * self.nc
        self.att = squeeze_w.shape[1]
        self.po = self.so * self.so
        self.pi = self.si * self.si
        self.no = self.b * self.po
        self.ni = self.b * self.pi
        self.grp = self.mid // 2
        self.kk = TAPS * self.grp
        cin = {1: self.ci, 2: self.co}
        self.piece_rows = {
            (k, name): rows
            for k in (1, 2)
            for name, rows in (
                (REDUCE, cin[k] // LANES * self.mids),
                (SPLIT, 2 * TAPS * self.mids),
                (SQUEEZE, self.mids),
                (EXCITE, 2 * self.mids),
                (EXPAND, self.cos // LANES * self.mid),
                (SHORTCUT, self.cos // LANES * self.ci),
            )
        }
        self.lay, self.rows = {}, {}
        for group, members in GROUPS.items():
            at = 0
            for key in members:
                self.lay[key] = (group, at)
                at += self.piece_rows[key]
            self.rows[group] = -(-at // (16 * self.near)) * 16 * self.near


GROUPS = {
    0: ((2, EXPAND), (2, EXCITE)),
    1: ((2, SPLIT), (2, SQUEEZE)),
    2: ((1, EXPAND), (1, EXCITE), (1, SHORTCUT)),
    3: ((1, SPLIT), (1, SQUEEZE)),
    4: ((1, REDUCE),),
    5: ((2, REDUCE),),
}
SPLIT_GROUPS = (1, 2, 3, 5)
VEC_ROWS = {
    1: SimpleNamespace(rg=0, rb=1, sg=2, sb=4, xb=6, eg=8, eb=10, hg=12, hb=14, qg=16, qb=17),
    2: SimpleNamespace(rg=18, rb=19, sg=20, sb=22, xb=24, eg=26, eb=28, qg=30, qb=31),
}
NVEC = 32
STO_ROWS = {
    2: SimpleNamespace(eb=0, eg=8, qb=16, qg=17, sb=18, sg=22, rb=26, rg=28, xb=30),
    1: SimpleNamespace(eb=34, eg=42, qb=50, qg=51, sb=52, sg=56, rb=60, rg=62, xb=64, hg=68),
}
NSTO = 80
QUARTERS = 4
KINDS = 9
OUT_PARTS = 4


def space(tree):
    if not isinstance(tree, dict):
        return tree
    inner = {k: space(v) for k, v in tree.items()}
    return SimpleNamespace(**inner) if all(isinstance(k, str) for k in inner) else inner


def scratch_tree(z, vec):
    def f32(*shape):
        return pltpu.VMEM(shape, F32)

    def bf16(*shape):
        return pltpu.VMEM(shape, BF16)

    def sem(*shape):
        return pltpu.SemaphoreType.DMA(shape)

    ns = z.nd * z.nc // 2
    return dict(
        x=bf16(z.ni, z.ci),
        cot=bf16(z.no, z.co),
        wsh=bf16(z.ci, z.co),
        vv=f32(z.nc, NVEC, LANES),
        vmine=f32(NVEC, LANES),
        vraw=[f32(*v.shape) for v in vec],
        vsem=sem(len(vec)),
        mo=f32(z.no, LANES),
        mi=bf16(z.ni, LANES),
        red1=f32(z.mid // LANES, z.b * z.so, 2, z.si, LANES),
        u1=f32(z.mid // LANES, z.b * z.so, 2, z.si, LANES),
        pool=bf16(z.no, z.ci),
        short=f32(z.no, z.co),
        h=bf16(z.no, z.co),
        red2=f32(z.no, z.mid),
        u2=f32(z.no, z.mid),
        g=f32(z.no, z.co),
        eg=bf16(z.no, z.co),
        shg=bf16(z.no, z.co),
        mg=f32(z.no, z.mid),
        su=f32(z.no, 2 * z.mid),
        sgb=bf16(z.no, 2 * z.mid),
        sgt=bf16(2 * z.mid, z.no),
        mixt=bf16(z.mid, z.no),
        dcol=f32(z.po + 2 * z.so, z.kk),
        rg1=bf16(z.ni, z.mid),
        rgt=bf16(z.mid, z.ni),
        pg=bf16(z.no, z.ci),
        ags=f32(8, 2 * z.mid),
        met=f32(z.nc, KINDS * z.b + 6, LANES),
        all=f32(z.nd, KINDS, 8, LANES),
        mgr=f32(8, z.mid),
        blk={
            k: dict(
                wrt=bf16(z.mid, z.ci if k == 1 else z.co),
                wst=bf16(TAPS, 2, z.mid, z.grp),
                sq=bf16(z.mid, z.att),
                ext=bf16(2, z.mid, z.att),
                we=bf16(z.mid, z.co),
                im=bf16(2, z.no + 2 * z.so, z.kk),
                sp=f32(z.no, 2 * z.mid),
                sa=f32(z.no, 2 * z.mid),
                mix=bf16(z.no, z.mid),
                exp=f32(z.no, z.co),
                att=f32(8, 2 * z.mid),
                pm=f32(8, z.mid),
                own=f32(KINDS * z.b + 6, LANES),
                group=f32(KINDS, 8, LANES),
                ms=sem(3),
                mr=sem(3),
            )
            for k in (1, 2)
        },
        group={
            n: dict(
                pk=bf16(z.nc // 2, 2, rows, LANES),
                r1=bf16(z.nc // 2, rows, LANES),
                r2=bf16(rows, LANES),
                r3=bf16(z.near, rows // z.near, LANES),
                r4=bf16(z.far, rows // z.near, LANES),
                q1=sem(2),
                q2=sem(2),
                q3s=sem(z.near),
                q3r=sem(z.near),
                q4s=sem(z.near),
                q4r=sem(z.near),
                q5s=sem(z.far),
                q5r=sem(z.far),
                ry=bf16(rows // 2 if n in SPLIT_GROUPS else 16, LANES),
                q6=sem(4),
            )
            for n, rows in z.rows.items()
        },
        sync={
            k: dict(sa=f32(rows, LANES), sb=f32(rows, LANES), st=f32(rows, LANES))
            for k, rows in enumerate(SYNC_ROWS)
        },
        slots={p: f32(ns, max(SYNC_ROWS), LANES) for p in range(2)},
        gather_send=sem(13, z.nc),
        gather_recv=sem(13, z.nc),
        image_send=sem(QUARTERS, z.nc),
        image_recv=sem(QUARTERS, z.nc),
        out_send=sem(OUT_PARTS + QUARTERS, z.nc),
        out_got=sem(OUT_PARTS + QUARTERS, z.nc),
        s0s=sem(1),
        s0r=sem(2),
        s1s=sem(1),
        s1r=sem(2),
    )


def mega_kernel(z, tree, *refs):
    given, made, r = (space(t) for t in jax.tree.unflatten(tree, refs))
    nc, nd = z.nc, z.nd
    b, so, si, po, pi_, no, ni = z.b, z.so, z.si, z.po, z.pi, z.no, z.ni
    mid, co, ci, att, grp, kk = z.mid, z.co, z.ci, z.att, z.grp, z.kk
    d, c = lax.axis_index(DP), lax.axis_index(CHAN)
    ns = nd * nc // 2
    me = d * (nc // 2) + lax.div(c, 2)
    odd = lax.rem(c, 2)

    def chan_at(i):
        return lax.rem(c + i, nc)

    def place(s):
        return (lax.div(s, nc // 2), lax.rem(s, nc // 2) * 2 + odd)

    partner = (d, c + 1 - 2 * odd)
    far_first = []
    if ns <= 16:
        for n in range(ns - 1):
            far_first.append(place(lax.rem(me + (n + ns // 3) % (ns - 1) + 1, ns)))

    barrier = pltpu.get_barrier_semaphore()
    for i in range(1, nc):
        pl.semaphore_signal(barrier, inc=1, device_id=(d, chan_at(i)), device_id_type=MESH)

    def greet(j, _):
        pl.semaphore_signal(
            barrier, inc=1, device_id=place(lax.rem(me + j, ns)), device_id_type=MESH
        )
        return 0

    lax.fori_loop(1, ns, greet, 0)
    pl.semaphore_wait(barrier, nc - 1 + ns - 1)

    class Exchange:
        def __init__(self, src, dst, send, recv):
            self.src, self.dst, self.send, self.recv = src, dst, send, recv

        def copy(self, i):
            to = chan_at(i)
            return pltpu.make_async_remote_copy(
                src_ref=self.src(to), dst_ref=self.dst(c), send_sem=self.send.at[i],
                recv_sem=self.recv.at[i], device_id=(d, to), device_id_type=MESH,
            )

        def local(self):
            return pltpu.make_async_copy(self.src(c), self.dst(c), self.recv.at[0])

        def start(self):
            for i in (2, 1, 3) if nc == 4 else range(1, nc):
                self.copy(i).start()
            self.local().start()

        def wait(self):
            self.local().wait()
            for i in range(1, nc):
                frm = lax.rem(c - i + nc, nc)
                pltpu.make_async_remote_copy(
                    src_ref=self.src(c), dst_ref=self.dst(frm), send_sem=self.send.at[i],
                    recv_sem=self.recv.at[i], device_id=(d, frm), device_id_type=MESH,
                ).wait_recv()
                self.copy(i).wait_send()

    class Relay:
        def __init__(self, src, dst, send, recv):
            self.src, self.dst, self.send, self.recv = src, dst, send, recv
            self.far = chan_at(2)

        def copy(self, n, src, which, to):
            return pltpu.make_async_remote_copy(
                src_ref=src, dst_ref=self.dst(which), send_sem=self.send.at[n],
                recv_sem=self.recv.at[n], device_id=to, device_id_type=MESH,
            )

        def across(self, which):
            return self.copy(1, self.src(c), which, (d, self.far))

        def beside(self, which):
            return self.copy(2, self.src(c), which, partner)

        def onward(self, which):
            return self.copy(3, self.dst(self.far), which, partner)

        def local(self):
            return pltpu.make_async_copy(self.src(c), self.dst(c), self.recv.at[0])

        def start(self):
            self.across(c).start()
            self.beside(c).start()
            self.local().start()

        def forward(self):
            self.across(self.far).wait_recv()
            self.onward(self.far).start()

        def wait(self):
            self.local().wait()
            self.across(c).wait_send()
            self.beside(c).wait_send()
            self.onward(self.far).wait_send()
            self.beside(partner[1]).wait_recv()
            self.onward(lax.rem(partner[1] + 2, nc)).wait_recv()

    gs_sem, gr_sem = r.gather_send, r.gather_recv
    xs_sem, xr_sem = r.image_send, r.image_recv
    os_sem, or_sem = r.out_send, r.out_got

    def lanes_of(ref, width):
        return lambda s: ref.at[:, pl.ds(pl.multiple_of(s * width, LANES), width)]

    def rows_of(ref, size):
        return lambda s: ref.at[pl.ds(pl.multiple_of(s * size, size), size), :]

    def mids_of(ref, size):
        return lambda s: ref.at[:, pl.ds(pl.multiple_of(s * size, size), size), :]

    def taps_of(ref, size):
        return lambda s: ref.at[:, :, pl.ds(pl.multiple_of(s * size, size), size), :]

    whole = lambda ref: (lambda s: ref)
    ms = z.mids
    sem_rows = iter(range(13))

    def gathered(src, dst, kind=Relay):
        e = next(sem_rows)
        return kind(src, dst, gs_sem.at[e], gr_sem.at[e])

    ex = SimpleNamespace(
        vec=gathered(whole(r.vmine), lambda s: r.vv.at[s], Exchange),
        wsh=gathered(whole(given.wsh), lanes_of(r.wsh, z.cos)),
        cot=gathered(rows_of(given.cot, no), lanes_of(r.cot, z.cos), Exchange),
        blk={
            k: SimpleNamespace(
                wrt=gathered(whole(given.blk[k].wrt), rows_of(r.blk[k].wrt, ms)),
                wst=gathered(whole(given.blk[k].wst), taps_of(r.blk[k].wst, ms)),
                sq=gathered(whole(given.blk[k].sq), rows_of(r.blk[k].sq, ms)),
                ext=gathered(whole(given.blk[k].ext), mids_of(r.blk[k].ext, ms)),
                we=gathered(whole(given.blk[k].we), lanes_of(r.blk[k].we, z.cos)),
            )
            for k in (1, 2)
        },
        x=[],
    )
    nq = QUARTERS
    part = ni // nq
    for q in range(nq):
        ex.x.append(Exchange(
            lambda s, q=q: given.images.at[pl.ds(pl.multiple_of(s * ni + q * part, part), part), :],
            lambda s, q=q: r.x.at[
                pl.ds(q * part, part), pl.ds(pl.multiple_of(s * z.cis, LANES), z.cis)
            ],
            xs_sem.at[q],
            xr_sem.at[q],
        ))
    first_w, second_w = ex.blk[1], ex.blk[2]
    first_w.wrt.start()
    raw = [
        pltpu.make_async_copy(v, to, r.vsem.at[n]) for n, (v, to) in enumerate(zip(given.vec, r.vraw))
    ]
    for copy in raw:
        copy.start()
    ex.x[0].start()
    for q in range(1, nq):
        ex.x[q].start()
    row = 0
    for copy, v in zip(raw, r.vraw):
        copy.wait()
        rows, width = v.shape
        for k in range(rows):
            one = v[k : k + 1, :]
            if width < LANES:
                one = jnp.concatenate([one, one], axis=1)
            for t in range(one.shape[1] // LANES):
                r.vmine[row : row + 1, :] = one[:, t * LANES : (t + 1) * LANES]
                row += 1
    ex.vec.start()

    ss0, rs0, ss1, rs1 = r.s0s, r.s0r, r.s1s, r.s1r

    def put(k, row, v):
        for t in range(v.shape[1] // LANES):
            r.sync[k].sa[row + t : row + t + 1, :] = v[:, t * LANES : (t + 1) * LANES]

    def allreduce(k, used, meanwhile=None):
        sa, sb, st = r.sync[k].sa, r.sync[k].sb, r.sync[k].st
        rows = SYNC_ROWS[k]
        sc = r.slots[k % 2].at[:, :rows, :]
        if used < rows:
            sa[used:rows, :] = jnp.zeros((rows - used, LANES), F32)
        first = pltpu.make_async_remote_copy(
            src_ref=sa, dst_ref=sb, send_sem=ss0.at[0], recv_sem=rs0.at[k % 2],
            device_id=partner, device_id_type=MESH,
        )
        first.start()
        first.wait()
        pair = sa[...] + sb[...]
        sc[me] = pair

        def send(to):
            pltpu.make_async_remote_copy(
                src_ref=sc.at[me], dst_ref=sc.at[me], send_sem=ss1.at[0],
                recv_sem=rs1.at[k % 2], device_id=to, device_id_type=MESH,
            ).start()

        if ns <= 16:
            for to in far_first:
                send(to)
        else:

            def send_one(j, _):
                send(place(lax.rem(me + j, ns)))
                return 0

            lax.fori_loop(1, ns, send_one, 0)
        if meanwhile is not None:
            meanwhile()
        others = sc.at[pl.ds(0, ns - 1)]
        pltpu.make_async_remote_copy(
            src_ref=others, dst_ref=others, send_sem=ss1.at[0], recv_sem=rs1.at[k % 2],
            device_id=partner, device_id_type=MESH,
        ).wait()
        if ns <= 16:
            total = sc[0]
            for s in range(1, ns):
                total = total + sc[s]
        else:
            total = lax.fori_loop(1, ns, lambda s, t: t + sc[s], sc[0])
        st[...] = total

    def total(k, row, width):
        st = r.sync[k].st
        return jnp.concatenate(
            [st[row + t : row + t + 1, :] for t in range(width // LANES)], axis=1
        )

    sto = made.sto

    def keep(row, v):
        for t in range(v.shape[1] // LANES):
            sto[row + t : row + t + 1, :] = v[:, t * LANES : (t + 1) * LANES]

    half = lambda rows: lax.broadcasted_iota(jnp.int32, (rows, LANES), 0)
    groups = given.groups
    sides = [(so - 4 + 2 * groups[c * b + k]) for k in range(b)]
    areas = [(s * s).astype(F32) for s in sides]
    for k in range(b):
        def fill_out(t, _, k=k):
            p = half(2 * so) + t * (2 * so)
            ok = (lax.div(p, so) < sides[k]) & (lax.rem(p, so) < sides[k])
            r.mo[span(k * po + t * (2 * so), 2 * so), :] = jnp.where(ok, 1.0, 0.0)
            return 0

        lax.fori_loop(0, po // (2 * so), fill_out, 0)

        def fill_in(t, _, k=k):
            p = half(2 * si) + t * (2 * si)
            ok = (lax.div(p, si) < 2 * sides[k]) & (lax.rem(p, si) < 2 * sides[k])
            r.mi[span(k * pi_ + t * (2 * si), 2 * si), :] = jnp.where(ok, 1.0, 0.0).astype(BF16)
            return 0

        lax.fori_loop(0, pi_ // (2 * si), fill_in, 0)
    row8 = lax.broadcasted_iota(jnp.int32, (8, LANES), 0)
    live8 = jnp.where(row8 < b, 1.0, 0.0)
    inv_area = jnp.zeros((8, LANES), F32)
    for k in range(b):
        inv_area = jnp.where(row8 == k, 1.0 / jnp.full((8, LANES), areas[k], F32), inv_area)
    for ref in (r.blk[1].pm, r.blk[2].pm, r.ags):
        ref[...] = jnp.zeros_like(ref)

    pool_rows = part // 4

    def pool_matrix(out_axis):
        shape = (pool_rows, part) if out_axis == 0 else (part, pool_rows)
        o = lax.broadcasted_iota(jnp.int32, shape, out_axis)
        p = lax.broadcasted_iota(jnp.int32, shape, 1 - out_axis)
        row, col = lax.div(p, si), lax.rem(p, si)
        hit = (lax.div(row, 2) * so + lax.div(col, 2)) == o
        return jnp.where(hit, 0.25, 0.0).astype(BF16)

    low_half = lax.broadcasted_iota(jnp.int32, (1, LANES), 1) < z.mids
    vv = r.vv

    def v_mid(row):
        return jnp.concatenate(
            [
                jnp.where(low_half, vv[s, row : row + 1, :], vv[s + 1, row : row + 1, :])
                for s in range(0, nc, 2)
            ],
            axis=1,
        )

    def v_split(row):
        return jnp.concatenate([v_mid(row), v_mid(row + 1)], axis=1)

    def v_co(row):
        return jnp.concatenate(
            [
                vv[s, row + t : row + t + 1, :]
                for s in range(nc)
                for t in range(z.cos // LANES)
            ],
            axis=1,
        )

    def norm(k, row1, row2, width, inv_n, gain, bias):
        n = tiled(inv_n, width)
        mean = total(k, row1, width) * n
        inv = lax.rsqrt(total(k, row2, width) * n - mean * mean + EPSILON)
        scale = gain * inv
        return SimpleNamespace(mean=mean, inv=inv, gs=scale, sh=bias - mean * scale)

    def norm_grad(k, rowu, rowv, width, inv_n, nm):
        return norm_grad_of(total(k, rowu, width), total(k, rowv, width), width, inv_n, nm)

    def norm_grad_of(su, sv, width, inv_n, nm):
        n = tiled(inv_n, width)
        sux = nm.inv * (sv - nm.mean * su)
        t = sux * n
        return (
            su,
            sux,
            nm.gs * (su * n - nm.mean * nm.inv * t),
            nm.gs * nm.inv * t,
        )

    def loop(n, tile, body, init):
        def step(i, carry):
            return body(pl.multiple_of(i * tile, tile), carry)

        return lax.fori_loop(0, n // tile, step, init, unroll=2 if n // tile % 2 == 0 else 1)

    def zero8(width):
        return jnp.zeros((8, width), F32)

    def moments(ref, rows, width, tile):
        def body(at, carry):
            s1, s2 = carry
            v = ref[pl.ds(at, tile), :]
            mv = v * tiled(r.mo[pl.ds(at, tile), :], width)
            return s1 + sum8(mv), s2 + sum8(mv * v)

        s1, s2 = loop(rows, tile, body, (zero8(width), zero8(width)))
        return fold(s1), fold(s2)

    red1 = r.red1

    def row_pair(ref, i):
        return jnp.concatenate(
            [ref[t, pl.ds(i, 1)].reshape(2 * si, LANES) for t in range(mid // LANES)], axis=1
        )

    def phase_of(t, lead, p, q):
        return red1[t, lead, p, pl.ds(q, so, stride=2), :].reshape(4 * so, LANES)

    pool_m = pool_matrix(0)
    first_w.wrt.forward()
    first_w.wrt.wait()
    r1, r2 = zero8(mid), zero8(mid)
    for q in range(nq):
        ex.x[q].wait()
        xv = r.x[q * part : (q + 1) * part, :]
        lead = part // (2 * si)
        reduced = dot(xv, r.blk[1].wrt[...], NT)
        for t in range(mid // LANES):
            red1[t, q * lead : (q + 1) * lead] = reduced[:, t * LANES : (t + 1) * LANES].reshape(
                lead, 2, si, LANES
            )

        def red_sums(i, carry, q=q, lead=lead):
            s1, s2 = carry
            v = row_pair(red1, q * lead + i)
            m = r.mi[span((q * lead + i) * 2 * si, 2 * si), :].astype(F32)
            mv = v * tiled(m, mid)
            return s1 + sum8(mv), s2 + sum8(mv * v)

        r1, r2 = lax.fori_loop(0, lead, red_sums, (r1, r2))
    first_w.wst.start()
    put(0, 0, fold(r1))
    put(0, mid // LANES, fold(r2))
    at = 2 * mid // LANES
    local_area = areas[0]
    for k in range(1, b):
        local_area = local_area + areas[k]
    put(0, at, jnp.full((1, LANES), local_area, F32))

    def pooling():
        for q in range(nq):
            r.pool[q * pool_rows : (q + 1) * pool_rows, :] = dot(
                pool_m, r.x[q * part : (q + 1) * part, :]
            ).astype(BF16)

    allreduce(0, at + 1, pooling)
    ex.vec.wait()
    count = total(0, at, LANES)
    inv_out = 1.0 / count
    inv_in = 0.25 * inv_out
    vr1, vr2 = VEC_ROWS[1], VEC_ROWS[2]
    nred1 = norm(0, 0, mid // LANES, mid, inv_in, v_mid(vr1.rg), v_mid(vr1.rb))
    lane16 = lax.rem(lax.broadcasted_iota(jnp.int32, (4 * so, mid), 0), so)
    not_first = lane16 > 0
    not_last = lane16 < so - 1

    def im_put(im, at, w, di, dj, shift):
        tap = di * 3 + dj
        low = w.astype(BF16)
        for g in range(2):
            im[g, pl.ds(pl.multiple_of(at + so + shift * so, so), 4 * so), tap * grp : (tap + 1) * grp] = (
                low[:, g * grp : (g + 1) * grp]
            )

    def im_zero(im, di, last):
        for k in range(b):
            row = so + k * po + (po - so if last else 0)
            for g in range(2):
                im[g, row : row + so, di * 3 * grp : (di + 1) * 3 * grp] = jnp.zeros(
                    (so, 3 * grp), BF16
                )

    im1 = r.blk[1].im

    def build1(i, _):
        at = pl.multiple_of(i * 4 * so, 4 * so)
        m = tiled(r.mo[pl.ds(at, 4 * so), :], mid)
        for p in range(2):
            for q in range(2):
                v = jnp.concatenate(
                    [phase_of(t, pl.ds(i * 4, 4), p, q) for t in range(mid // LANES)], axis=1
                )
                w = silu(v * nred1.gs + nred1.sh) * m
                for dj in ((1,) if q == 0 else (2, 0)):
                    wj = w
                    if dj == 0:
                        wj = jnp.where(not_first, pltpu.roll(w, 1, 0), 0.0)
                    for di in ((1,) if p == 0 else (2, 0)):
                        im_put(im1, at, wj, di, dj, 1 if di == 0 else 0)
        return 0

    for e in (first_w.sq, first_w.ext, first_w.we, ex.wsh):
        e.start()
    lax.fori_loop(0, no // (4 * so), build1, 0)
    first_w.wst.forward()
    im_zero(im1, 0, False)

    def split_weights(k, g):
        return jnp.concatenate([r.blk[k].wst[t, g] for t in range(TAPS)], axis=1)

    def split_conv(k):
        ex.blk[k].wst.wait()
        for g in range(2):
            r.blk[k].sp[:, g * mid : (g + 1) * mid] = dot(
                r.blk[k].im[g, so : so + no, :], split_weights(k, g), NT
            )
        return moments(r.blk[k].sp, no, 2 * mid, 32)

    class Meeting:
        def __init__(self, k):
            blk = r.blk[k]
            self.own, self.group, self.ms, self.mr = blk.own, blk.group, blk.ms, blk.mr

        def near(self, to, src):
            return pltpu.make_async_remote_copy(
                src_ref=self.own, dst_ref=r.met.at[src], send_sem=self.ms.at[0],
                recv_sem=self.mr.at[0], device_id=(d, to), device_id_type=MESH,
            )

        def far(self, to):
            return pltpu.make_async_remote_copy(
                src_ref=self.group, dst_ref=r.all.at[d], send_sem=self.ms.at[1],
                recv_sem=self.mr.at[1], device_id=(to, c), device_id_type=MESH,
            )

        def wait(self, ref, n):
            some = ref.at[pl.ds(0, n)]
            pltpu.make_async_remote_copy(
                src_ref=some, dst_ref=some, send_sem=self.ms.at[0 if n == nc - 1 else 1],
                recv_sem=self.mr.at[0 if n == nc - 1 else 1], device_id=partner,
                device_id_type=MESH,
            ).wait()

        def start(self):
            for n in range(1, nc):
                self.near(chan_at(n), c).start()

        def gather(self):
            self.wait(r.met, nc - 1)
            r.met[c] = self.own[...]
            for kind in range(KINDS):
                for s in range(nc):
                    self.group[kind, s * b : (s + 1) * b, :] = r.met[
                        s, kind * b : (kind + 1) * b, :
                    ]

        def send(self):
            def step(j, _):
                self.far(lax.rem(d + j, nd)).start()
                return 0

            lax.fori_loop(1, nd, step, 0)

        def finish(self):
            self.wait(r.all, nd - 1)
            r.all[d] = self.group[...]

    meet = {k: Meeting(k) for k in (1, 2)}

    def attention_forward(k, vr, sync, fills):
        s1, s2 = split_conv(k)
        put(sync, 0, s1)
        put(sync, 4, s2)
        allreduce(sync, 8, fills[0])
        nsplit = norm(sync, 0, 4, 2 * mid, inv_out, v_split(vr.sg), v_split(vr.sb))
        sp, sa, pm = r.blk[k].sp, r.blk[k].sa, r.blk[k].pm
        for img in range(b):
            def act(at, carry, img=img):
                s, ds, dv = carry
                rows = pl.ds(pl.multiple_of(at + img * po, 32), 32)
                raw = sp[rows, :]
                v = raw * nsplit.gs + nsplit.sh
                q = sigmoid(v)
                qm = q * tiled(r.mo[rows, :], 2 * mid)
                slope = qm * (1.0 + v * (1.0 - q))
                v = v * qm
                sa[rows, :] = v
                return s + sum8(v), ds + sum8(slope), dv + sum8(slope * raw)

            zero = zero8(2 * mid)
            s, ds, dv = (fold(v) for v in loop(po, 32, act, (zero, zero, zero)))
            own = r.blk[k].own
            for t in range(4):
                lanes = slice(t * LANES, (t + 1) * LANES)
                for kind, v in ((t, ds), (t + 4, dv)):
                    at = kind * b + img
                    own[at : at + 1, :] = v[:, lanes] * inv_area[img : img + 1, :]
            pm[img : img + 1, :] = (s[:, :mid] + s[:, mid:]) * tiled(inv_area[img : img + 1, :], mid)
        ex.blk[k].sq.wait()
        squeezed = dot_exact(pm[...], r.blk[k].sq[...])
        put(sync + 1, 0, fold(squeezed))
        put(sync + 1, 1, fold(squeezed * squeezed))
        put(sync + 1, 2, fold(pm[...]))
        allreduce(sync + 1, 4, fills[1])
        inv_images = jnp.full((1, LANES), 1.0 / (b * nc * nd), F32)
        natt = norm(
            sync + 1, 0, 1, att, inv_images, vv[0, vr.qg : vr.qg + 1, :],
            vv[0, vr.qb : vr.qb + 1, :],
        )
        xhat = (squeezed - natt.mean) * natt.inv
        centred = pm[...] - total(sync + 1, 2, mid) * tiled(inv_images, mid)
        r.blk[k].own[8 * b : 9 * b, :] = xhat[:b, :]
        meet[k].start()
        pre = squeezed * natt.gs + natt.sh
        excited = silu(pre) * live8
        ex.blk[k].ext.wait()
        halves = []
        for g in range(2):
            bias = v_mid(vr.xb + g)
            halves.append(dot_exact(excited, r.blk[k].ext[g], NT) + bias)
        top = jnp.maximum(halves[0], halves[1])
        e0, e1 = jnp.exp(halves[0] - top), jnp.exp(halves[1] - top)
        whole_sum = e0 + e1
        at_ref = r.blk[k].att
        at_ref[:, :mid] = e0 / whole_sum
        at_ref[:, mid:] = e1 / whole_sum
        for img in range(b):
            def mix(at, _, img=img):
                rows = pl.ds(pl.multiple_of(at + img * po, 32), 32)
                v = sa[rows, :] * at_ref[img : img + 1, :]
                r.blk[k].mix[rows, :] = (v[:, :mid] + v[:, mid:]).astype(BF16)
                return 0

            loop(po, 32, mix, 0)
        ex.blk[k].we.wait()
        for n0 in range(0, co, 256):
            r.blk[k].exp[:, n0 : n0 + 256] = dot(r.blk[k].mix[...], r.blk[k].we[:, n0 : n0 + 256])
        s1, s2 = moments(r.blk[k].exp, no, co, 16)
        put(sync + 2, 0, s1)
        put(sync + 2, co // LANES, s2)
        if k == 1:
            for n, v in enumerate(short_sums):
                put(sync + 2, (2 + n) * co // LANES, v)
        allreduce(sync + 2, (4 if k == 1 else 2) * co // LANES, fills[2])
        nexp = norm(sync + 2, 0, co // LANES, co, inv_out, v_co(vr.eg), v_co(vr.eb))
        return SimpleNamespace(nsplit=nsplit, natt=natt, xhat=xhat, pre=pre, excited=excited, nexp=nexp, centred=centred)

    short_sums = []

    def shortcut_forward():
        ex.wsh.wait()
        for n0 in range(0, co, 256):
            r.short[:, n0 : n0 + 256] = dot(r.pool[...], r.wsh[:, n0 : n0 + 256])
        short_sums.extend(moments(r.short, no, co, 16))

    def forward_first():
        for e in (first_w.sq, first_w.ext, first_w.we):
            e.forward()
        second_w.wrt.start()

    def between():
        ex.wsh.forward()
        second_w.wst.start()
        shortcut_forward()

    def forward_second():
        meet[1].gather()
        second_w.wrt.forward()
        for e in (second_w.sq, second_w.ext, second_w.we):
            e.start()

    f1 = attention_forward(1, vr1, 1, (forward_first, between, forward_second))
    nshort = norm(
        3, 2 * co // LANES, 3 * co // LANES, co, inv_out, v_co(vr1.hg), v_co(vr1.hb)
    )

    def summed1(rows):
        return (
            r.blk[1].exp[rows, :] * f1.nexp.gs
            + f1.nexp.sh
            + r.short[rows, :] * nshort.gs
            + nshort.sh
        )

    def hidden(at, _):
        rows = pl.ds(at, 16)
        r.h[rows, :] = (silu(summed1(rows)) * tiled(r.mo[rows, :], co)).astype(BF16)
        return 0

    loop(no, 16, hidden, 0)

    ex.blk[2].wrt.wait()
    r.red2[...] = dot(r.h[...], r.blk[2].wrt[...], NT)
    s1, s2 = moments(r.red2, no, mid, 64)
    put(4, 0, s1)
    put(4, 2, s2)

    def forward_rest():
        ex.cot.start()
        second_w.wst.forward()
        for e in (second_w.sq, second_w.ext, second_w.we):
            e.forward()

    allreduce(4, 4, forward_rest)
    nred2 = norm(4, 0, 2, mid, inv_out, v_mid(vr2.rg), v_mid(vr2.rb))
    im2 = r.blk[2].im

    def build2(i, _):
        at = pl.multiple_of(i * 4 * so, 4 * so)
        m = tiled(r.mo[pl.ds(at, 4 * so), :], mid)
        w = silu(r.red2[pl.ds(at, 4 * so), :] * nred2.gs + nred2.sh) * m
        for dj in range(3):
            wj = w
            if dj == 0:
                wj = jnp.where(not_first, pltpu.roll(w, 1, 0), 0.0)
            if dj == 2:
                wj = jnp.where(not_last, pltpu.roll(w, 4 * so - 1, 0), 0.0)
            for di in range(3):
                im_put(im2, at, wj, di, dj, 1 - di)
        return 0

    lax.fori_loop(0, no // (4 * so), build2, 0)
    im_zero(im2, 0, False)
    im_zero(im2, 2, True)
    f2 = attention_forward(2, vr2, 5, (None, None, meet[2].gather))
    meet[2].send()

    ex.cot.wait()

    def finish(at, carry):
        su, sv = carry
        rows = pl.ds(at, 16)
        m = tiled(r.mo[rows, :], co)
        v = r.blk[2].exp[rows, :]
        s = v * f2.nexp.gs + f2.nexp.sh + r.h[rows, :].astype(F32)
        q = sigmoid(s)
        u = r.cot[rows, :].astype(F32) * m * (q * (1.0 + s * (1.0 - q)))
        r.cot[rows, :] = (s * q * m).astype(BF16)
        r.g[rows, :] = u
        return su + sum8(u), sv + sum8(u * v)

    su, sv = loop(no, 16, finish, (zero8(co), zero8(co)))
    out_part = no // OUT_PARTS
    out_ex = [
        Exchange(
            lambda s, n=n: r.cot.at[
                pl.ds(n * out_part, out_part), pl.ds(pl.multiple_of(s * z.cos, LANES), z.cos)
            ],
            lambda s, n=n: made.out.at[
                pl.ds(pl.multiple_of(s * no + n * out_part, out_part), out_part), :
            ],
            os_sem.at[n],
            or_sem.at[n],
        )
        for n in range(OUT_PARTS)
    ]
    put(8, 0, fold(su))
    put(8, co // LANES, fold(sv))
    allreduce(8, 2 * co // LANES)
    out_ex[0].start()

    def pack_rows(k, name, skip, v):
        group, at = z.lay[(k, name)]
        at, share = at + skip * z.mids, z.mids
        for s in range(nc):
            for t in range(v.shape[1] // LANES):
                r.group[group].pk[s // 2, s % 2, at + t * share : at + (t + 1) * share, :] = v[
                    s * share : (s + 1) * share, t * LANES : (t + 1) * LANES
                ].astype(BF16)

    def pack_lanes(k, name, s, v):
        group, at = z.lay[(k, name)]
        rows = v.shape[0]
        for t in range(v.shape[1] // LANES):
            r.group[group].pk[s // 2, s % 2, at + t * rows : at + (t + 1) * rows, :] = v[
                :, t * LANES : (t + 1) * LANES
            ].astype(BF16)

    class Reduction:
        def __init__(self, group):
            own = r.group[group]
            self.pk, self.r1, self.r2, self.r3 = own.pk, own.r1, own.r2, own.r3
            self.rows = z.rows[group]
            self.piece = self.rows // z.near
            self.r4 = own.r4
            self.near, self.mine = lax.rem(d, z.near), lax.div(d, z.near)
            self.res = made.res[group]
            self.sems = [own.q1, own.q2, own.q3s, own.q3r, own.q4s, own.q4r, own.q5s, own.q5r]
            self.across = lax.div(c, 2)

        def piece_at(self, n):
            return pl.ds(pl.multiple_of(n * self.piece, 16), self.piece)

        def copy1(self):
            return pltpu.make_async_remote_copy(
                src_ref=self.pk.at[:, 1 - odd], dst_ref=self.r1, send_sem=self.sems[0].at[0],
                recv_sem=self.sems[0].at[1], device_id=partner, device_id_type=MESH,
            )

        def copy2(self):
            return pltpu.make_async_remote_copy(
                src_ref=self.pk.at[1 - self.across, odd], dst_ref=self.r2,
                send_sem=self.sems[1].at[0], recv_sem=self.sems[1].at[1],
                device_id=(d, chan_at(2)), device_id_type=MESH,
            )

        def at_near(self, n):
            return (self.mine * z.near + n, c)

        def copy3(self, to, src):
            return pltpu.make_async_remote_copy(
                src_ref=self.pk.at[self.across, odd, self.piece_at(to), :],
                dst_ref=self.r3.at[src], send_sem=self.sems[2].at[to],
                recv_sem=self.sems[3].at[src], device_id=self.at_near(to), device_id_type=MESH,
            )

        def copy4(self, to, src):
            return pltpu.make_async_remote_copy(
                src_ref=self.r3.at[self.near], dst_ref=self.res.at[self.piece_at(src), :],
                send_sem=self.sems[4].at[to], recv_sem=self.sems[5].at[src],
                device_id=self.at_near(to), device_id_type=MESH,
            )

        def copy5(self, to, src):
            return pltpu.make_async_remote_copy(
                src_ref=self.r4.at[self.mine], dst_ref=self.r4.at[src],
                send_sem=self.sems[6].at[to], recv_sem=self.sems[7].at[src],
                device_id=(to * z.near + self.near, c), device_id_type=MESH,
            )

        def local4(self):
            return pltpu.make_async_copy(
                self.r3.at[self.near], self.res.at[self.piece_at(self.near), :],
                self.sems[5].at[self.near],
            )

        def others(self, body, me, n):
            def step(j, _):
                body(lax.rem(me + j, n), lax.rem(me - j + n, n))
                return 0

            lax.fori_loop(1, n, step, 0)

        def total(self, slots, n, to):
            tile = self.piece if self.piece <= 256 else tile_of(self.piece)

            def body(at, _):
                rows = pl.ds(at, tile)
                t = slots[0, rows, :].astype(F32)
                for k in range(1, n):
                    t = t + slots[k, rows, :].astype(F32)
                to[rows, :] = t.astype(BF16)
                return 0

            loop(self.piece, tile, body, 0)

        def add(self, which, other):
            tile = tile_of(self.rows)

            def body(at, _):
                rows = pl.ds(at, tile)
                self.pk[which, odd, rows, :] = (
                    self.pk[which, odd, rows, :].astype(F32) + other(rows).astype(F32)
                ).astype(BF16)
                return 0

            loop(self.rows, tile, body, 0)

        def step1(self):
            self.copy1().start()

        def ready2(self):
            self.copy1().wait()
            for which in (1 - self.across, self.across):
                self.add(which, lambda rows, which=which: self.r1[which, rows, :])

        def step2(self):
            self.copy2().start()

        def ready3(self):
            self.copy2().wait()
            self.add(self.across, lambda rows: self.r2[rows, :])

        def step3(self):
            self.others(lambda to, _: self.copy3(to, self.near).start(), self.near, z.near)

        def ready4(self):
            self.r3[self.near] = self.pk[self.across, odd, self.piece_at(self.near), :]

            def arrive(to, src):
                self.copy3(to, self.near).wait_send()
                self.copy3(src, src).wait_recv()

            self.others(arrive, self.near, z.near)
            mine = self.r3.at[self.near]
            if z.far == 1:
                self.total(self.r3, z.near, mine)
            else:
                self.total(self.r3, z.near, self.r4.at[self.mine])
                self.others(lambda to, _: self.copy5(to, self.mine).start(), self.mine, z.far)

                def arrive_far(to, src):
                    self.copy5(to, self.mine).wait_send()
                    self.copy5(src, src).wait_recv()

                self.others(arrive_far, self.mine, z.far)
                self.total(self.r4, z.far, mine)

        def step4(self):
            self.local4().start()
            self.others(lambda to, _: self.copy4(to, self.near).start(), self.near, z.near)

        def finish(self):
            self.local4().wait()

            def arrive(to, src):
                self.copy4(to, self.near).wait_send()
                self.copy4(src, src).wait_recv()

            self.others(arrive, self.near, z.near)

    class SplitReduction(Reduction):
        def __init__(self, group):
            super().__init__(group)
            self.ry, self.q6 = r.group[group].ry, r.group[group].q6
            self.half = self.rows // 2
            self.par, self.far_at = lax.rem(self.near, 2), lax.div(self.near, 2)
            self.quad = z.near // 2
            self.mate = self.at_near(self.near + 1 - 2 * self.par)

        def half_at(self, par):
            return pl.ds(pl.multiple_of(par * self.half, 16), self.half)

        def piece_at(self, n):
            at = lax.rem(n, 2) * self.half + lax.div(n, 2) * self.piece
            return pl.ds(pl.multiple_of(at, 16), self.piece)

        def copy_half(self):
            return pltpu.make_async_remote_copy(
                src_ref=self.pk.at[self.across, odd, self.half_at(1 - self.par), :],
                dst_ref=self.ry, send_sem=self.q6.at[0], recv_sem=self.q6.at[1],
                device_id=self.mate, device_id_type=MESH,
            )

        def copy_back(self, par):
            rows = self.half_at(par)
            return pltpu.make_async_remote_copy(
                src_ref=self.res.at[rows, :], dst_ref=self.res.at[rows, :],
                send_sem=self.q6.at[2], recv_sem=self.q6.at[3],
                device_id=self.mate, device_id_type=MESH,
            )

        def slot3(self, to, src):
            n = 2 * to + self.par
            return pltpu.make_async_remote_copy(
                src_ref=self.pk.at[self.across, odd, self.piece_at(n), :],
                dst_ref=self.r3.at[src], send_sem=self.sems[2].at[to],
                recv_sem=self.sems[3].at[src], device_id=self.at_near(n), device_id_type=MESH,
            )

        def slot4(self, to, src):
            return pltpu.make_async_remote_copy(
                src_ref=self.r3.at[self.far_at],
                dst_ref=self.res.at[self.piece_at(2 * src + self.par), :],
                send_sem=self.sems[4].at[to], recv_sem=self.sems[5].at[src],
                device_id=self.at_near(2 * to + self.par), device_id_type=MESH,
            )

        def local5(self):
            return pltpu.make_async_copy(
                self.r3.at[self.far_at], self.res.at[self.piece_at(self.near), :],
                self.sems[5].at[self.far_at],
            )

        def step3(self):
            self.copy_half().start()

        def ready4(self):
            self.copy_half().wait()
            tile = tile_of(self.half)

            def body(at, _):
                rows = pl.ds(pl.multiple_of(self.par * self.half + at, 16), tile)
                self.pk[self.across, odd, rows, :] = (
                    self.pk[self.across, odd, rows, :].astype(F32)
                    + self.ry[pl.ds(at, tile), :].astype(F32)
                ).astype(BF16)
                return 0

            loop(self.half, tile, body, 0)

        def step4(self):
            self.others(lambda to, _: self.slot3(to, self.far_at).start(), self.far_at, self.quad)

        def ready5(self):
            self.r3[self.far_at] = self.pk[self.across, odd, self.piece_at(self.near), :]

            def arrive(to, src):
                self.slot3(to, self.far_at).wait_send()
                self.slot3(src, src).wait_recv()

            self.others(arrive, self.far_at, self.quad)
            mine = self.r3.at[self.far_at]
            if z.far == 1:
                self.total(self.r3, self.quad, mine)
            else:
                self.total(self.r3, self.quad, self.r4.at[self.mine])
                self.others(lambda to, _: self.copy5(to, self.mine).start(), self.mine, z.far)

                def arrive_far(to, src):
                    self.copy5(to, self.mine).wait_send()
                    self.copy5(src, src).wait_recv()

                self.others(arrive_far, self.mine, z.far)
                self.total(self.r4, z.far, mine)

        def step5(self):
            self.local5().start()
            self.others(lambda to, _: self.slot4(to, self.far_at).start(), self.far_at, self.quad)

        def ready6(self):
            self.local5().wait()

            def arrive(to, src):
                self.slot4(to, self.far_at).wait_send()
                self.slot4(src, src).wait_recv()

            self.others(arrive, self.far_at, self.quad)

        def step6(self):
            self.copy_back(self.par).start()

        def finish(self):
            self.copy_back(self.par).wait_send()
            self.copy_back(1 - self.par).wait_recv()

    sums_of = {group: (SplitReduction if group in SPLIT_GROUPS else Reduction)(group) for group in GROUPS}

    def attention_backward(k, f, sync):
        srow = STO_ROWS[k]
        nexp, nsplit, natt = f.nexp, f.nsplit, f.natt
        first = k == 1
        cw = co // LANES
        su, sux, ea, eb = norm_grad(sync, 0, cw, co, inv_out, nexp)
        keep(srow.eb, su)
        keep(srow.eg, sux)
        if first:
            _, suxh, ha, hb = norm_grad(sync, 0, 2 * cw, co, inv_out, nshort)
            keep(srow.hg, suxh)

        def expand_grad(at, _):
            rows = pl.ds(at, 16)
            m = tiled(r.mo[rows, :], co)
            u = r.g[rows, :]
            r.eg[rows, :] = (nexp.gs * u - m * (ea + eb * r.blk[k].exp[rows, :])).astype(BF16)
            if first:
                r.shg[rows, :] = (
                    nshort.gs * u - m * (ha + hb * r.short[rows, :])
                ).astype(BF16)
            return 0

        loop(no, 16, expand_grad, 0)
        r.mg[...] = dot(r.eg[...], r.blk[k].we[...], NT)
        sa = r.blk[k].sa
        for img in range(b):
            def att_grad(at, s, img=img):
                rows = pl.ds(pl.multiple_of(at + img * po, 32), 32)
                return s + sum8(sa[rows, :] * tiled_pair(r.mg[rows, :]))

            r.ags[img : img + 1, :] = fold(loop(po, 32, att_grad, zero8(2 * mid)))
        ags, at_ref = r.ags, r.blk[k].att
        a0, a1 = at_ref[:, :mid], at_ref[:, mid:]
        g0, g1 = ags[:, :mid], ags[:, mid:]
        mean = a0 * g0 + a1 * g1
        l0, l1 = a0 * (g0 - mean), a1 * (g1 - mean)
        ext = r.blk[k].ext
        excited_grad = dot_exact(l0, ext[0]) + dot_exact(l1, ext[1])
        au = excited_grad * silu_slope(f.pre)
        sq = r.blk[k].sq
        sp = r.blk[k].sp
        r.mgr[...] = dot_exact(natt.gs * au * live8, sq[...], NT) * tiled(inv_area, mid)
        carry = (zero8(2 * mid), zero8(2 * mid))
        for img in range(b):
            def split_up(at, carry, img=img):
                s1, s2 = carry
                rows = pl.ds(pl.multiple_of(at + img * po, 32), 32)
                v = sp[rows, :]
                slope = tiled(r.mo[rows, :], 2 * mid) * silu_slope(v * nsplit.gs + nsplit.sh)
                r.su[rows, :] = slope
                u = slope * (
                    tiled_pair(r.mg[rows, :]) * at_ref[img : img + 1, :]
                    + tiled_pair(r.mgr[img : img + 1, :])
                )
                return s1 + sum8(u), s2 + sum8(u * v)

            carry = loop(po, 32, split_up, carry)
        put(sync + 1, 0, fold(au))
        put(sync + 1, 1, fold(au * f.xhat))
        put(sync + 1, 2, fold(l0))
        put(sync + 1, 4, fold(l1))
        put(sync + 1, 6, fold(carry[0]))
        put(sync + 1, 10, fold(carry[1]))

        def matrices():
            r.mixt[...] = jnp.transpose(r.blk[k].mix[...])
            for s in range(nc):
                share = slice(s * z.cos, (s + 1) * z.cos)
                pack_lanes(k, EXPAND, s, dot(r.mixt[...], r.eg[:, share]))
            pack_rows(k, EXCITE, 0, dot_exact(l0, f.excited, TN))
            pack_rows(k, EXCITE, 1, dot_exact(l1, f.excited, TN))
            if first:
                r.sgt[...] = jnp.transpose(r.pool[...])
                for s in range(nc):
                    share = slice(s * z.cos, (s + 1) * z.cos)
                    pack_lanes(k, SHORTCUT, s, dot(r.sgt[...], r.shg[:, share]))
                sums_of[2].step1()
                sums_of[5].ready2()
                sums_of[0].ready4()
                sums_of[1].ready3()
                r.pg[...] = dot(r.shg[...], r.wsh[...], NT).astype(BF16)

            else:
                sums_of[0].step1()

        if first:
            meet[1].finish()
        allreduce(sync + 1, 14, matrices)
        if first:
            sums_of[5].step2()
            sums_of[2].ready2()
            sums_of[2].step2()
            sums_of[0].step4()
            sums_of[1].step3()
        else:
            out_ex[1].start()
        inv_images = 1.0 / (b * nc * nd)
        su, sux = total(sync + 1, 0, att), total(sync + 1, 1, att)
        keep(srow.qb, su)
        keep(srow.qg, sux)
        keep(srow.xb, total(sync + 1, 2, 2 * mid))
        su, sux = su * inv_images, sux * inv_images
        sb = natt.gs * (au - su - f.xhat * sux) * live8
        r.mgr[...] = dot_exact(sb, sq[...], NT) * tiled(inv_area, mid)
        seen = nd * 8
        off = dot_exact(natt.gs * (su + r.all[:, 8].reshape(seen, LANES) * sux), sq[...], NT)
        taken = []
        for kind in range(8):
            lanes = slice(kind % 2 * LANES, (kind % 2 + 1) * LANES)
            taken.append(fold(sum8(off[:, lanes] * r.all[:, kind].reshape(seen, LANES))))
        su = total(sync + 1, 6, 2 * mid) - jnp.concatenate(taken[:4], axis=1)
        sv = total(sync + 1, 10, 2 * mid) - jnp.concatenate(taken[4:], axis=1)
        su, sux, ca, cb = norm_grad_of(su, sv, 2 * mid, inv_out, nsplit)
        keep(srow.sb, su)
        keep(srow.sg, sux)

        def split_grad(at, _, img=0):
            rows = pl.ds(pl.multiple_of(at + img * po, 32), 32)
            m = tiled(r.mo[rows, :], 2 * mid)
            u = r.su[rows, :] * (
                tiled_pair(r.mg[rows, :]) * at_ref[img : img + 1, :]
                + tiled_pair(r.mgr[img : img + 1, :])
            )
            r.sgb[rows, :] = (nsplit.gs * u - m * (ca + cb * sp[rows, :])).astype(BF16)
            return 0

        for img in range(b):
            loop(po, 32, functools.partial(split_grad, img=img), 0)

        def squeeze_matrix():
            pack_rows(k, SQUEEZE, 0, dot_exact(f.centred, sb, TN))

        return squeeze_matrix

    def tiled_pair(v):
        return jnp.concatenate([v, v], axis=1)

    def split_matrix(k):
        r.sgt[...] = jnp.transpose(r.sgb[...])
        for g in range(2):
            for t in range(3):
                v = dot(
                    r.sgt[g * mid : (g + 1) * mid, :],
                    r.blk[k].im[g, so : so + no, 3 * t * grp : 3 * (t + 1) * grp],
                )
                for u in range(3):
                    pack_rows(
                        k, SPLIT, (3 * t + u) * 2 + g, v[:, u * grp : (u + 1) * grp]
                    )

    dcol = r.dcol
    dcol[:so, :] = jnp.zeros((so, kk), F32)
    dcol[so + po :, :] = jnp.zeros((so, kk), F32)

    def columns(k, img, g):
        dcol[so : so + po, :] = dot(
            r.sgb[img * po : (img + 1) * po, g * mid : (g + 1) * mid], split_weights(k, g)
        )

    tile = 4 * so
    first_g, last_g = not_first[:, :grp], not_last[:, :grp]

    def tap(at, di, dj, shift):
        t = di * 3 + dj
        return dcol[pl.ds(pl.multiple_of(at + so - shift * so, so), tile), t * grp : (t + 1) * grp]

    def from_left(v):
        return jnp.where(first_g, pltpu.roll(v, 1, 0), 0.0)

    def from_right(v):
        return jnp.where(last_g, pltpu.roll(v, tile - 1, 0), 0.0)

    meet[2].finish()
    squeeze_matrix2 = attention_backward(2, f2, 8)
    sums = []
    for g in range(2):
        carry = (zero8(grp), zero8(grp))
        lanes = slice(g * grp, (g + 1) * grp)
        for img in range(b):
            columns(2, img, g)

            def back2(at, carry, img=img, g=g, lanes=lanes):
                s1, s2 = carry
                cols = [
                    tap(at, 0, dj, -1) + tap(at, 1, dj, 0) + tap(at, 2, dj, 1) for dj in range(3)
                ]
                grad = cols[1] + from_right(cols[0]) + from_left(cols[2])
                rows = pl.ds(pl.multiple_of(at + img * po, tile), tile)
                v = r.red2[rows, lanes]
                u = (
                    grad
                    * tiled(r.mo[rows, :], grp)
                    * silu_slope(v * nred2.gs[:, lanes] + nred2.sh[:, lanes])
                )
                r.u2[rows, lanes] = u
                return s1 + sum8(u), s2 + sum8(u * v)

            carry = loop(po, tile, back2, carry)
        sums.append(carry)
    put(10, 0, jnp.concatenate([fold(s[0]) for s in sums], axis=1))
    put(10, 2, jnp.concatenate([fold(s[1]) for s in sums], axis=1))
    def split_matrix2():
        split_matrix(2)
        squeeze_matrix2()
        sums_of[1].step1()
        sums_of[0].ready2()

    allreduce(10, 4, split_matrix2)
    sums_of[0].step2()
    out_ex[2].start()
    meet[1].send()
    su, sux, ca, cb = norm_grad(10, 0, 2, mid, inv_out, nred2)
    keep(STO_ROWS[2].rb, su)
    keep(STO_ROWS[2].rg, sux)

    def reduce_grad2(at, _):
        rows = pl.ds(at, 64)
        m = tiled(r.mo[rows, :], mid)
        r.rg1[rows, :] = (
            nred2.gs * r.u2[rows, :] - m * (ca + cb * r.red2[rows, :])
        ).astype(BF16)
        return 0

    loop(no, 64, reduce_grad2, 0)
    for n0 in range(0, co, 256):
        cols = slice(n0, n0 + 256)
        r.g[:, cols] = r.g[:, cols] + dot(r.rg1[:no, :], r.blk[2].wrt[:, cols])

    def first_up(at, carry):
        s1, s2, s3 = carry
        rows = pl.ds(at, 16)
        u = r.g[rows, :] * tiled(r.mo[rows, :], co) * silu_slope(summed1(rows))
        r.g[rows, :] = u
        return (
            s1 + sum8(u),
            s2 + sum8(u * r.blk[1].exp[rows, :]),
            s3 + sum8(u * r.short[rows, :]),
        )

    s1, s2, s3 = loop(no, 16, first_up, (zero8(co), zero8(co), zero8(co)))
    put(11, 0, fold(s1))
    put(11, co // LANES, fold(s2))
    put(11, 2 * co // LANES, fold(s3))

    def reduce_matrix2():
        r.rgt[:, :no] = jnp.transpose(r.rg1[:no, :])
        for n0 in range(0, co, 256):
            pack_rows(2, REDUCE, n0 // LANES, dot(r.rgt[:, :no], r.h[:, n0 : n0 + 256]))
        sums_of[5].step1()
        sums_of[1].ready2()
        sums_of[0].ready3()

    allreduce(11, 3 * co // LANES, reduce_matrix2)
    sums_of[1].step2()
    sums_of[0].step3()
    out_ex[3].start()

    squeeze_matrix1 = attention_backward(1, f1, 11)
    split_matrix(1)
    squeeze_matrix1()
    sums_of[3].step1()
    sums = []
    for g in range(2):
        carry = (zero8(grp), zero8(grp))
        lanes = slice(g * grp, (g + 1) * grp)
        for img in range(b):
            columns(1, img, g)

            def back1(at, carry, img=img, g=g, lanes=lanes):
                s1, s2 = carry
                rows = pl.ds(pl.multiple_of(at + img * po, tile), tile)
                m = tiled(r.mo[rows, :], grp)
                lead = pl.ds(pl.multiple_of(lax.div(at, so) + img * so, 4), 4)
                for p in range(2):
                    for q in range(2):
                        def col(dj):
                            if p == 0:
                                return tap(at, 1, dj, 0)
                            return tap(at, 0, dj, -1) + tap(at, 2, dj, 0)

                        grad = col(1) if q == 0 else col(2) + from_right(col(0))
                        v = phase_of(g, lead, p, q)
                        u = grad * m * silu_slope(v * nred1.gs[:, lanes] + nred1.sh[:, lanes])
                        r.u1[g, lead, p, pl.ds(q, so, stride=2), :] = u.reshape(4, so, grp)
                        s1, s2 = s1 + sum8(u), s2 + sum8(u * v)
                return s1, s2

            carry = loop(po, tile, back1, carry)
        sums.append(carry)
    put(13, 0, jnp.concatenate([fold(s[0]) for s in sums], axis=1))
    put(13, 2, jnp.concatenate([fold(s[1]) for s in sums], axis=1))

    def behind_last():
        sums_of[3].ready2()
        sums_of[3].step2()
        sums_of[1].ready4()
        sums_of[5].ready3()

    allreduce(13, 4, behind_last)
    sums_of[1].step4()
    sums_of[5].step3()
    su, sux, ca, cb = norm_grad(13, 0, 2, mid, inv_in, nred1)
    keep(STO_ROWS[1].rb, su)
    keep(STO_ROWS[1].rg, sux)

    def reduce_grad1(i, _):
        rows = pl.ds(pl.multiple_of(i * 2 * si, 2 * si), 2 * si)
        m = tiled(r.mi[rows, :].astype(F32), mid)
        u, v = row_pair(r.u1, i), row_pair(red1, i)
        r.rg1[rows, :] = (nred1.gs * u - m * (ca + cb * v)).astype(BF16)
        return 0

    spread = pool_matrix(1)
    grads = (r.h, r.eg)
    last = []

    def send_quarter(q):
        rows = slice(q * part, (q + 1) * part)
        m = tiled(r.mi[rows, :].astype(F32), 256)
        for n0 in range(0, ci, 256):
            cols = slice(n0, n0 + 256)
            v = dot(r.rg1[rows, :], r.blk[1].wrt[:, cols]) + dot(
                spread, r.pg[q * pool_rows : (q + 1) * pool_rows, cols]
            )
            at = (q % 2) * ci + n0
            grads[q // 2][:, at : at + 256] = (v * m).astype(BF16)
        e = Exchange(
            lambda s, q=q: grads[q // 2].at[
                :, pl.ds(pl.multiple_of((q % 2) * ci + s * z.cis, LANES), z.cis)
            ],
            lambda s, q=q: made.gx.at[
                pl.ds(pl.multiple_of(s * ni + q * part, part), part), :
            ],
            os_sem.at[OUT_PARTS + q],
            or_sem.at[OUT_PARTS + q],
        )
        e.start()
        last.append(e)

    lead = part // (2 * si)
    lax.fori_loop(0, lead, reduce_grad1, 0)
    send_quarter(0)
    sums_of[2].ready3()
    sums_of[2].step3()
    lax.fori_loop(lead, nq * lead, reduce_grad1, 0)
    r.rgt[...] = jnp.transpose(r.rg1[...])
    for n0 in range(0, ci, 256):
        pack_rows(1, REDUCE, n0 // LANES, dot(r.rgt[...], r.x[:, n0 : n0 + 256]))
    sums_of[4].step1()
    sums_of[3].ready3()
    sums_of[3].step3()
    sums_of[4].ready2()
    sums_of[4].step2()
    send_quarter(1)
    sums_of[2].ready4()
    sums_of[2].step4()
    sums_of[1].ready5()
    sums_of[1].step5()
    sums_of[5].ready4()
    sums_of[5].step4()
    for q in range(2, nq):
        send_quarter(q)
    sums_of[3].ready4()
    sums_of[3].step4()
    sums_of[2].ready5()
    sums_of[2].step5()
    sums_of[1].ready6()
    sums_of[1].step6()
    sums_of[5].ready5()
    sums_of[5].step5()
    sums_of[4].ready3()
    sums_of[4].step3()
    sums_of[3].ready5()
    sums_of[3].step5()
    sums_of[2].ready6()
    sums_of[2].step6()
    sums_of[5].ready6()
    sums_of[5].step6()
    sums_of[4].ready4()
    sums_of[4].step4()
    sums_of[3].ready6()
    sums_of[3].step6()
    for e in out_ex + last:
        e.wait()
    for sums in sums_of.values():
        sums.finish()


class Weights:
    def __init__(self, values):
        (
            self.reduce, self.reducegain, self.reducebias,
            self.split, self.splitgain, self.splitbias,
            self.squeeze, self.squeezegain, self.squeezebias,
            self.excite, self.excitebias,
            self.expand, self.expandgain, self.expandbias,
        ) = values[:14]
        self.extra = values[14:]


def doubled(v):
    return jnp.concatenate([v, v], axis=-1).reshape(-1, LANES)


def per_device(mesh, images, cotangent, groups, *weights):
    first, second = Weights(weights[:17]), Weights(weights[17:])
    z = Sizes(mesh, images, first.reduce, first.expand, first.squeeze)

    def vectors(w):
        parts = (w.reducegain, w.reducebias, w.splitgain, w.splitbias, w.excitebias)
        parts += (w.expandgain, w.expandbias) + w.extra[1:] + (w.squeezegain, w.squeezebias)
        return [v if v.ndim == 2 else v.reshape(1, -1) for v in parts]

    def block(w):
        return dict(
            wrt=w.reduce.T,
            wst=jnp.transpose(w.split, (0, 1, 3, 4, 2)).reshape(TAPS, 2, z.mids, z.grp),
            sq=w.squeeze,
            ext=jnp.transpose(w.excite, (1, 2, 0)),
            we=w.expand,
        )

    inputs = dict(
        images=images.reshape(-1, z.cis),
        cot=cotangent.reshape(-1, z.cos),
        groups=groups,
        vec=vectors(first) + vectors(second),
        wsh=first.extra[0],
        blk={1: block(first), 2: block(second)},
    )
    in_specs = jax.tree.map(lambda v: pl.BlockSpec(memory_space=pl.ANY), inputs)
    in_specs.update(groups=pl.BlockSpec(memory_space=pltpu.SMEM))
    outs = dict(
        out=jax.ShapeDtypeStruct((z.nc * z.no, z.cos), BF16),
        gx=jax.ShapeDtypeStruct((z.nc * z.ni, z.cis), BF16),
        sto=jax.ShapeDtypeStruct((NSTO, LANES), F32),
        res={n: jax.ShapeDtypeStruct((rows, LANES), BF16) for n, rows in z.rows.items()},
    )
    out_specs = jax.tree.map(lambda v: pl.BlockSpec(memory_space=pl.ANY), outs)
    out_specs.update(sto=pl.BlockSpec(memory_space=pltpu.VMEM))
    scratch = scratch_tree(z, vectors(first) + vectors(second))
    tree = jax.tree.structure((inputs, outs, scratch))
    results = pl.pallas_call(
        functools.partial(mega_kernel, z, tree),
        out_shape=jax.tree.leaves(outs),
        in_specs=jax.tree.leaves(in_specs),
        out_specs=jax.tree.leaves(out_specs),
        scratch_shapes=jax.tree.leaves(scratch),
        compiler_params=pltpu.CompilerParams(
            collective_id=0, has_side_effects=True, vmem_limit_bytes=63 << 20
        ),
        name="two_blocks",
    )(*jax.tree.leaves(inputs))
    return unpack(z, jax.tree.unflatten(jax.tree.structure(outs), results))


def unpack_kernel(z, plan, tree, *refs):
    given, (out_image, gx, *outs) = jax.tree.unflatten(tree, refs)
    given = space(given)
    out_in, gx_in, sto, res = given.out, given.gx, given.sto, given.res
    c = lax.axis_index(CHAN)
    out_image[...] = out_in[...].astype(F32)
    gx[...] = gx_in[...].astype(F32)

    def mid_share(row):
        v = sto[pl.ds(row + lax.div(c, 2), 1), :]
        return jnp.where(lax.rem(c, 2) == 0, v[:, : z.mids], v[:, z.mids :])

    @pl.when(pl.program_id(0) == 0)
    def _():
        for (kind, k, name), o in zip(plan, outs):
            if kind == MATRIX:
                group, at = z.lay[(k, name)]
                rows = o.shape[0]
                for t in range(o.shape[1] // LANES):
                    o[:, t * LANES : (t + 1) * LANES] = res[group][
                        at + t * rows : at + (t + 1) * rows, :
                    ].astype(F32)
                continue
            row = name
            if kind == MID_VECTOR:
                o[...] = mid_share(row)
            elif kind == PAIR_VECTOR:
                o[0:1, :] = mid_share(row)
                o[1:2, :] = mid_share(row + z.mid // LANES)
            elif kind == ATT_VECTOR:
                o[...] = sto[row : row + 1, :]
            else:
                n = z.cos // LANES
                for t in range(n):
                    o[:, t * LANES : (t + 1) * LANES] = sto[pl.ds(row + c * n + t, 1), :]


def unpack(z, results):
    plan = []
    for k in (1, 2):
        v = STO_ROWS[k]
        plan += [
            (MATRIX, k, REDUCE), (MID_VECTOR, k, v.rg), (MID_VECTOR, k, v.rb),
            (MATRIX, k, SPLIT), (PAIR_VECTOR, k, v.sg), (PAIR_VECTOR, k, v.sb),
            (MATRIX, k, SQUEEZE), (ATT_VECTOR, k, v.qg), (ATT_VECTOR, k, v.qb),
            (MATRIX, k, EXCITE), (PAIR_VECTOR, k, v.xb),
            (MATRIX, k, EXPAND), (OUT_VECTOR, k, v.eg), (OUT_VECTOR, k, v.eb),
        ]
        if k == 1:
            plan += [(MATRIX, k, SHORTCUT), (OUT_VECTOR, k, v.hg), (OUT_VECTOR, k, v.eb)]

    def shape_of(kind, k, name):
        if kind == MATRIX:
            return (
                (z.mids, z.ci if k == 1 else z.co),
                (2 * TAPS * z.mids, LANES),
                (z.mids, z.att),
                (2 * z.mids, z.att),
                (z.mid, z.cos),
                (z.ci, z.cos),
            )[name]
        return (None, (1, z.mids), (2, z.mids), (1, z.att), (1, z.cos))[kind]

    shapes = [shape_of(*entry) for entry in plan]
    steps = 4
    whole = lambda shape: pl.BlockSpec(shape, lambda i: (0, 0))
    slab = lambda v: pl.BlockSpec((v.shape[0] // steps, v.shape[1]), lambda i: (i, 0))
    in_specs = {n: slab(v) if n in ("out", "gx") else jax.tree.map(lambda a: whole(a.shape), v)
                for n, v in results.items()}
    images = [results["out"], results["gx"]]
    outs = [jax.ShapeDtypeStruct(v.shape, F32) for v in images]
    outs += [jax.ShapeDtypeStruct(s, F32) for s in shapes]
    flat = pl.pallas_call(
        functools.partial(unpack_kernel, z, plan, jax.tree.structure((results, outs))),
        grid=(steps,),
        out_shape=outs,
        in_specs=jax.tree.leaves(in_specs),
        out_specs=[slab(v) for v in images] + [whole(s) for s in shapes],
        compiler_params=pltpu.CompilerParams(vmem_limit_bytes=62 << 20),
        name="unpack",
    )(*jax.tree.leaves(results))
    final = [
        flat[0].reshape(z.nc * z.b, z.so, z.so, z.cos),
        flat[1].reshape(z.nc * z.b, z.si, z.si, z.cis),
    ]
    for (kind, _, name), v in zip(plan, flat[2:]):
        if (kind, name) == (MATRIX, REDUCE):
            v = v.T
        elif (kind, name) == (MATRIX, SPLIT):
            v = jnp.transpose(v.reshape(3, 3, 2, z.mids, z.grp), (0, 1, 4, 2, 3))
        elif (kind, name) == (MATRIX, EXCITE):
            v = jnp.transpose(v.reshape(2, z.mids, z.att), (2, 0, 1))
        elif kind in (MID_VECTOR, ATT_VECTOR, OUT_VECTOR):
            v = v.reshape(-1)
        final.append(v)
    return tuple(final)


def specs():
    block = [
        P(None, CHAN), P(CHAN), P(CHAN),
        P(None, None, None, None, CHAN), P(None, CHAN), P(None, CHAN),
        P(CHAN, None), P(), P(), P(None, None, CHAN), P(None, CHAN),
        P(None, CHAN), P(CHAN), P(CHAN),
    ]
    short = [P(None, CHAN), P(CHAN), P(CHAN)]
    return block + short + block


def solution(mesh):
    image = P(DP, None, None, CHAN)
    return jax.shard_map(
        functools.partial(per_device, mesh),
        mesh=mesh,
        in_specs=tuple([image, image, P(DP)] + specs()),
        out_specs=tuple([image, image] + specs()),
        check_vma=False,
    )
```

```python
import functools
from types import SimpleNamespace

import jax
import jax.numpy as jnp
from jax import lax
from jax.experimental import pallas as pl
from jax.experimental.pallas import tpu as pltpu
from jax.sharding import PartitionSpec as P

EPSILON = 1e-05
F32, BF16 = jnp.float32, jnp.bfloat16
HIGHEST = lax.Precision.HIGHEST
MESH = pl.DeviceIdType.MESH
LANES = 128
TAPS = 9
DP, CHAN = "dp", "chan"
REDUCE, SPLIT, SQUEEZE, EXCITE, EXPAND, SHORTCUT = range(6)
MATRIX, MID_VECTOR, PAIR_VECTOR, ATT_VECTOR, OUT_VECTOR = range(5)
SYNC_ROWS = (8, 8, 8, 32, 8, 8, 8, 16, 16, 16, 8, 24, 16, 8)

NT = (((1,), (1,)), ((), ()))
NN = (((1,), (0,)), ((), ()))
TN = (((0,), (0,)), ((), ()))


def dot(a, b, dims=NN):
    return lax.dot_general(a, b, dims, preferred_element_type=F32)


def dot_exact(a, b, dims=NN):
    return lax.dot_general(
        a.astype(F32), b.astype(F32), dims, precision=HIGHEST, preferred_element_type=F32
    )


def sigmoid(v):
    return 0.5 * jnp.tanh(0.5 * v) + 0.5


def silu(v):
    return v * sigmoid(v)


def silu_slope(v):
    q = sigmoid(v)
    return q * (1.0 + v * (1.0 - q))


def tiled(v, width):
    return jnp.concatenate([v] * (width // LANES), axis=1) if width > LANES else v


def sum8(v):
    return jnp.sum(v.reshape(v.shape[0] // 8, 8, v.shape[1]), axis=0)


def fold(v):
    return jnp.sum(v, axis=0, keepdims=True)


def span(start, size):
    if isinstance(start, int):
        return pl.ds(start, size)
    return pl.ds(pl.multiple_of(start, size), size)


def tile_of(rows):
    return next(t for t in (256, 128, 64, 32, 16) if rows % t == 0)


class Sizes:
    def __init__(self, mesh, images, reduce_w, expand_w, squeeze_w):
        self.nd, self.nc = mesh.shape[DP], mesh.shape[CHAN]
        self.near = min(self.nd, 8)
        self.far = self.nd // self.near
        self.b = images.shape[0] // self.nc
        self.si = images.shape[1]
        self.so = self.si // 2
        self.cis = images.shape[3]
        self.ci = self.cis * self.nc
        self.mids = reduce_w.shape[1]
        self.mid = self.mids * self.nc
        self.cos = expand_w.shape[1]
        self.co = self.cos * self.nc
        self.att = squeeze_w.shape[1]
        self.po = self.so * self.so
        self.pi = self.si * self.si
        self.no = self.b * self.po
        self.ni = self.b * self.pi
        self.grp = self.mid // 2
        self.kk = TAPS * self.grp
        cin = {1: self.ci, 2: self.co}
        self.piece_rows = {
            (k, name): rows
            for k in (1, 2)
            for name, rows in (
                (REDUCE, cin[k] // LANES * self.mids),
                (SPLIT, 2 * TAPS * self.mids),
                (SQUEEZE, self.mids),
                (EXCITE, 2 * self.mids),
                (EXPAND, self.cos // LANES * self.mid),
                (SHORTCUT, self.cos // LANES * self.ci),
            )
        }
        self.lay, self.rows = {}, {}
        for group, members in GROUPS.items():
            at = 0
            for key in members:
                self.lay[key] = (group, at)
                at += self.piece_rows[key]
            self.rows[group] = -(-at // (16 * self.near)) * 16 * self.near


GROUPS = {
    0: ((2, EXPAND), (2, EXCITE)),
    1: ((2, SPLIT), (2, SQUEEZE)),
    2: ((1, EXPAND), (1, EXCITE), (1, SHORTCUT)),
    3: ((1, SPLIT), (1, SQUEEZE)),
    4: ((1, REDUCE),),
    5: ((2, REDUCE),),
}
SPLIT_GROUPS = (1, 2, 3)
VEC_ROWS = {
    1: SimpleNamespace(rg=0, rb=1, sg=2, sb=4, xb=6, eg=8, eb=10, hg=12, hb=14, qg=16, qb=17),
    2: SimpleNamespace(rg=18, rb=19, sg=20, sb=22, xb=24, eg=26, eb=28, qg=30, qb=31),
}
NVEC = 32
STO_ROWS = {
    2: SimpleNamespace(eb=0, eg=8, qb=16, qg=17, sb=18, sg=22, rb=26, rg=28, xb=30),
    1: SimpleNamespace(eb=34, eg=42, qb=50, qg=51, sb=52, sg=56, rb=60, rg=62, xb=64, hg=68),
}
NSTO = 80
QUARTERS = 4
KINDS = 9
OUT_PARTS = 4


def space(tree):
    if not isinstance(tree, dict):
        return tree
    inner = {k: space(v) for k, v in tree.items()}
    return SimpleNamespace(**inner) if all(isinstance(k, str) for k in inner) else inner


def scratch_tree(z, vec):
    def f32(*shape):
        return pltpu.VMEM(shape, F32)

    def bf16(*shape):
        return pltpu.VMEM(shape, BF16)

    def sem(*shape):
        return pltpu.SemaphoreType.DMA(shape)

    ns = z.nd * z.nc // 2
    return dict(
        x=bf16(z.ni, z.ci),
        cot=bf16(z.no, z.co),
        wsh=bf16(z.ci, z.co),
        vv=f32(z.nc, NVEC, LANES),
        vmine=f32(NVEC, LANES),
        vraw=[f32(*v.shape) for v in vec],
        vsem=sem(len(vec)),
        mo=f32(z.no, LANES),
        mi=bf16(z.ni, LANES),
        red1=f32(z.mid // LANES, z.b * z.so, 2, z.si, LANES),
        u1=f32(z.mid // LANES, z.b * z.so, 2, z.si, LANES),
        pool=bf16(z.no, z.ci),
        short=f32(z.no, z.co),
        h=bf16(z.no, z.co),
        red2=f32(z.no, z.mid),
        u2=f32(z.no, z.mid),
        g=f32(z.no, z.co),
        eg=bf16(z.no, z.co),
        shg=bf16(z.no, z.co),
        mg=f32(z.no, z.mid),
        su=f32(z.no, 2 * z.mid),
        sgb=bf16(z.no, 2 * z.mid),
        sgt=bf16(2 * z.mid, z.no),
        mixt=bf16(z.mid, z.no),
        dcol=f32(z.po + 2 * z.so, z.kk),
        rg1=bf16(z.ni, z.mid),
        rgt=bf16(z.mid, z.ni),
        pg=bf16(z.no, z.ci),
        ags=f32(8, 2 * z.mid),
        met=f32(z.nc, KINDS * z.b + 6, LANES),
        all=f32(z.nd, KINDS, 8, LANES),
        mgr=f32(8, z.mid),
        blk={
            k: dict(
                wrt=bf16(z.mid, z.ci if k == 1 else z.co),
                wst=bf16(TAPS, 2, z.mid, z.grp),
                sq=bf16(z.mid, z.att),
                ext=bf16(2, z.mid, z.att),
                we=bf16(z.mid, z.co),
                im=bf16(2, z.no + 2 * z.so, z.kk),
                sp=f32(z.no, 2 * z.mid),
                sa=f32(z.no, 2 * z.mid),
                mix=bf16(z.no, z.mid),
                exp=f32(z.no, z.co),
                att=f32(8, 2 * z.mid),
                pm=f32(8, z.mid),
                own=f32(KINDS * z.b + 6, LANES),
                group=f32(KINDS, 8, LANES),
                ms=sem(3),
                mr=sem(3),
            )
            for k in (1, 2)
        },
        group={
            n: dict(
                pk=bf16(z.nc // 2, 2, rows, LANES),
                r1=bf16(z.nc // 2, rows, LANES),
                r2=bf16(rows, LANES),
                r3=bf16(z.near, rows // z.near, LANES),
                r4=bf16(z.far, rows // z.near, LANES),
                q1=sem(2),
                q2=sem(2),
                q3s=sem(z.near),
                q3r=sem(z.near),
                q4s=sem(z.near),
                q4r=sem(z.near),
                q5s=sem(z.far),
                q5r=sem(z.far),
                ry=bf16(rows // 2 if n in SPLIT_GROUPS else 16, LANES),
                q6=sem(4),
            )
            for n, rows in z.rows.items()
        },
        sync={
            k: dict(sa=f32(rows, LANES), sb=f32(rows, LANES), st=f32(rows, LANES))
            for k, rows in enumerate(SYNC_ROWS)
        },
        slots={p: f32(ns, max(SYNC_ROWS), LANES) for p in range(2)},
        gather_send=sem(13, z.nc),
        gather_recv=sem(13, z.nc),
        image_send=sem(QUARTERS, z.nc),
        image_recv=sem(QUARTERS, z.nc),
        out_send=sem(OUT_PARTS + QUARTERS, z.nc),
        out_got=sem(OUT_PARTS + QUARTERS, z.nc),
        s0s=sem(1),
        s0r=sem(2),
        s1s=sem(1),
        s1r=sem(2),
    )


def mega_kernel(z, tree, *refs):
    given, made, r = (space(t) for t in jax.tree.unflatten(tree, refs))
    nc, nd = z.nc, z.nd
    b, so, si, po, pi_, no, ni = z.b, z.so, z.si, z.po, z.pi, z.no, z.ni
    mid, co, ci, att, grp, kk = z.mid, z.co, z.ci, z.att, z.grp, z.kk
    d, c = lax.axis_index(DP), lax.axis_index(CHAN)
    ns = nd * nc // 2
    me = d * (nc // 2) + lax.div(c, 2)
    odd = lax.rem(c, 2)

    def chan_at(i):
        return lax.rem(c + i, nc)

    def place(s):
        return (lax.div(s, nc // 2), lax.rem(s, nc // 2) * 2 + odd)

    partner = (d, c + 1 - 2 * odd)
    far_first = []
    if ns <= 16:
        for n in range(ns - 1):
            far_first.append(place(lax.rem(me + (n + ns // 3) % (ns - 1) + 1, ns)))

    barrier = pltpu.get_barrier_semaphore()
    for i in range(1, nc):
        pl.semaphore_signal(barrier, inc=1, device_id=(d, chan_at(i)), device_id_type=MESH)

    def greet(j, _):
        pl.semaphore_signal(
            barrier, inc=1, device_id=place(lax.rem(me + j, ns)), device_id_type=MESH
        )
        return 0

    lax.fori_loop(1, ns, greet, 0)
    pl.semaphore_wait(barrier, nc - 1 + ns - 1)

    class Exchange:
        def __init__(self, src, dst, send, recv):
            self.src, self.dst, self.send, self.recv = src, dst, send, recv

        def copy(self, i):
            to = chan_at(i)
            return pltpu.make_async_remote_copy(
                src_ref=self.src(to), dst_ref=self.dst(c), send_sem=self.send.at[i],
                recv_sem=self.recv.at[i], device_id=(d, to), device_id_type=MESH,
            )

        def local(self):
            return pltpu.make_async_copy(self.src(c), self.dst(c), self.recv.at[0])

        def start(self):
            for i in (2, 1, 3) if nc == 4 else range(1, nc):
                self.copy(i).start()
            self.local().start()

        def wait(self):
            self.local().wait()
            for i in range(1, nc):
                frm = lax.rem(c - i + nc, nc)
                pltpu.make_async_remote_copy(
                    src_ref=self.src(c), dst_ref=self.dst(frm), send_sem=self.send.at[i],
                    recv_sem=self.recv.at[i], device_id=(d, frm), device_id_type=MESH,
                ).wait_recv()
                self.copy(i).wait_send()

    class Relay:
        def __init__(self, src, dst, send, recv):
            self.src, self.dst, self.send, self.recv = src, dst, send, recv
            self.far = chan_at(2)

        def copy(self, n, src, which, to):
            return pltpu.make_async_remote_copy(
                src_ref=src, dst_ref=self.dst(which), send_sem=self.send.at[n],
                recv_sem=self.recv.at[n], device_id=to, device_id_type=MESH,
            )

        def across(self, which):
            return self.copy(1, self.src(c), which, (d, self.far))

        def beside(self, which):
            return self.copy(2, self.src(c), which, partner)

        def onward(self, which):
            return self.copy(3, self.dst(self.far), which, partner)

        def local(self):
            return pltpu.make_async_copy(self.src(c), self.dst(c), self.recv.at[0])

        def start(self):
            self.across(c).start()
            self.beside(c).start()
            self.local().start()

        def forward(self):
            self.across(self.far).wait_recv()
            self.onward(self.far).start()

        def wait(self):
            self.local().wait()
            self.across(c).wait_send()
            self.beside(c).wait_send()
            self.onward(self.far).wait_send()
            self.beside(partner[1]).wait_recv()
            self.onward(lax.rem(partner[1] + 2, nc)).wait_recv()

    gs_sem, gr_sem = r.gather_send, r.gather_recv
    xs_sem, xr_sem = r.image_send, r.image_recv
    os_sem, or_sem = r.out_send, r.out_got

    def lanes_of(ref, width):
        return lambda s: ref.at[:, pl.ds(pl.multiple_of(s * width, LANES), width)]

    def rows_of(ref, size):
        return lambda s: ref.at[pl.ds(pl.multiple_of(s * size, size), size), :]

    def mids_of(ref, size):
        return lambda s: ref.at[:, pl.ds(pl.multiple_of(s * size, size), size), :]

    def taps_of(ref, size):
        return lambda s: ref.at[:, :, pl.ds(pl.multiple_of(s * size, size), size), :]

    whole = lambda ref: (lambda s: ref)
    ms = z.mids
    sem_rows = iter(range(13))

    def gathered(src, dst, kind=Relay):
        e = next(sem_rows)
        return kind(src, dst, gs_sem.at[e], gr_sem.at[e])

    ex = SimpleNamespace(
        vec=gathered(whole(r.vmine), lambda s: r.vv.at[s], Exchange),
        wsh=gathered(whole(given.wsh), lanes_of(r.wsh, z.cos)),
        cot=gathered(rows_of(given.cot, no), lanes_of(r.cot, z.cos), Exchange),
        blk={
            k: SimpleNamespace(
                wrt=gathered(whole(given.blk[k].wrt), rows_of(r.blk[k].wrt, ms)),
                wst=gathered(whole(given.blk[k].wst), taps_of(r.blk[k].wst, ms)),
                sq=gathered(whole(given.blk[k].sq), rows_of(r.blk[k].sq, ms)),
                ext=gathered(whole(given.blk[k].ext), mids_of(r.blk[k].ext, ms)),
                we=gathered(whole(given.blk[k].we), lanes_of(r.blk[k].we, z.cos)),
            )
            for k in (1, 2)
        },
        x=[],
    )
    nq = QUARTERS
    part = ni // nq
    for q in range(nq):
        ex.x.append(Exchange(
            lambda s, q=q: given.images.at[pl.ds(pl.multiple_of(s * ni + q * part, part), part), :],
            lambda s, q=q: r.x.at[
                pl.ds(q * part, part), pl.ds(pl.multiple_of(s * z.cis, LANES), z.cis)
            ],
            xs_sem.at[q],
            xr_sem.at[q],
        ))
    first_w, second_w = ex.blk[1], ex.blk[2]
    first_w.wrt.start()
    raw = [
        pltpu.make_async_copy(v, to, r.vsem.at[n]) for n, (v, to) in enumerate(zip(given.vec, r.vraw))
    ]
    for copy in raw:
        copy.start()
    ex.x[0].start()
    for q in range(1, nq):
        ex.x[q].start()
    row = 0
    for copy, v in zip(raw, r.vraw):
        copy.wait()
        rows, width = v.shape
        for k in range(rows):
            one = v[k : k + 1, :]
            if width < LANES:
                one = jnp.concatenate([one, one], axis=1)
            for t in range(one.shape[1] // LANES):
                r.vmine[row : row + 1, :] = one[:, t * LANES : (t + 1) * LANES]
                row += 1
    ex.vec.start()

    ss0, rs0, ss1, rs1 = r.s0s, r.s0r, r.s1s, r.s1r

    def put(k, row, v):
        for t in range(v.shape[1] // LANES):
            r.sync[k].sa[row + t : row + t + 1, :] = v[:, t * LANES : (t + 1) * LANES]

    def allreduce(k, used, meanwhile=None):
        sa, sb, st = r.sync[k].sa, r.sync[k].sb, r.sync[k].st
        rows = SYNC_ROWS[k]
        sc = r.slots[k % 2].at[:, :rows, :]
        if used < rows:
            sa[used:rows, :] = jnp.zeros((rows - used, LANES), F32)
        first = pltpu.make_async_remote_copy(
            src_ref=sa, dst_ref=sb, send_sem=ss0.at[0], recv_sem=rs0.at[k % 2],
            device_id=partner, device_id_type=MESH,
        )
        first.start()
        first.wait()
        pair = sa[...] + sb[...]
        sc[me] = pair

        def send(to):
            pltpu.make_async_remote_copy(
                src_ref=sc.at[me], dst_ref=sc.at[me], send_sem=ss1.at[0],
                recv_sem=rs1.at[k % 2], device_id=to, device_id_type=MESH,
            ).start()

        if ns <= 16:
            for to in far_first:
                send(to)
        else:

            def send_one(j, _):
                send(place(lax.rem(me + j, ns)))
                return 0

            lax.fori_loop(1, ns, send_one, 0)
        if meanwhile is not None:
            meanwhile()
        others = sc.at[pl.ds(0, ns - 1)]
        pltpu.make_async_remote_copy(
            src_ref=others, dst_ref=others, send_sem=ss1.at[0], recv_sem=rs1.at[k % 2],
            device_id=partner, device_id_type=MESH,
        ).wait()
        if ns <= 16:
            total = sc[0]
            for s in range(1, ns):
                total = total + sc[s]
        else:
            total = lax.fori_loop(1, ns, lambda s, t: t + sc[s], sc[0])
        st[...] = total

    def total(k, row, width):
        st = r.sync[k].st
        return jnp.concatenate(
            [st[row + t : row + t + 1, :] for t in range(width // LANES)], axis=1
        )

    sto = made.sto

    def keep(row, v):
        for t in range(v.shape[1] // LANES):
            sto[row + t : row + t + 1, :] = v[:, t * LANES : (t + 1) * LANES]

    half = lambda rows: lax.broadcasted_iota(jnp.int32, (rows, LANES), 0)
    groups = given.groups
    sides = [(so - 4 + 2 * groups[c * b + k]) for k in range(b)]
    areas = [(s * s).astype(F32) for s in sides]
    for k in range(b):
        def fill_out(t, _, k=k):
            p = half(2 * so) + t * (2 * so)
            ok = (lax.div(p, so) < sides[k]) & (lax.rem(p, so) < sides[k])
            r.mo[span(k * po + t * (2 * so), 2 * so), :] = jnp.where(ok, 1.0, 0.0)
            return 0

        lax.fori_loop(0, po // (2 * so), fill_out, 0)

        def fill_in(t, _, k=k):
            p = half(2 * si) + t * (2 * si)
            ok = (lax.div(p, si) < 2 * sides[k]) & (lax.rem(p, si) < 2 * sides[k])
            r.mi[span(k * pi_ + t * (2 * si), 2 * si), :] = jnp.where(ok, 1.0, 0.0).astype(BF16)
            return 0

        lax.fori_loop(0, pi_ // (2 * si), fill_in, 0)
    row8 = lax.broadcasted_iota(jnp.int32, (8, LANES), 0)
    live8 = jnp.where(row8 < b, 1.0, 0.0)
    inv_area = jnp.zeros((8, LANES), F32)
    for k in range(b):
        inv_area = jnp.where(row8 == k, 1.0 / jnp.full((8, LANES), areas[k], F32), inv_area)
    for ref in (r.blk[1].pm, r.blk[2].pm, r.ags):
        ref[...] = jnp.zeros_like(ref)

    pool_rows = part // 4

    def pool_matrix(out_axis):
        shape = (pool_rows, part) if out_axis == 0 else (part, pool_rows)
        o = lax.broadcasted_iota(jnp.int32, shape, out_axis)
        p = lax.broadcasted_iota(jnp.int32, shape, 1 - out_axis)
        row, col = lax.div(p, si), lax.rem(p, si)
        hit = (lax.div(row, 2) * so + lax.div(col, 2)) == o
        return jnp.where(hit, 0.25, 0.0).astype(BF16)

    low_half = lax.broadcasted_iota(jnp.int32, (1, LANES), 1) < z.mids
    vv = r.vv

    def v_mid(row):
        return jnp.concatenate(
            [
                jnp.where(low_half, vv[s, row : row + 1, :], vv[s + 1, row : row + 1, :])
                for s in range(0, nc, 2)
            ],
            axis=1,
        )

    def v_split(row):
        return jnp.concatenate([v_mid(row), v_mid(row + 1)], axis=1)

    def v_co(row):
        return jnp.concatenate(
            [
                vv[s, row + t : row + t + 1, :]
                for s in range(nc)
                for t in range(z.cos // LANES)
            ],
            axis=1,
        )

    def norm(k, row1, row2, width, inv_n, gain, bias):
        n = tiled(inv_n, width)
        mean = total(k, row1, width) * n
        inv = lax.rsqrt(total(k, row2, width) * n - mean * mean + EPSILON)
        scale = gain * inv
        return SimpleNamespace(mean=mean, inv=inv, gs=scale, sh=bias - mean * scale)

    def norm_grad(k, rowu, rowv, width, inv_n, nm):
        return norm_grad_of(total(k, rowu, width), total(k, rowv, width), width, inv_n, nm)

    def norm_grad_of(su, sv, width, inv_n, nm):
        n = tiled(inv_n, width)
        sux = nm.inv * (sv - nm.mean * su)
        t = sux * n
        return (
            su,
            sux,
            nm.gs * (su * n - nm.mean * nm.inv * t),
            nm.gs * nm.inv * t,
        )

    def loop(n, tile, body, init):
        def step(i, carry):
            return body(pl.multiple_of(i * tile, tile), carry)

        return lax.fori_loop(0, n // tile, step, init, unroll=2 if n // tile % 2 == 0 else 1)

    def zero8(width):
        return jnp.zeros((8, width), F32)

    def moments(ref, rows, width, tile):
        def body(at, carry):
            s1, s2 = carry
            v = ref[pl.ds(at, tile), :]
            mv = v * tiled(r.mo[pl.ds(at, tile), :], width)
            return s1 + sum8(mv), s2 + sum8(mv * v)

        s1, s2 = loop(rows, tile, body, (zero8(width), zero8(width)))
        return fold(s1), fold(s2)

    red1 = r.red1

    def row_pair(ref, i):
        return jnp.concatenate(
            [ref[t, pl.ds(i, 1)].reshape(2 * si, LANES) for t in range(mid // LANES)], axis=1
        )

    def phase_of(t, lead, p, q):
        return red1[t, lead, p, pl.ds(q, so, stride=2), :].reshape(4 * so, LANES)

    pool_m = pool_matrix(0)
    first_w.wrt.forward()
    first_w.wrt.wait()
    r1, r2 = zero8(mid), zero8(mid)
    for q in range(nq):
        ex.x[q].wait()
        xv = r.x[q * part : (q + 1) * part, :]
        lead = part // (2 * si)
        reduced = dot(xv, r.blk[1].wrt[...], NT)
        for t in range(mid // LANES):
            red1[t, q * lead : (q + 1) * lead] = reduced[:, t * LANES : (t + 1) * LANES].reshape(
                lead, 2, si, LANES
            )

        def red_sums(i, carry, q=q, lead=lead):
            s1, s2 = carry
            v = row_pair(red1, q * lead + i)
            m = r.mi[span((q * lead + i) * 2 * si, 2 * si), :].astype(F32)
            mv = v * tiled(m, mid)
            return s1 + sum8(mv), s2 + sum8(mv * v)

        r1, r2 = lax.fori_loop(0, lead, red_sums, (r1, r2))
    first_w.wst.start()
    put(0, 0, fold(r1))
    put(0, mid // LANES, fold(r2))
    at = 2 * mid // LANES
    local_area = areas[0]
    for k in range(1, b):
        local_area = local_area + areas[k]
    put(0, at, jnp.full((1, LANES), local_area, F32))

    def pooling():
        for q in range(nq):
            r.pool[q * pool_rows : (q + 1) * pool_rows, :] = dot(
                pool_m, r.x[q * part : (q + 1) * part, :]
            ).astype(BF16)

    allreduce(0, at + 1, pooling)
    ex.vec.wait()
    count = total(0, at, LANES)
    inv_out = 1.0 / count
    inv_in = 0.25 * inv_out
    vr1, vr2 = VEC_ROWS[1], VEC_ROWS[2]
    nred1 = norm(0, 0, mid // LANES, mid, inv_in, v_mid(vr1.rg), v_mid(vr1.rb))
    lane16 = lax.rem(lax.broadcasted_iota(jnp.int32, (4 * so, mid), 0), so)
    not_first = lane16 > 0
    not_last = lane16 < so - 1

    def im_put(im, at, w, di, dj, shift):
        tap = di * 3 + dj
        low = w.astype(BF16)
        for g in range(2):
            im[g, pl.ds(pl.multiple_of(at + so + shift * so, so), 4 * so), tap * grp : (tap + 1) * grp] = (
                low[:, g * grp : (g + 1) * grp]
            )

    def im_zero(im, di, last):
        for k in range(b):
            row = so + k * po + (po - so if last else 0)
            for g in range(2):
                im[g, row : row + so, di * 3 * grp : (di + 1) * 3 * grp] = jnp.zeros(
                    (so, 3 * grp), BF16
                )

    im1 = r.blk[1].im

    def build1(i, _):
        at = pl.multiple_of(i * 4 * so, 4 * so)
        m = tiled(r.mo[pl.ds(at, 4 * so), :], mid)
        for p in range(2):
            for q in range(2):
                v = jnp.concatenate(
                    [phase_of(t, pl.ds(i * 4, 4), p, q) for t in range(mid // LANES)], axis=1
                )
                w = silu(v * nred1.gs + nred1.sh) * m
                for dj in ((1,) if q == 0 else (2, 0)):
                    wj = w
                    if dj == 0:
                        wj = jnp.where(not_first, pltpu.roll(w, 1, 0), 0.0)
                    for di in ((1,) if p == 0 else (2, 0)):
                        im_put(im1, at, wj, di, dj, 1 if di == 0 else 0)
        return 0

    for e in (first_w.sq, first_w.ext, first_w.we, ex.wsh):
        e.start()
    lax.fori_loop(0, no // (4 * so), build1, 0)
    first_w.wst.forward()
    im_zero(im1, 0, False)

    def split_weights(k, g):
        return jnp.concatenate([r.blk[k].wst[t, g] for t in range(TAPS)], axis=1)

    def split_conv(k):
        ex.blk[k].wst.wait()
        for g in range(2):
            r.blk[k].sp[:, g * mid : (g + 1) * mid] = dot(
                r.blk[k].im[g, so : so + no, :], split_weights(k, g), NT
            )
        return moments(r.blk[k].sp, no, 2 * mid, 32)

    class Meeting:
        def __init__(self, k):
            blk = r.blk[k]
            self.own, self.group, self.ms, self.mr = blk.own, blk.group, blk.ms, blk.mr

        def near(self, to, src):
            return pltpu.make_async_remote_copy(
                src_ref=self.own, dst_ref=r.met.at[src], send_sem=self.ms.at[0],
                recv_sem=self.mr.at[0], device_id=(d, to), device_id_type=MESH,
            )

        def far(self, to):
            return pltpu.make_async_remote_copy(
                src_ref=self.group, dst_ref=r.all.at[d], send_sem=self.ms.at[1],
                recv_sem=self.mr.at[1], device_id=(to, c), device_id_type=MESH,
            )

        def wait(self, ref, n):
            some = ref.at[pl.ds(0, n)]
            pltpu.make_async_remote_copy(
                src_ref=some, dst_ref=some, send_sem=self.ms.at[0 if n == nc - 1 else 1],
                recv_sem=self.mr.at[0 if n == nc - 1 else 1], device_id=partner,
                device_id_type=MESH,
            ).wait()

        def start(self):
            for n in range(1, nc):
                self.near(chan_at(n), c).start()

        def gather(self):
            self.wait(r.met, nc - 1)
            r.met[c] = self.own[...]
            for kind in range(KINDS):
                for s in range(nc):
                    self.group[kind, s * b : (s + 1) * b, :] = r.met[
                        s, kind * b : (kind + 1) * b, :
                    ]

        def send(self):
            def step(j, _):
                self.far(lax.rem(d + j, nd)).start()
                return 0

            lax.fori_loop(1, nd, step, 0)

        def finish(self):
            self.wait(r.all, nd - 1)
            r.all[d] = self.group[...]

    meet = {k: Meeting(k) for k in (1, 2)}

    def attention_forward(k, vr, sync, fills):
        s1, s2 = split_conv(k)
        put(sync, 0, s1)
        put(sync, 4, s2)
        allreduce(sync, 8, fills[0])
        nsplit = norm(sync, 0, 4, 2 * mid, inv_out, v_split(vr.sg), v_split(vr.sb))
        sp, sa, pm = r.blk[k].sp, r.blk[k].sa, r.blk[k].pm
        for img in range(b):
            def act(at, carry, img=img):
                s, ds, dv = carry
                rows = pl.ds(pl.multiple_of(at + img * po, 32), 32)
                raw = sp[rows, :]
                v = raw * nsplit.gs + nsplit.sh
                q = sigmoid(v)
                qm = q * tiled(r.mo[rows, :], 2 * mid)
                slope = qm * (1.0 + v * (1.0 - q))
                v = v * qm
                sa[rows, :] = v
                return s + sum8(v), ds + sum8(slope), dv + sum8(slope * raw)

            zero = zero8(2 * mid)
            s, ds, dv = (fold(v) for v in loop(po, 32, act, (zero, zero, zero)))
            own = r.blk[k].own
            for t in range(4):
                lanes = slice(t * LANES, (t + 1) * LANES)
                for kind, v in ((t, ds), (t + 4, dv)):
                    at = kind * b + img
                    own[at : at + 1, :] = v[:, lanes] * inv_area[img : img + 1, :]
            pm[img : img + 1, :] = (s[:, :mid] + s[:, mid:]) * tiled(inv_area[img : img + 1, :], mid)
        ex.blk[k].sq.wait()
        squeezed = dot_exact(pm[...], r.blk[k].sq[...])
        put(sync + 1, 0, fold(squeezed))
        put(sync + 1, 1, fold(squeezed * squeezed))
        put(sync + 1, 2, fold(pm[...]))
        allreduce(sync + 1, 4, fills[1])
        inv_images = jnp.full((1, LANES), 1.0 / (b * nc * nd), F32)
        natt = norm(
            sync + 1, 0, 1, att, inv_images, vv[0, vr.qg : vr.qg + 1, :],
            vv[0, vr.qb : vr.qb + 1, :],
        )
        xhat = (squeezed - natt.mean) * natt.inv
        centred = pm[...] - total(sync + 1, 2, mid) * tiled(inv_images, mid)
        r.blk[k].own[8 * b : 9 * b, :] = xhat[:b, :]
        meet[k].start()
        pre = squeezed * natt.gs + natt.sh
        excited = silu(pre) * live8
        ex.blk[k].ext.wait()
        halves = []
        for g in range(2):
            bias = v_mid(vr.xb + g)
            halves.append(dot_exact(excited, r.blk[k].ext[g], NT) + bias)
        top = jnp.maximum(halves[0], halves[1])
        e0, e1 = jnp.exp(halves[0] - top), jnp.exp(halves[1] - top)
        whole_sum = e0 + e1
        at_ref = r.blk[k].att
        at_ref[:, :mid] = e0 / whole_sum
        at_ref[:, mid:] = e1 / whole_sum
        for img in range(b):
            def mix(at, _, img=img):
                rows = pl.ds(pl.multiple_of(at + img * po, 32), 32)
                v = sa[rows, :] * at_ref[img : img + 1, :]
                r.blk[k].mix[rows, :] = (v[:, :mid] + v[:, mid:]).astype(BF16)
                return 0

            loop(po, 32, mix, 0)
        ex.blk[k].we.wait()
        for n0 in range(0, co, 256):
            r.blk[k].exp[:, n0 : n0 + 256] = dot(r.blk[k].mix[...], r.blk[k].we[:, n0 : n0 + 256])
        s1, s2 = moments(r.blk[k].exp, no, co, 16)
        put(sync + 2, 0, s1)
        put(sync + 2, co // LANES, s2)
        if k == 1:
            for n, v in enumerate(short_sums):
                put(sync + 2, (2 + n) * co // LANES, v)
        allreduce(sync + 2, (4 if k == 1 else 2) * co // LANES, fills[2])
        nexp = norm(sync + 2, 0, co // LANES, co, inv_out, v_co(vr.eg), v_co(vr.eb))
        return SimpleNamespace(nsplit=nsplit, natt=natt, xhat=xhat, pre=pre, excited=excited, nexp=nexp, centred=centred)

    short_sums = []

    def shortcut_forward():
        ex.wsh.wait()
        for n0 in range(0, co, 256):
            r.short[:, n0 : n0 + 256] = dot(r.pool[...], r.wsh[:, n0 : n0 + 256])
        short_sums.extend(moments(r.short, no, co, 16))

    def forward_first():
        for e in (first_w.sq, first_w.ext, first_w.we):
            e.forward()
        second_w.wrt.start()

    def between():
        ex.wsh.forward()
        second_w.wst.start()
        shortcut_forward()

    def forward_second():
        meet[1].gather()
        second_w.wrt.forward()
        for e in (second_w.sq, second_w.ext, second_w.we):
            e.start()

    f1 = attention_forward(1, vr1, 1, (forward_first, between, forward_second))
    nshort = norm(
        3, 2 * co // LANES, 3 * co // LANES, co, inv_out, v_co(vr1.hg), v_co(vr1.hb)
    )

    def summed1(rows):
        return (
            r.blk[1].exp[rows, :] * f1.nexp.gs
            + f1.nexp.sh
            + r.short[rows, :] * nshort.gs
            + nshort.sh
        )

    def hidden(at, _):
        rows = pl.ds(at, 16)
        r.h[rows, :] = (silu(summed1(rows)) * tiled(r.mo[rows, :], co)).astype(BF16)
        return 0

    loop(no, 16, hidden, 0)

    ex.blk[2].wrt.wait()
    r.red2[...] = dot(r.h[...], r.blk[2].wrt[...], NT)
    s1, s2 = moments(r.red2, no, mid, 64)
    put(4, 0, s1)
    put(4, 2, s2)

    def forward_rest():
        ex.cot.start()
        second_w.wst.forward()
        for e in (second_w.sq, second_w.ext, second_w.we):
            e.forward()

    allreduce(4, 4, forward_rest)
    nred2 = norm(4, 0, 2, mid, inv_out, v_mid(vr2.rg), v_mid(vr2.rb))
    im2 = r.blk[2].im

    def build2(i, _):
        at = pl.multiple_of(i * 4 * so, 4 * so)
        m = tiled(r.mo[pl.ds(at, 4 * so), :], mid)
        w = silu(r.red2[pl.ds(at, 4 * so), :] * nred2.gs + nred2.sh) * m
        for dj in range(3):
            wj = w
            if dj == 0:
                wj = jnp.where(not_first, pltpu.roll(w, 1, 0), 0.0)
            if dj == 2:
                wj = jnp.where(not_last, pltpu.roll(w, 4 * so - 1, 0), 0.0)
            for di in range(3):
                im_put(im2, at, wj, di, dj, 1 - di)
        return 0

    lax.fori_loop(0, no // (4 * so), build2, 0)
    im_zero(im2, 0, False)
    im_zero(im2, 2, True)
    f2 = attention_forward(2, vr2, 5, (None, None, meet[2].gather))
    meet[2].send()

    ex.cot.wait()

    def finish(at, carry):
        su, sv = carry
        rows = pl.ds(at, 16)
        m = tiled(r.mo[rows, :], co)
        v = r.blk[2].exp[rows, :]
        s = v * f2.nexp.gs + f2.nexp.sh + r.h[rows, :].astype(F32)
        q = sigmoid(s)
        u = r.cot[rows, :].astype(F32) * m * (q * (1.0 + s * (1.0 - q)))
        r.cot[rows, :] = (s * q * m).astype(BF16)
        r.g[rows, :] = u
        return su + sum8(u), sv + sum8(u * v)

    su, sv = loop(no, 16, finish, (zero8(co), zero8(co)))
    out_part = no // OUT_PARTS
    out_ex = [
        Exchange(
            lambda s, n=n: r.cot.at[
                pl.ds(n * out_part, out_part), pl.ds(pl.multiple_of(s * z.cos, LANES), z.cos)
            ],
            lambda s, n=n: made.out.at[
                pl.ds(pl.multiple_of(s * no + n * out_part, out_part), out_part), :
            ],
            os_sem.at[n],
            or_sem.at[n],
        )
        for n in range(OUT_PARTS)
    ]
    put(8, 0, fold(su))
    put(8, co // LANES, fold(sv))
    allreduce(8, 2 * co // LANES)
    out_ex[0].start()

    def pack_rows(k, name, skip, v):
        group, at = z.lay[(k, name)]
        at, share = at + skip * z.mids, z.mids
        for s in range(nc):
            for t in range(v.shape[1] // LANES):
                r.group[group].pk[s // 2, s % 2, at + t * share : at + (t + 1) * share, :] = v[
                    s * share : (s + 1) * share, t * LANES : (t + 1) * LANES
                ].astype(BF16)

    def pack_lanes(k, name, s, v):
        group, at = z.lay[(k, name)]
        rows = v.shape[0]
        for t in range(v.shape[1] // LANES):
            r.group[group].pk[s // 2, s % 2, at + t * rows : at + (t + 1) * rows, :] = v[
                :, t * LANES : (t + 1) * LANES
            ].astype(BF16)

    class Reduction:
        def __init__(self, group):
            own = r.group[group]
            self.pk, self.r1, self.r2, self.r3 = own.pk, own.r1, own.r2, own.r3
            self.rows = z.rows[group]
            self.piece = self.rows // z.near
            self.r4 = own.r4
            self.near, self.mine = lax.rem(d, z.near), lax.div(d, z.near)
            self.res = made.res[group]
            self.sems = [own.q1, own.q2, own.q3s, own.q3r, own.q4s, own.q4r, own.q5s, own.q5r]
            self.across = lax.div(c, 2)

        def piece_at(self, n):
            return pl.ds(pl.multiple_of(n * self.piece, 16), self.piece)

        def copy1(self):
            return pltpu.make_async_remote_copy(
                src_ref=self.pk.at[:, 1 - odd], dst_ref=self.r1, send_sem=self.sems[0].at[0],
                recv_sem=self.sems[0].at[1], device_id=partner, device_id_type=MESH,
            )

        def copy2(self):
            return pltpu.make_async_remote_copy(
                src_ref=self.pk.at[1 - self.across, odd], dst_ref=self.r2,
                send_sem=self.sems[1].at[0], recv_sem=self.sems[1].at[1],
                device_id=(d, chan_at(2)), device_id_type=MESH,
            )

        def at_near(self, n):
            return (self.mine * z.near + n, c)

        def copy3(self, to, src):
            return pltpu.make_async_remote_copy(
                src_ref=self.pk.at[self.across, odd, self.piece_at(to), :],
                dst_ref=self.r3.at[src], send_sem=self.sems[2].at[to],
                recv_sem=self.sems[3].at[src], device_id=self.at_near(to), device_id_type=MESH,
            )

        def copy4(self, to, src):
            return pltpu.make_async_remote_copy(
                src_ref=self.r3.at[self.near], dst_ref=self.res.at[self.piece_at(src), :],
                send_sem=self.sems[4].at[to], recv_sem=self.sems[5].at[src],
                device_id=self.at_near(to), device_id_type=MESH,
            )

        def copy5(self, to, src):
            return pltpu.make_async_remote_copy(
                src_ref=self.r4.at[self.mine], dst_ref=self.r4.at[src],
                send_sem=self.sems[6].at[to], recv_sem=self.sems[7].at[src],
                device_id=(to * z.near + self.near, c), device_id_type=MESH,
            )

        def local4(self):
            return pltpu.make_async_copy(
                self.r3.at[self.near], self.res.at[self.piece_at(self.near), :],
                self.sems[5].at[self.near],
            )

        def others(self, body, me, n):
            def step(j, _):
                body(lax.rem(me + j, n), lax.rem(me - j + n, n))
                return 0

            lax.fori_loop(1, n, step, 0)

        def total(self, slots, n, to):
            tile = self.piece if self.piece <= 256 else tile_of(self.piece)

            def body(at, _):
                rows = pl.ds(at, tile)
                t = slots[0, rows, :].astype(F32)
                for k in range(1, n):
                    t = t + slots[k, rows, :].astype(F32)
                to[rows, :] = t.astype(BF16)
                return 0

            loop(self.piece, tile, body, 0)

        def add(self, which, other):
            tile = tile_of(self.rows)

            def body(at, _):
                rows = pl.ds(at, tile)
                self.pk[which, odd, rows, :] = (
                    self.pk[which, odd, rows, :].astype(F32) + other(rows).astype(F32)
                ).astype(BF16)
                return 0

            loop(self.rows, tile, body, 0)

        def step1(self):
            self.copy1().start()

        def ready2(self):
            self.copy1().wait()
            for which in (1 - self.across, self.across):
                self.add(which, lambda rows, which=which: self.r1[which, rows, :])

        def step2(self):
            self.copy2().start()

        def ready3(self):
            self.copy2().wait()
            self.add(self.across, lambda rows: self.r2[rows, :])

        def step3(self):
            self.others(lambda to, _: self.copy3(to, self.near).start(), self.near, z.near)

        def ready4(self):
            self.r3[self.near] = self.pk[self.across, odd, self.piece_at(self.near), :]

            def arrive(to, src):
                self.copy3(to, self.near).wait_send()
                self.copy3(src, src).wait_recv()

            self.others(arrive, self.near, z.near)
            mine = self.r3.at[self.near]
            if z.far == 1:
                self.total(self.r3, z.near, mine)
            else:
                self.total(self.r3, z.near, self.r4.at[self.mine])
                self.others(lambda to, _: self.copy5(to, self.mine).start(), self.mine, z.far)

                def arrive_far(to, src):
                    self.copy5(to, self.mine).wait_send()
                    self.copy5(src, src).wait_recv()

                self.others(arrive_far, self.mine, z.far)
                self.total(self.r4, z.far, mine)

        def step4(self):
            self.local4().start()
            self.others(lambda to, _: self.copy4(to, self.near).start(), self.near, z.near)

        def finish(self):
            self.local4().wait()

            def arrive(to, src):
                self.copy4(to, self.near).wait_send()
                self.copy4(src, src).wait_recv()

            self.others(arrive, self.near, z.near)

    class SplitReduction(Reduction):
        def __init__(self, group):
            super().__init__(group)
            self.ry, self.q6 = r.group[group].ry, r.group[group].q6
            self.half = self.rows // 2
            self.par, self.far_at = lax.rem(self.near, 2), lax.div(self.near, 2)
            self.quad = z.near // 2
            self.mate = self.at_near(self.near + 1 - 2 * self.par)

        def half_at(self, par):
            return pl.ds(pl.multiple_of(par * self.half, 16), self.half)

        def piece_at(self, n):
            at = lax.rem(n, 2) * self.half + lax.div(n, 2) * self.piece
            return pl.ds(pl.multiple_of(at, 16), self.piece)

        def copy_half(self):
            return pltpu.make_async_remote_copy(
                src_ref=self.pk.at[self.across, odd, self.half_at(1 - self.par), :],
                dst_ref=self.ry, send_sem=self.q6.at[0], recv_sem=self.q6.at[1],
                device_id=self.mate, device_id_type=MESH,
            )

        def copy_back(self, par):
            rows = self.half_at(par)
            return pltpu.make_async_remote_copy(
                src_ref=self.res.at[rows, :], dst_ref=self.res.at[rows, :],
                send_sem=self.q6.at[2], recv_sem=self.q6.at[3],
                device_id=self.mate, device_id_type=MESH,
            )

        def slot3(self, to, src):
            n = 2 * to + self.par
            return pltpu.make_async_remote_copy(
                src_ref=self.pk.at[self.across, odd, self.piece_at(n), :],
                dst_ref=self.r3.at[src], send_sem=self.sems[2].at[to],
                recv_sem=self.sems[3].at[src], device_id=self.at_near(n), device_id_type=MESH,
            )

        def slot4(self, to, src):
            return pltpu.make_async_remote_copy(
                src_ref=self.r3.at[self.far_at],
                dst_ref=self.res.at[self.piece_at(2 * src + self.par), :],
                send_sem=self.sems[4].at[to], recv_sem=self.sems[5].at[src],
                device_id=self.at_near(2 * to + self.par), device_id_type=MESH,
            )

        def local5(self):
            return pltpu.make_async_copy(
                self.r3.at[self.far_at], self.res.at[self.piece_at(self.near), :],
                self.sems[5].at[self.far_at],
            )

        def step3(self):
            self.copy_half().start()

        def ready4(self):
            self.copy_half().wait()
            tile = tile_of(self.half)

            def body(at, _):
                rows = pl.ds(pl.multiple_of(self.par * self.half + at, 16), tile)
                self.pk[self.across, odd, rows, :] = (
                    self.pk[self.across, odd, rows, :].astype(F32)
                    + self.ry[pl.ds(at, tile), :].astype(F32)
                ).astype(BF16)
                return 0

            loop(self.half, tile, body, 0)

        def step4(self):
            self.others(lambda to, _: self.slot3(to, self.far_at).start(), self.far_at, self.quad)

        def ready5(self):
            self.r3[self.far_at] = self.pk[self.across, odd, self.piece_at(self.near), :]

            def arrive(to, src):
                self.slot3(to, self.far_at).wait_send()
                self.slot3(src, src).wait_recv()

            self.others(arrive, self.far_at, self.quad)
            mine = self.r3.at[self.far_at]
            if z.far == 1:
                self.total(self.r3, self.quad, mine)
            else:
                self.total(self.r3, self.quad, self.r4.at[self.mine])
                self.others(lambda to, _: self.copy5(to, self.mine).start(), self.mine, z.far)

                def arrive_far(to, src):
                    self.copy5(to, self.mine).wait_send()
                    self.copy5(src, src).wait_recv()

                self.others(arrive_far, self.mine, z.far)
                self.total(self.r4, z.far, mine)

        def step5(self):
            self.local5().start()
            self.others(lambda to, _: self.slot4(to, self.far_at).start(), self.far_at, self.quad)

        def ready6(self):
            self.local5().wait()

            def arrive(to, src):
                self.slot4(to, self.far_at).wait_send()
                self.slot4(src, src).wait_recv()

            self.others(arrive, self.far_at, self.quad)

        def step6(self):
            self.copy_back(self.par).start()

        def finish(self):
            self.copy_back(self.par).wait_send()
            self.copy_back(1 - self.par).wait_recv()

    sums_of = {group: (SplitReduction if group in SPLIT_GROUPS else Reduction)(group) for group in GROUPS}

    def attention_backward(k, f, sync):
        srow = STO_ROWS[k]
        nexp, nsplit, natt = f.nexp, f.nsplit, f.natt
        first = k == 1
        cw = co // LANES
        su, sux, ea, eb = norm_grad(sync, 0, cw, co, inv_out, nexp)
        keep(srow.eb, su)
        keep(srow.eg, sux)
        if first:
            _, suxh, ha, hb = norm_grad(sync, 0, 2 * cw, co, inv_out, nshort)
            keep(srow.hg, suxh)

        def expand_grad(at, _):
            rows = pl.ds(at, 16)
            m = tiled(r.mo[rows, :], co)
            u = r.g[rows, :]
            r.eg[rows, :] = (nexp.gs * u - m * (ea + eb * r.blk[k].exp[rows, :])).astype(BF16)
            if first:
                r.shg[rows, :] = (
                    nshort.gs * u - m * (ha + hb * r.short[rows, :])
                ).astype(BF16)
            return 0

        loop(no, 16, expand_grad, 0)
        r.mg[...] = dot(r.eg[...], r.blk[k].we[...], NT)
        sa = r.blk[k].sa
        for img in range(b):
            def att_grad(at, s, img=img):
                rows = pl.ds(pl.multiple_of(at + img * po, 32), 32)
                return s + sum8(sa[rows, :] * tiled_pair(r.mg[rows, :]))

            r.ags[img : img + 1, :] = fold(loop(po, 32, att_grad, zero8(2 * mid)))
        ags, at_ref = r.ags, r.blk[k].att
        a0, a1 = at_ref[:, :mid], at_ref[:, mid:]
        g0, g1 = ags[:, :mid], ags[:, mid:]
        mean = a0 * g0 + a1 * g1
        l0, l1 = a0 * (g0 - mean), a1 * (g1 - mean)
        ext = r.blk[k].ext
        excited_grad = dot_exact(l0, ext[0]) + dot_exact(l1, ext[1])
        au = excited_grad * silu_slope(f.pre)
        sq = r.blk[k].sq
        sp = r.blk[k].sp
        r.mgr[...] = dot_exact(natt.gs * au * live8, sq[...], NT) * tiled(inv_area, mid)
        carry = (zero8(2 * mid), zero8(2 * mid))
        for img in range(b):
            def split_up(at, carry, img=img):
                s1, s2 = carry
                rows = pl.ds(pl.multiple_of(at + img * po, 32), 32)
                v = sp[rows, :]
                slope = tiled(r.mo[rows, :], 2 * mid) * silu_slope(v * nsplit.gs + nsplit.sh)
                r.su[rows, :] = slope
                u = slope * (
                    tiled_pair(r.mg[rows, :]) * at_ref[img : img + 1, :]
                    + tiled_pair(r.mgr[img : img + 1, :])
                )
                return s1 + sum8(u), s2 + sum8(u * v)

            carry = loop(po, 32, split_up, carry)
        put(sync + 1, 0, fold(au))
        put(sync + 1, 1, fold(au * f.xhat))
        put(sync + 1, 2, fold(l0))
        put(sync + 1, 4, fold(l1))
        put(sync + 1, 6, fold(carry[0]))
        put(sync + 1, 10, fold(carry[1]))

        def matrices():
            r.mixt[...] = jnp.transpose(r.blk[k].mix[...])
            for s in range(nc):
                share = slice(s * z.cos, (s + 1) * z.cos)
                pack_lanes(k, EXPAND, s, dot(r.mixt[...], r.eg[:, share]))
            pack_rows(k, EXCITE, 0, dot_exact(l0, f.excited, TN))
            pack_rows(k, EXCITE, 1, dot_exact(l1, f.excited, TN))
            if first:
                r.sgt[...] = jnp.transpose(r.pool[...])
                for s in range(nc):
                    share = slice(s * z.cos, (s + 1) * z.cos)
                    pack_lanes(k, SHORTCUT, s, dot(r.sgt[...], r.shg[:, share]))
                sums_of[2].step1()
                sums_of[5].ready2()
                sums_of[0].ready4()
                sums_of[1].ready3()
                r.pg[...] = dot(r.shg[...], r.wsh[...], NT).astype(BF16)

            else:
                sums_of[0].step1()

        if first:
            meet[1].finish()
        allreduce(sync + 1, 14, matrices)
        if first:
            sums_of[5].step2()
            sums_of[2].ready2()
            sums_of[2].step2()
            sums_of[0].step4()
            sums_of[1].step3()
        else:
            out_ex[1].start()
            out_ex[2].start()
        inv_images = 1.0 / (b * nc * nd)
        su, sux = total(sync + 1, 0, att), total(sync + 1, 1, att)
        keep(srow.qb, su)
        keep(srow.qg, sux)
        keep(srow.xb, total(sync + 1, 2, 2 * mid))
        su, sux = su * inv_images, sux * inv_images
        sb = natt.gs * (au - su - f.xhat * sux) * live8
        r.mgr[...] = dot_exact(sb, sq[...], NT) * tiled(inv_area, mid)
        seen = nd * 8
        off = dot_exact(natt.gs * (su + r.all[:, 8].reshape(seen, LANES) * sux), sq[...], NT)
        taken = []
        for kind in range(8):
            lanes = slice(kind % 2 * LANES, (kind % 2 + 1) * LANES)
            taken.append(fold(sum8(off[:, lanes] * r.all[:, kind].reshape(seen, LANES))))
        su = total(sync + 1, 6, 2 * mid) - jnp.concatenate(taken[:4], axis=1)
        sv = total(sync + 1, 10, 2 * mid) - jnp.concatenate(taken[4:], axis=1)
        su, sux, ca, cb = norm_grad_of(su, sv, 2 * mid, inv_out, nsplit)
        keep(srow.sb, su)
        keep(srow.sg, sux)

        def split_grad(at, _, img=0):
            rows = pl.ds(pl.multiple_of(at + img * po, 32), 32)
            m = tiled(r.mo[rows, :], 2 * mid)
            u = r.su[rows, :] * (
                tiled_pair(r.mg[rows, :]) * at_ref[img : img + 1, :]
                + tiled_pair(r.mgr[img : img + 1, :])
            )
            r.sgb[rows, :] = (nsplit.gs * u - m * (ca + cb * sp[rows, :])).astype(BF16)
            return 0

        for img in range(b):
            loop(po, 32, functools.partial(split_grad, img=img), 0)

        def squeeze_matrix():
            pack_rows(k, SQUEEZE, 0, dot_exact(f.centred, sb, TN))

        return squeeze_matrix

    def tiled_pair(v):
        return jnp.concatenate([v, v], axis=1)

    def split_matrix(k):
        r.sgt[...] = jnp.transpose(r.sgb[...])
        for g in range(2):
            for t in range(3):
                v = dot(
                    r.sgt[g * mid : (g + 1) * mid, :],
                    r.blk[k].im[g, so : so + no, 3 * t * grp : 3 * (t + 1) * grp],
                )
                for u in range(3):
                    pack_rows(
                        k, SPLIT, (3 * t + u) * 2 + g, v[:, u * grp : (u + 1) * grp]
                    )

    dcol = r.dcol
    dcol[:so, :] = jnp.zeros((so, kk), F32)
    dcol[so + po :, :] = jnp.zeros((so, kk), F32)

    def columns(k, img, g):
        dcol[so : so + po, :] = dot(
            r.sgb[img * po : (img + 1) * po, g * mid : (g + 1) * mid], split_weights(k, g)
        )

    tile = 4 * so
    first_g, last_g = not_first[:, :grp], not_last[:, :grp]

    def tap(at, di, dj, shift):
        t = di * 3 + dj
        return dcol[pl.ds(pl.multiple_of(at + so - shift * so, so), tile), t * grp : (t + 1) * grp]

    def from_left(v):
        return jnp.where(first_g, pltpu.roll(v, 1, 0), 0.0)

    def from_right(v):
        return jnp.where(last_g, pltpu.roll(v, tile - 1, 0), 0.0)

    meet[2].finish()
    squeeze_matrix2 = attention_backward(2, f2, 8)
    sums = []
    for g in range(2):
        carry = (zero8(grp), zero8(grp))
        lanes = slice(g * grp, (g + 1) * grp)
        for img in range(b):
            columns(2, img, g)

            def back2(at, carry, img=img, g=g, lanes=lanes):
                s1, s2 = carry
                cols = [
                    tap(at, 0, dj, -1) + tap(at, 1, dj, 0) + tap(at, 2, dj, 1) for dj in range(3)
                ]
                grad = cols[1] + from_right(cols[0]) + from_left(cols[2])
                rows = pl.ds(pl.multiple_of(at + img * po, tile), tile)
                v = r.red2[rows, lanes]
                u = (
                    grad
                    * tiled(r.mo[rows, :], grp)
                    * silu_slope(v * nred2.gs[:, lanes] + nred2.sh[:, lanes])
                )
                r.u2[rows, lanes] = u
                return s1 + sum8(u), s2 + sum8(u * v)

            carry = loop(po, tile, back2, carry)
        sums.append(carry)
    put(10, 0, jnp.concatenate([fold(s[0]) for s in sums], axis=1))
    put(10, 2, jnp.concatenate([fold(s[1]) for s in sums], axis=1))
    def split_matrix2():
        split_matrix(2)
        squeeze_matrix2()
        sums_of[1].step1()
        sums_of[0].ready2()

    allreduce(10, 4, split_matrix2)
    sums_of[0].step2()
    out_ex[3].start()
    meet[1].send()
    su, sux, ca, cb = norm_grad(10, 0, 2, mid, inv_out, nred2)
    keep(STO_ROWS[2].rb, su)
    keep(STO_ROWS[2].rg, sux)

    def reduce_grad2(at, _):
        rows = pl.ds(at, 64)
        m = tiled(r.mo[rows, :], mid)
        r.rg1[rows, :] = (
            nred2.gs * r.u2[rows, :] - m * (ca + cb * r.red2[rows, :])
        ).astype(BF16)
        return 0

    loop(no, 64, reduce_grad2, 0)
    for n0 in range(0, co, 256):
        cols = slice(n0, n0 + 256)
        r.g[:, cols] = r.g[:, cols] + dot(r.rg1[:no, :], r.blk[2].wrt[:, cols])

    def first_up(at, carry):
        s1, s2, s3 = carry
        rows = pl.ds(at, 16)
        u = r.g[rows, :] * tiled(r.mo[rows, :], co) * silu_slope(summed1(rows))
        r.g[rows, :] = u
        return (
            s1 + sum8(u),
            s2 + sum8(u * r.blk[1].exp[rows, :]),
            s3 + sum8(u * r.short[rows, :]),
        )

    s1, s2, s3 = loop(no, 16, first_up, (zero8(co), zero8(co), zero8(co)))
    put(11, 0, fold(s1))
    put(11, co // LANES, fold(s2))
    put(11, 2 * co // LANES, fold(s3))

    def reduce_matrix2():
        r.rgt[:, :no] = jnp.transpose(r.rg1[:no, :])
        for n0 in range(0, co, 256):
            pack_rows(2, REDUCE, n0 // LANES, dot(r.rgt[:, :no], r.h[:, n0 : n0 + 256]))
        sums_of[5].step1()
        sums_of[1].ready2()
        sums_of[0].ready3()

    allreduce(11, 3 * co // LANES, reduce_matrix2)
    sums_of[1].step2()
    sums_of[0].step3()

    squeeze_matrix1 = attention_backward(1, f1, 11)
    split_matrix(1)
    squeeze_matrix1()
    sums_of[3].step1()
    sums = []
    for g in range(2):
        carry = (zero8(grp), zero8(grp))
        lanes = slice(g * grp, (g + 1) * grp)
        for img in range(b):
            columns(1, img, g)

            def back1(at, carry, img=img, g=g, lanes=lanes):
                s1, s2 = carry
                rows = pl.ds(pl.multiple_of(at + img * po, tile), tile)
                m = tiled(r.mo[rows, :], grp)
                lead = pl.ds(pl.multiple_of(lax.div(at, so) + img * so, 4), 4)
                for p in range(2):
                    for q in range(2):
                        def col(dj):
                            if p == 0:
                                return tap(at, 1, dj, 0)
                            return tap(at, 0, dj, -1) + tap(at, 2, dj, 0)

                        grad = col(1) if q == 0 else col(2) + from_right(col(0))
                        v = phase_of(g, lead, p, q)
                        u = grad * m * silu_slope(v * nred1.gs[:, lanes] + nred1.sh[:, lanes])
                        r.u1[g, lead, p, pl.ds(q, so, stride=2), :] = u.reshape(4, so, grp)
                        s1, s2 = s1 + sum8(u), s2 + sum8(u * v)
                return s1, s2

            carry = loop(po, tile, back1, carry)
        sums.append(carry)
    put(13, 0, jnp.concatenate([fold(s[0]) for s in sums], axis=1))
    put(13, 2, jnp.concatenate([fold(s[1]) for s in sums], axis=1))

    def behind_last():
        sums_of[3].ready2()
        sums_of[3].step2()
        sums_of[1].ready4()

    allreduce(13, 4, behind_last)
    sums_of[1].step4()
    su, sux, ca, cb = norm_grad(13, 0, 2, mid, inv_in, nred1)
    keep(STO_ROWS[1].rb, su)
    keep(STO_ROWS[1].rg, sux)

    def reduce_grad1(i, _):
        rows = pl.ds(pl.multiple_of(i * 2 * si, 2 * si), 2 * si)
        m = tiled(r.mi[rows, :].astype(F32), mid)
        u, v = row_pair(r.u1, i), row_pair(red1, i)
        r.rg1[rows, :] = (nred1.gs * u - m * (ca + cb * v)).astype(BF16)
        return 0

    spread = pool_matrix(1)
    grads = (r.h, r.eg)
    last = []

    def send_quarter(q):
        rows = slice(q * part, (q + 1) * part)
        m = tiled(r.mi[rows, :].astype(F32), 256)
        for n0 in range(0, ci, 256):
            cols = slice(n0, n0 + 256)
            v = dot(r.rg1[rows, :], r.blk[1].wrt[:, cols]) + dot(
                spread, r.pg[q * pool_rows : (q + 1) * pool_rows, cols]
            )
            at = (q % 2) * ci + n0
            grads[q // 2][:, at : at + 256] = (v * m).astype(BF16)
        e = Exchange(
            lambda s, q=q: grads[q // 2].at[
                :, pl.ds(pl.multiple_of((q % 2) * ci + s * z.cis, LANES), z.cis)
            ],
            lambda s, q=q: made.gx.at[
                pl.ds(pl.multiple_of(s * ni + q * part, part), part), :
            ],
            os_sem.at[OUT_PARTS + q],
            or_sem.at[OUT_PARTS + q],
        )
        e.start()
        last.append(e)

    lead = part // (2 * si)
    lax.fori_loop(0, lead, reduce_grad1, 0)
    send_quarter(0)
    sums_of[5].ready3()
    sums_of[5].step3()
    sums_of[2].ready3()
    sums_of[2].step3()
    lax.fori_loop(lead, nq * lead, reduce_grad1, 0)
    r.rgt[...] = jnp.transpose(r.rg1[...])
    for n0 in range(0, ci, 256):
        pack_rows(1, REDUCE, n0 // LANES, dot(r.rgt[...], r.x[:, n0 : n0 + 256]))
    sums_of[4].step1()
    sums_of[3].ready3()
    sums_of[3].step3()
    sums_of[4].ready2()
    sums_of[4].step2()
    send_quarter(1)
    sums_of[2].ready4()
    sums_of[2].step4()
    sums_of[1].ready5()
    sums_of[1].step5()
    for q in range(2, nq):
        send_quarter(q)
    sums_of[5].ready4()
    sums_of[5].step4()
    sums_of[3].ready4()
    sums_of[3].step4()
    sums_of[2].ready5()
    sums_of[2].step5()
    sums_of[1].ready6()
    sums_of[1].step6()
    sums_of[4].ready3()
    sums_of[4].step3()
    sums_of[3].ready5()
    sums_of[3].step5()
    sums_of[2].ready6()
    sums_of[2].step6()
    sums_of[4].ready4()
    sums_of[4].step4()
    sums_of[3].ready6()
    sums_of[3].step6()
    for e in out_ex + last:
        e.wait()
    for sums in sums_of.values():
        sums.finish()


class Weights:
    def __init__(self, values):
        (
            self.reduce, self.reducegain, self.reducebias,
            self.split, self.splitgain, self.splitbias,
            self.squeeze, self.squeezegain, self.squeezebias,
            self.excite, self.excitebias,
            self.expand, self.expandgain, self.expandbias,
        ) = values[:14]
        self.extra = values[14:]


def doubled(v):
    return jnp.concatenate([v, v], axis=-1).reshape(-1, LANES)


def per_device(mesh, images, cotangent, groups, *weights):
    first, second = Weights(weights[:17]), Weights(weights[17:])
    z = Sizes(mesh, images, first.reduce, first.expand, first.squeeze)

    def vectors(w):
        parts = (w.reducegain, w.reducebias, w.splitgain, w.splitbias, w.excitebias)
        parts += (w.expandgain, w.expandbias) + w.extra[1:] + (w.squeezegain, w.squeezebias)
        return [v if v.ndim == 2 else v.reshape(1, -1) for v in parts]

    def block(w):
        return dict(
            wrt=w.reduce.T,
            wst=jnp.transpose(w.split, (0, 1, 3, 4, 2)).reshape(TAPS, 2, z.mids, z.grp),
            sq=w.squeeze,
            ext=jnp.transpose(w.excite, (1, 2, 0)),
            we=w.expand,
        )

    inputs = dict(
        images=images.reshape(-1, z.cis),
        cot=cotangent.reshape(-1, z.cos),
        groups=groups,
        vec=vectors(first) + vectors(second),
        wsh=first.extra[0],
        blk={1: block(first), 2: block(second)},
    )
    in_specs = jax.tree.map(lambda v: pl.BlockSpec(memory_space=pl.ANY), inputs)
    in_specs.update(groups=pl.BlockSpec(memory_space=pltpu.SMEM))
    outs = dict(
        out=jax.ShapeDtypeStruct((z.nc * z.no, z.cos), BF16),
        gx=jax.ShapeDtypeStruct((z.nc * z.ni, z.cis), BF16),
        sto=jax.ShapeDtypeStruct((NSTO, LANES), F32),
        res={n: jax.ShapeDtypeStruct((rows, LANES), BF16) for n, rows in z.rows.items()},
    )
    out_specs = jax.tree.map(lambda v: pl.BlockSpec(memory_space=pl.ANY), outs)
    out_specs.update(sto=pl.BlockSpec(memory_space=pltpu.VMEM))
    scratch = scratch_tree(z, vectors(first) + vectors(second))
    tree = jax.tree.structure((inputs, outs, scratch))
    results = pl.pallas_call(
        functools.partial(mega_kernel, z, tree),
        out_shape=jax.tree.leaves(outs),
        in_specs=jax.tree.leaves(in_specs),
        out_specs=jax.tree.leaves(out_specs),
        scratch_shapes=jax.tree.leaves(scratch),
        compiler_params=pltpu.CompilerParams(
            collective_id=0, has_side_effects=True, vmem_limit_bytes=63 << 20
        ),
        name="two_blocks",
    )(*jax.tree.leaves(inputs))
    return unpack(z, jax.tree.unflatten(jax.tree.structure(outs), results))


def unpack_kernel(z, plan, tree, *refs):
    given, (out_image, gx, *outs) = jax.tree.unflatten(tree, refs)
    given = space(given)
    out_in, gx_in, sto, res = given.out, given.gx, given.sto, given.res
    c = lax.axis_index(CHAN)
    out_image[...] = out_in[...].astype(F32)
    gx[...] = gx_in[...].astype(F32)

    def mid_share(row):
        v = sto[pl.ds(row + lax.div(c, 2), 1), :]
        return jnp.where(lax.rem(c, 2) == 0, v[:, : z.mids], v[:, z.mids :])

    @pl.when(pl.program_id(0) == 0)
    def _():
        for (kind, k, name), o in zip(plan, outs):
            if kind == MATRIX:
                group, at = z.lay[(k, name)]
                rows = o.shape[0]
                for t in range(o.shape[1] // LANES):
                    o[:, t * LANES : (t + 1) * LANES] = res[group][
                        at + t * rows : at + (t + 1) * rows, :
                    ].astype(F32)
                continue
            row = name
            if kind == MID_VECTOR:
                o[...] = mid_share(row)
            elif kind == PAIR_VECTOR:
                o[0:1, :] = mid_share(row)
                o[1:2, :] = mid_share(row + z.mid // LANES)
            elif kind == ATT_VECTOR:
                o[...] = sto[row : row + 1, :]
            else:
                n = z.cos // LANES
                for t in range(n):
                    o[:, t * LANES : (t + 1) * LANES] = sto[pl.ds(row + c * n + t, 1), :]


def unpack(z, results):
    plan = []
    for k in (1, 2):
        v = STO_ROWS[k]
        plan += [
            (MATRIX, k, REDUCE), (MID_VECTOR, k, v.rg), (MID_VECTOR, k, v.rb),
            (MATRIX, k, SPLIT), (PAIR_VECTOR, k, v.sg), (PAIR_VECTOR, k, v.sb),
            (MATRIX, k, SQUEEZE), (ATT_VECTOR, k, v.qg), (ATT_VECTOR, k, v.qb),
            (MATRIX, k, EXCITE), (PAIR_VECTOR, k, v.xb),
            (MATRIX, k, EXPAND), (OUT_VECTOR, k, v.eg), (OUT_VECTOR, k, v.eb),
        ]
        if k == 1:
            plan += [(MATRIX, k, SHORTCUT), (OUT_VECTOR, k, v.hg), (OUT_VECTOR, k, v.eb)]

    def shape_of(kind, k, name):
        if kind == MATRIX:
            return (
                (z.mids, z.ci if k == 1 else z.co),
                (2 * TAPS * z.mids, LANES),
                (z.mids, z.att),
                (2 * z.mids, z.att),
                (z.mid, z.cos),
                (z.ci, z.cos),
            )[name]
        return (None, (1, z.mids), (2, z.mids), (1, z.att), (1, z.cos))[kind]

    shapes = [shape_of(*entry) for entry in plan]
    steps = 4
    whole = lambda shape: pl.BlockSpec(shape, lambda i: (0, 0))
    slab = lambda v: pl.BlockSpec((v.shape[0] // steps, v.shape[1]), lambda i: (i, 0))
    in_specs = {n: slab(v) if n in ("out", "gx") else jax.tree.map(lambda a: whole(a.shape), v)
                for n, v in results.items()}
    images = [results["out"], results["gx"]]
    outs = [jax.ShapeDtypeStruct(v.shape, F32) for v in images]
    outs += [jax.ShapeDtypeStruct(s, F32) for s in shapes]
    flat = pl.pallas_call(
        functools.partial(unpack_kernel, z, plan, jax.tree.structure((results, outs))),
        grid=(steps,),
        out_shape=outs,
        in_specs=jax.tree.leaves(in_specs),
        out_specs=[slab(v) for v in images] + [whole(s) for s in shapes],
        compiler_params=pltpu.CompilerParams(vmem_limit_bytes=62 << 20),
        name="unpack",
    )(*jax.tree.leaves(results))
    final = [
        flat[0].reshape(z.nc * z.b, z.so, z.so, z.cos),
        flat[1].reshape(z.nc * z.b, z.si, z.si, z.cis),
    ]
    for (kind, _, name), v in zip(plan, flat[2:]):
        if (kind, name) == (MATRIX, REDUCE):
            v = v.T
        elif (kind, name) == (MATRIX, SPLIT):
            v = jnp.transpose(v.reshape(3, 3, 2, z.mids, z.grp), (0, 1, 4, 2, 3))
        elif (kind, name) == (MATRIX, EXCITE):
            v = jnp.transpose(v.reshape(2, z.mids, z.att), (2, 0, 1))
        elif kind in (MID_VECTOR, ATT_VECTOR, OUT_VECTOR):
            v = v.reshape(-1)
        final.append(v)
    return tuple(final)


def specs():
    block = [
        P(None, CHAN), P(CHAN), P(CHAN),
        P(None, None, None, None, CHAN), P(None, CHAN), P(None, CHAN),
        P(CHAN, None), P(), P(), P(None, None, CHAN), P(None, CHAN),
        P(None, CHAN), P(CHAN), P(CHAN),
    ]
    short = [P(None, CHAN), P(CHAN), P(CHAN)]
    return block + short + block


def solution(mesh):
    image = P(DP, None, None, CHAN)
    return jax.shard_map(
        functools.partial(per_device, mesh),
        mesh=mesh,
        in_specs=tuple([image, image, P(DP)] + specs()),
        out_specs=tuple([image, image] + specs()),
        check_vma=False,
    )
```
